32 devices in a mesh: dp: 8 (over y, x, core), tm: 4 (over z).
Axes of the slice: x: 2, y: 2, z: 4, core: 2. Of those that a mesh axis runs over, the one named last changes fastest.
Arguments:
- clips_x: bfloat16 [2, 16, 4, 8, 8, 512], P(None, 'dp', 'tm'), may hold values from -6 to 6
- frames: int32 [2, 16], P(None, 'dp'), may hold values from 8 to 32, as said below
- labels: int32 [2, 16], P(None, 'dp'), may hold values from 0 to 399
- spatial_weight: float32 [512, 2, 9, 1152], P(('dp', 'tm'))
- temporal_weight: float32 [512, 2, 3, 1152], P(('dp', 'tm'))
- head_weight: float32 [512, 400], P(('dp', 'tm'))
- affine: float32 [2, 2, 1664], replicated
- head_bias: float32 [400], replicated, may hold values from -2 to 2
- spatial_first: float32 [512, 2, 9, 1152], P(('dp', 'tm'))
- spatial_second: float32 [512, 2, 9, 1152], P(('dp', 'tm')), as said below
- temporal_first: float32 [512, 2, 3, 1152], P(('dp', 'tm'))
- temporal_second: float32 [512, 2, 3, 1152], P(('dp', 'tm')), as said below
- head_first: float32 [512, 400], P(('dp', 'tm'))
- head_second: float32 [512, 400], P(('dp', 'tm')), as said below
- affine_first: float32 [2, 2, 1664], replicated
- affine_second: float32 [2, 2, 1664], replicated, as said below
- bias_first: float32 [400], replicated
- bias_second: float32 [400], replicated, as said below
Outputs:
- loss_sum: float32 [], replicated
- new_spatial_first: float32 [512, 2, 9, 1152], P(('dp', 'tm'))
- new_spatial_second: float32 [512, 2, 9, 1152], P(('dp', 'tm'))
- new_spatial_weight: float32 [512, 2, 9, 1152], P(('dp', 'tm'))
- new_temporal_first: float32 [512, 2, 3, 1152], P(('dp', 'tm'))
- new_temporal_second: float32 [512, 2, 3, 1152], P(('dp', 'tm'))
- new_temporal_weight: float32 [512, 2, 3, 1152], P(('dp', 'tm'))
- new_head_first: float32 [512, 400], P(('dp', 'tm'))
- new_head_second: float32 [512, 400], P(('dp', 'tm'))
- new_head_weight: float32 [512, 400], P(('dp', 'tm'))
- new_affine_first: float32 [2, 2, 1664], replicated
- new_affine_second: float32 [2, 2, 1664], replicated
- new_affine: float32 [2, 2, 1664], replicated
- new_bias_first: float32 [400], replicated
- new_bias_second: float32 [400], replicated
- new_head_bias: float32 [400], replicated
- norms: float32 [2, 5], replicated
The draws below stay inside these ranges and needn't reach their ends.
Inputs may be any that keep to these rules, and one draw needn't show every extreme that they name: `frames`: each value is 8, 16 or 32; in every aligned block of 2 clips of one micro-batch at least one clip has 32. `spatial_second`: entries are positive. `temporal_second`: entries are positive. `head_second`: entries are positive. `affine_second`: entries are positive. `bias_second`: entries are positive.
All inputs are finite; a program needn't handle non-finite values.
Results may differ from the reference program's by a relative error of at most 0.014.
Values may be sent and summed in bfloat16 or wider, within the bound.
No kernel may reach another device: no remote copies, remote signals or barrier semaphores. Data moves between devices by JAX's collectives and lax.ppermute only.
A program may use at most 192 MiB of HBM per device.

```python
import math
import jax
import jax.numpy as jnp
from jax import lax

C = 512
M = 1152
K = 400
CLIP_DEV = 2
MICRO = 2
FR = 4
HT = 8
WD = 8
STEP = 5
CLIPS = 16


CONV_SCALE = 0.006


HEAD_SCALE = 0.025


AFFINE_SCALE = 0.015


BIAS_SCALE = 0.05


def ramp(count, highest):
    places = jnp.arange(count, dtype=jnp.float32) / max(count - 1, 1)
    return (1.0 + (highest - 1.0) * places) / math.sqrt((highest * highest + highest + 1.0) / 3.0)


def gauss_moment(key, shape, scale):
    return scale * jax.random.normal(key, shape, jnp.float32)


def square_moment(key, shape, scale):
    return scale * scale * jnp.exp(jax.random.uniform(key, shape, jnp.float32, math.log(0.5), math.log(8.0)))


def draw_frames(key, part):
    key = jax.random.fold_in(key, 1)
    key_one, key_two = jax.random.split(key)
    ticket = jax.random.randint(key_one, (MICRO, CLIPS), 0, 64)
    places = jnp.arange(CLIPS, dtype=jnp.int32)[None, :]
    cutoff = 56 - 56 * places // CLIPS
    counts = jnp.where(ticket < cutoff, 8, jnp.where(ticket < cutoff + 8, 16, 32))
    chosen = jax.random.randint(key_two, (MICRO, CLIPS // CLIP_DEV), 0, CLIP_DEV)
    forced = places % CLIP_DEV == jnp.repeat(chosen, CLIP_DEV, axis=1)
    return jnp.where(forced, 32, counts).astype(jnp.int32)


def draw_spatial_weight(key, part):
    key = jax.random.fold_in(key, 11)
    base = jax.random.normal(key, (C, 2, 9, M), jnp.float32)
    highest = 3.0
    return base * ramp(C, highest)[:, None, None, None] / math.sqrt(9 * C)


def draw_temporal_weight(key, part):
    key = jax.random.fold_in(key, 12)
    base = jax.random.normal(key, (C, 2, 3, M), jnp.float32)
    highest = 3.0
    return base * ramp(C, highest)[:, None, None, None] / math.sqrt(3 * M)


def draw_head_weight(key, part):
    key = jax.random.fold_in(key, 13)
    base = jax.random.normal(key, (C, K), jnp.float32)
    highest = 3.0
    return base * ramp(C, highest)[:, None] * 3.0 / math.sqrt(C)


def draw_affine(key, part):
    key = jax.random.fold_in(key, 14)
    key_one, key_two = jax.random.split(key)
    gains = 1.0 + 0.3 * jax.random.uniform(key_one, (2, M + C), jnp.float32, -1.0, 1.0)
    shifts = 0.3 * jax.random.normal(key_two, (2, M + C), jnp.float32)
    return jnp.stack([gains, shifts], axis=1)


def draw_spatial_first(key, part):
    key = jax.random.fold_in(key, 21)
    highest = 3.0
    return gauss_moment(key, (C, 2, 9, M), CONV_SCALE / math.sqrt(MICRO * CLIPS)) * ramp(C, highest)[:, None, None, None]


def draw_spatial_second(key, part):
    key = jax.random.fold_in(key, 22)
    return square_moment(key, (C, 2, 9, M), CONV_SCALE / math.sqrt(MICRO * CLIPS))


def draw_temporal_first(key, part):
    key = jax.random.fold_in(key, 23)
    highest = 3.0
    return gauss_moment(key, (C, 2, 3, M), CONV_SCALE / math.sqrt(MICRO * CLIPS)) * ramp(C, highest)[:, None, None, None]


def draw_temporal_second(key, part):
    key = jax.random.fold_in(key, 24)
    return square_moment(key, (C, 2, 3, M), CONV_SCALE / math.sqrt(MICRO * CLIPS))


def draw_head_first(key, part):
    key = jax.random.fold_in(key, 25)
    highest = 3.0
    return gauss_moment(key, (C, K), HEAD_SCALE / math.sqrt(MICRO * CLIPS)) * ramp(C, highest)[:, None]


def draw_head_second(key, part):
    key = jax.random.fold_in(key, 26)
    return square_moment(key, (C, K), HEAD_SCALE / math.sqrt(MICRO * CLIPS))


def draw_affine_first(key, part):
    key = jax.random.fold_in(key, 27)
    return gauss_moment(key, (2, 2, M + C), AFFINE_SCALE / math.sqrt(MICRO * CLIPS))


def draw_affine_second(key, part):
    key = jax.random.fold_in(key, 28)
    return square_moment(key, (2, 2, M + C), AFFINE_SCALE / math.sqrt(MICRO * CLIPS))


def draw_bias_first(key, part):
    key = jax.random.fold_in(key, 29)
    return gauss_moment(key, (K,), BIAS_SCALE / math.sqrt(MICRO * CLIPS))


def draw_bias_second(key, part):
    key = jax.random.fold_in(key, 30)
    return square_moment(key, (K,), BIAS_SCALE / math.sqrt(MICRO * CLIPS))


def place_ends(array, key, low, top_value):
    longest = array.shape.index(max(array.shape))
    spots = []
    for shift in (0, 1):
        where = [jax.random.randint(jax.random.fold_in(key, axis), (), 0, length) for axis, length in enumerate(array.shape)]
        where[longest] = (where[longest] + shift) % array.shape[longest]
        spots.append(tuple(where))
    return array.at[spots[0]].set(low).at[spots[1]].set(top_value)


def steps_of(stream_key, dims, cuts, least, largest):
    def one(position, parts):
        steps = jax.random.uniform(jax.random.fold_in(jax.random.fold_in(stream_key, 6), position), (parts,), jnp.float32, least / len(cuts), largest / len(cuts))
        return jnp.repeat(jnp.exp(steps), dims[position] // parts).reshape((-1,) + (1,) * (len(dims) - position - 1))

    level = one(*cuts[0])
    for cut in cuts[1:]:
        level = level * one(*cut)
    return level


def noise(key, shape, deviation, reach, pieces=(), held_as=jnp.bfloat16):
    drawn = deviation * jax.random.normal(key, shape, jnp.float32)
    if pieces:
        drawn = drawn * steps_of(key, shape, pieces, -0.22, 0.18)
    return jnp.clip(drawn, -reach, reach).astype(held_as)


def setup_inputs(seed: int = 0) -> dict:
    key_of = jax.random.split(jax.random.key(seed), 19)
    return {
        "clips_x": noise(key_of[0], (MICRO, CLIPS, FR, HT, WD, C), 1.0, 6.0, ((1, 8), (2, 4))),
        "frames": draw_frames(jax.random.fold_in(key_of[18], 71), 0),
        "labels": place_ends(jax.random.randint(key_of[2], (MICRO, CLIPS), 0, K), jax.random.fold_in(key_of[2], 1), 0, K - 1).astype(jnp.int32),
        "spatial_weight": draw_spatial_weight(jax.random.fold_in(key_of[18], 71), 0),
        "temporal_weight": draw_temporal_weight(jax.random.fold_in(key_of[18], 71), 0),
        "head_weight": draw_head_weight(jax.random.fold_in(key_of[18], 71), 0),
        "affine": draw_affine(jax.random.fold_in(key_of[18], 71), 0),
        "head_bias": noise(key_of[7], (K,), 0.3, 2.0, (), jnp.float32),
        "spatial_first": draw_spatial_first(jax.random.fold_in(key_of[18], 71), 0),
        "spatial_second": draw_spatial_second(jax.random.fold_in(key_of[18], 71), 0),
        "temporal_first": draw_temporal_first(jax.random.fold_in(key_of[18], 71), 0),
        "temporal_second": draw_temporal_second(jax.random.fold_in(key_of[18], 71), 0),
        "head_first": draw_head_first(jax.random.fold_in(key_of[18], 71), 0),
        "head_second": draw_head_second(jax.random.fold_in(key_of[18], 71), 0),
        "affine_first": draw_affine_first(jax.random.fold_in(key_of[18], 71), 0),
        "affine_second": draw_affine_second(jax.random.fold_in(key_of[18], 71), 0),
        "bias_first": draw_bias_first(jax.random.fold_in(key_of[18], 71), 0),
        "bias_second": draw_bias_second(jax.random.fold_in(key_of[18], 71), 0),
    }


HIGH = lax.Precision.HIGHEST
EPS_NORM = 1e-05
EPS_ADAM = 1e-06
BETA_ONE = 0.5
BETA_TWO = 0.5
DECAY = 0.01
RATE = 0.3
RATE_SMALL = 0.1

@jax.custom_vjp
def low(v):
    return lax.optimization_barrier(v.astype(jnp.bfloat16)).astype(jnp.float32)

@jax.custom_vjp
def low_back(v):
    return v

def low_keep(v):
    return (low(v), None)

def low_pass(kept, grad):
    return (grad,)

def back_keep(v):
    return (v, None)

def back_low(kept, grad):
    return (low(grad),)
low.defvjp(low_keep, low_pass)
low_back.defvjp(back_keep, back_low)

def conv_space(values, weight):
    height, breadth = (values.shape[2], values.shape[3])
    padded = jnp.pad(values, ((0, 0), (0, 0), (1, 1), (1, 1), (0, 0)))
    result = None
    for k in range(9):
        window = padded[:, :, k // 3:k // 3 + height, k % 3:k % 3 + breadth]
        term = jnp.einsum('nfhwc,cm->nfhwm', window, weight[:, k], precision=HIGH)
        result = term if result is None else result + term
    return result

def conv_time(values, weight):
    length = values.shape[1]
    padded = jnp.pad(values, ((0, 0), (1, 1), (0, 0), (0, 0), (0, 0)))
    result = None
    for k in range(3):
        term = jnp.einsum('nfhwm,cm->nfhwc', padded[:, k:k + length], weight[:, k], precision=HIGH)
        result = term if result is None else result + term
    return result

def normalize(values, gain, shift, masks, residual):
    count = jnp.sum(masks) * values.shape[2] * values.shape[3]
    average = lax.optimization_barrier(jnp.sum(values * masks, axis=(0, 1, 2, 3))) / count
    squares = lax.optimization_barrier(jnp.sum(values * values * masks, axis=(0, 1, 2, 3))) / count
    scale = lax.rsqrt(squares - average * average + EPS_NORM)
    pre_act = gain * ((values - average) * scale) + shift + residual
    return jax.nn.silu(pre_act) * masks

def adam_part(weight, gradient, moment_one, moment_two, decay):
    new_one = BETA_ONE * moment_one + (1.0 - BETA_ONE) * gradient
    new_two = BETA_TWO * moment_two + (1.0 - BETA_TWO) * gradient * gradient
    direction = new_one / (1.0 - BETA_ONE ** STEP) / (jnp.sqrt(new_two / (1.0 - BETA_TWO ** STEP)) + EPS_ADAM) + decay * weight
    return (new_one, new_two, direction)

def reference(clips_x, frames, labels, spatial_weight, temporal_weight, head_weight, affine, head_bias, spatial_first, spatial_second, temporal_first, temporal_second, head_first, head_second, affine_first, affine_second, bias_first, bias_second):
    lengths = (frames // 8).astype(jnp.float32)
    frame_mask = (jnp.arange(FR, dtype=jnp.int32)[None, None, :] * 8 < frames[:, :, None]).astype(jnp.float32)
    onehot = (labels[:, :, None] == jnp.arange(K, dtype=jnp.int32)[None, None, :]).astype(jnp.float32)
    inputs = clips_x.astype(jnp.float32)

    def forward(space_w, time_w, head_w, affine_p, bias_p):
        running = jnp.zeros((), jnp.float32)
        for u in range(MICRO):
            residual = inputs[u]
            masks = frame_mask[u][:, :, None, None, None]
            current = residual
            for l in range(2):
                spatial_out = low_back(conv_space(low(current), low(space_w[:, l])))
                current = normalize(spatial_out, affine_p[l, 0, :M], affine_p[l, 1, :M], masks, 0.0)
                temporal_out = low(low_back(conv_time(low_back(low(current)), low(time_w[:, l]))))
                current = normalize(temporal_out, affine_p[l, 0, M:], affine_p[l, 1, M:], masks, residual if l == 1 else 0.0)
            pooled = lax.optimization_barrier(jnp.sum(current, axis=(1, 2, 3))) / (lengths[u] * HT * WD)[:, None]
            logits = low_back(jnp.dot(low(pooled), low(head_w), precision=HIGH)) + bias_p
            picked = lax.optimization_barrier(jnp.sum(logits * onehot[u], axis=1))
            running = running + jnp.sum(jax.nn.logsumexp(logits, axis=1) - picked)
        return running
    loss_sum, pullback = jax.vjp(forward, spatial_weight, temporal_weight, head_weight, affine, head_bias)
    grad_space, grad_time, grad_head, grad_affine, grad_bias = pullback(jnp.full((), 1.0 / (MICRO * CLIPS), jnp.float32))
    space_one, space_two, space_dir = adam_part(spatial_weight, grad_space, spatial_first, spatial_second, DECAY)
    time_one, time_two, time_dir = adam_part(temporal_weight, grad_time, temporal_first, temporal_second, DECAY)
    head_one, head_two, head_dir = adam_part(head_weight, grad_head, head_first, head_second, DECAY)
    affine_one, affine_two, affine_dir = adam_part(affine, grad_affine, affine_first, affine_second, 0.0)
    bias_one, bias_two, bias_dir = adam_part(head_bias, grad_bias, bias_first, bias_second, 0.0)
    weight_norms = jnp.concatenate([jnp.sqrt(lax.optimization_barrier(jnp.sum(spatial_weight * spatial_weight, axis=(0, 2, 3)))), jnp.sqrt(lax.optimization_barrier(jnp.sum(temporal_weight * temporal_weight, axis=(0, 2, 3)))), jnp.sqrt(jnp.sum(head_weight * head_weight))[None]])
    dir_norms = jnp.concatenate([jnp.sqrt(lax.optimization_barrier(jnp.sum(space_dir * space_dir, axis=(0, 2, 3)))), jnp.sqrt(lax.optimization_barrier(jnp.sum(time_dir * time_dir, axis=(0, 2, 3)))), jnp.sqrt(jnp.sum(head_dir * head_dir))[None]])
    trust = weight_norms / dir_norms
    new_space = spatial_weight - RATE * trust[0:2][None, :, None, None] * space_dir
    new_time = temporal_weight - RATE * trust[2:4][None, :, None, None] * time_dir
    new_head = head_weight - RATE * trust[4] * head_dir
    new_affine = affine - RATE_SMALL * affine_dir
    new_bias = head_bias - RATE_SMALL * bias_dir
    norms = jnp.stack([weight_norms, dir_norms])
    return (loss_sum, space_one, space_two, new_space, time_one, time_two, new_time, head_one, head_two, new_head, affine_one, affine_two, new_affine, bias_one, bias_two, new_bias, norms)
```

```python
import functools

import jax
import jax.numpy as jnp
from jax import lax
from jax.experimental import pallas as pl
from jax.experimental.pallas import tpu as pltpu
from jax.sharding import Mesh
from jax.sharding import PartitionSpec as P

STEP = 5
EPS_NORM = 1e-05
EPS_ADAM = 1e-06
BETA_ONE = 0.5
BETA_TWO = 0.5
DECAY = 0.01
RATE = 0.3
RATE_SMALL = 0.1

F32 = jnp.float32
BF = jnp.bfloat16
LANES = 128
SPACE, TIME = 9, 3
ALL = ("yy", "s", "u", "tm")
DATA = ("yy", "tm")
MB = 1 << 20


def whole():
    return pl.BlockSpec(memory_space=pltpu.VMEM)


def anywhere():
    return pl.BlockSpec(memory_space=pl.ANY)


def smem():
    return pl.BlockSpec(memory_space=pltpu.SMEM)


def dot(a, b):
    return jnp.dot(a, b, preferred_element_type=F32)


def dot_nt(a, b):
    return lax.dot_general(a, b, (((1,), (1,)), ((), ())), preferred_element_type=F32)


class Dims:
    def __init__(self, clips, frames, height, width, channels, mid, rows, ny, nz):
        self.clips, self.frames, self.height, self.width = clips, frames, height, width
        self.channels, self.mid, self.rows, self.ny, self.nz = channels, mid, rows, ny, nz
        self.line = width * clips
        self.plane = height * self.line
        self.cells = frames * self.plane
        tiles = mid // LANES
        self.half = (tiles + 1) // 2 * LANES
        self.groups = ny * nz
        self.pieces = rows % 16 == 0

    def row_base(self, yy, s, u, z):
        return (((yy * 2 + s) * 2 + u) * self.nz + z) * self.rows


def start_weights(d, ids, refs, scratch, sems):
    copies = []
    if not d.pieces:
        copies.append(pltpu.make_async_copy(refs[0], scratch, sems.at[0]))
    else:
        for urel in range(2):
            for yy in range(d.ny):
                for z in range(d.nz):
                    for srel in range(2):
                        row = d.row_base(yy, srel ^ ids[0], urel ^ ids[1], z)
                        row = pl.multiple_of(row, 16)
                        copies.append(
                            pltpu.make_async_copy(
                                refs[urel].at[yy * d.nz + z, srel],
                                scratch.at[:, pl.ds(row, d.rows), :],
                                sems.at[len(copies)],
                            )
                        )
    for copy in copies:
        copy.start()
    return copies


def weight_scratch(d, taps):
    count = 4 * d.groups if d.pieces else 1
    return [pltpu.VMEM((taps, d.channels, d.half), BF), pltpu.SemaphoreType.DMA((count,))]


def space_scratch(d, width):
    return pltpu.VMEM((3, d.frames, (d.height + 2) * d.line, width), BF)


def time_scratch(d, width):
    return pltpu.VMEM(((d.frames + 2) * d.plane, width), BF)


def fill_space(d, pad, values):
    cells, width = values.shape
    place = lax.broadcasted_iota(jnp.int32, (cells, width), 0)
    column = lax.rem(lax.div(place, d.clips), d.width)
    edge = jnp.zeros((3, d.frames, d.line, width), BF)
    pad[:, :, 0 : d.line, :] = edge
    pad[:, :, d.line + d.plane :, :] = edge
    left = jnp.where(column > 0, pltpu.roll(values, d.clips, 0), 0.0)
    right = jnp.where(column < d.width - 1, pltpu.roll(values, cells - d.clips, 0), 0.0)
    for j, moved in enumerate((left, values, right)):
        pad[j, :, d.line : d.line + d.plane, :] = moved.astype(BF).reshape(
            d.frames, d.plane, width
        )


def space_window(d, pad, i, j):
    start = pl.multiple_of(i * d.line, d.line)
    block = pad[j, :, pl.ds(start, d.plane), :]
    return block.reshape(d.cells, block.shape[-1])


def fill_time(d, pad, values):
    width = values.shape[1]
    edge = jnp.zeros((d.plane, width), BF)
    pad[0 : d.plane, :] = edge
    pad[d.plane + d.cells :, :] = edge
    pad[d.plane : d.plane + d.cells, :] = values


def time_window(d, pad, k):
    return pad[pl.ds(pl.multiple_of(k * d.plane, d.plane), d.cells), :]


def sums_of(first, second, extra=None):
    width = first.shape[1]
    rows = [jnp.sum(first, axis=0, keepdims=True), jnp.sum(second, axis=0, keepdims=True)]
    if extra is not None:
        rows.append(extra)
    rows.append(jnp.zeros((8 - len(rows), width), F32))
    return jnp.concatenate(rows, axis=0)


def coefs_of(total, count, gains):
    average = total[0:1] / count
    scale = lax.rsqrt(total[1:2] / count - average * average + EPS_NORM)
    return jnp.concatenate(
        [average, scale, gains[0:2], jnp.zeros((4, total.shape[1]), F32)], axis=0
    )


def normed_of(values, coef):
    return (values - coef[0:1]) * coef[1:2]


def act_slope(pre):
    sigma = jax.nn.sigmoid(pre)
    return sigma * (1.0 + pre * (1.0 - sigma))


def norm_back(grad_pre, normed, coef, total, count, mask):
    scale = coef[2:3] * coef[1:2]
    return mask * (scale * (grad_pre - (total[0:1] + normed * total[1:2]) / count))


def conv_space_into(d, acc, pad, weight):
    acc[...] = jnp.zeros_like(acc)

    @pl.loop(0, SPACE)
    def _(k):
        window = space_window(d, pad, lax.div(k, 3), lax.rem(k, 3))
        acc[...] += dot(window, weight[k])


def split_weight(refs, pieces):
    count = 2 if pieces else 1
    return refs[:count], refs[count:]


def first_space_kernel(d, *refs):
    ids, *refs = refs
    w_refs, refs = split_weight(refs, d.pieces)
    x, mask, s_out, sums_out, weight, sems, pad = refs
    copies = start_weights(d, ids, w_refs, weight, sems)
    fill_space(d, pad, x[...].astype(F32))
    for copy in copies:
        copy.wait()
    conv_space_into(d, s_out, pad, weight)
    m = mask[...]
    values = s_out[...]
    count = jnp.sum(m, axis=0, keepdims=True) + jnp.zeros((1, d.half), F32)
    sums_out[...] = sums_of(values * m, values * values * m, count)


def second_space_kernel(d, *refs):
    ids, *refs = refs
    w_refs, refs = split_weight(refs, d.pieces)
    q, va, vb, count, gains, mask, a_out, coef_out, s_out, sums_out, weight, sems, pad = refs
    copies = start_weights(d, ids, w_refs, weight, sems)
    m = mask[...]
    coef = coefs_of(va[...] + vb[...], count[...], gains[...])
    coef_out[...] = coef
    pre = coef[2:3] * normed_of(q[...].astype(F32), coef) + coef[3:4]
    act = jax.nn.silu(pre) * m
    a_out[...] = act.astype(BF)
    fill_space(d, pad, act)
    for copy in copies:
        copy.wait()
    conv_space_into(d, s_out, pad, weight)
    values = s_out[...]
    sums_out[...] = sums_of(values * m, values * values * m)


def time_kernel(d, *refs):
    ids, *refs = refs
    w_refs, refs = split_weight(refs, d.pieces)
    s, va, vb, count, gains, mask, a_out, q_out, coef_out, weight, sems, pad = refs
    copies = start_weights(d, ids, w_refs, weight, sems)
    coef = coefs_of(va[...] + vb[...], count[...], gains[...])
    coef_out[...] = coef
    pre = coef[2:3] * normed_of(s[...], coef) + coef[3:4]
    act = (jax.nn.silu(pre) * mask[...]).astype(BF)
    a_out[...] = act
    fill_time(d, pad, act)
    for copy in copies:
        copy.wait()
    total = dot_nt(time_window(d, pad, 0), weight[0])
    for k in range(1, TIME):
        total = total + dot_nt(time_window(d, pad, k), weight[k])
    q_out[...] = total.astype(BF)


def join_kernel(qa, qb, mask, q_out, sums_out):
    total = (qa[...].astype(F32) + qb[...].astype(F32)).astype(BF)
    q_out[...] = total
    values = total.astype(F32)
    m = mask[...]
    sums_out[...] = sums_of(values * m, values * values * m)


def head_kernel(
    d,
    denominator,
    classes,
    q,
    va,
    vb,
    count,
    gains,
    mask,
    x,
    head,
    bias,
    clip_info,
    labels,
    coef_out,
    grad_out,
    sums_out,
):
    m = mask[...]
    coef = coefs_of(va[...] + vb[...], count[...], gains[...])
    coef_out[...] = coef
    normed = normed_of(q[...].astype(F32), coef)
    pre = coef[2:3] * normed + coef[3:4] + x[...].astype(F32)
    sigma = jax.nn.sigmoid(pre)
    y = pre * sigma * m
    folded = jnp.sum(y.reshape(d.cells // 8, 8, d.channels), axis=0)
    step = d.clips
    total = folded
    for k in range(1, 8 // step):
        total = total + pltpu.roll(folded, k * step, 0)
    inverse = 1.0 / clip_info[:, 0:1]
    pooled = total * inverse
    pooled_bf = pooled.astype(BF)
    weight = head[...]
    logits = dot(pooled_bf, weight) + bias[...]
    largest = jnp.max(logits, axis=1, keepdims=True)
    shifted = jnp.exp(logits - largest)
    log_total = largest + jnp.log(jnp.sum(shifted, axis=1, keepdims=True))
    lane = lax.broadcasted_iota(jnp.int32, logits.shape, 1)
    onehot = jnp.where(lane == labels[:, 0:1], 1.0, 0.0)
    inside = lane < classes
    kept = jnp.where(inside, logits, 0.0)
    loss = log_total - jnp.sum(kept * onehot, axis=1, keepdims=True)
    grad_logits = jnp.where(inside, (jnp.exp(logits - log_total) - onehot) / denominator, 0.0)
    grad_pooled = dot_nt(grad_logits.astype(BF), weight) * inverse
    grad_y = jnp.broadcast_to(grad_pooled[None], (d.cells // 8, 8, d.channels)).reshape(
        d.cells, d.channels
    )
    grad_pre = grad_y * m * (sigma * (1.0 + pre * (1.0 - sigma)))
    grad_out[...] = grad_pre
    sums_out[0:8, :] = sums_of(grad_pre, grad_pre * normed)
    carried = jnp.where(lane == classes, loss, grad_logits)
    sums_out[8:16, :] = jnp.concatenate(
        [
            pooled_bf.astype(F32)[0 : d.clips],
            carried[0 : d.clips],
            jnp.zeros((8 - 2 * d.clips, d.channels), F32),
        ],
        axis=0,
    )


def time_back_kernel(d, *refs):
    ids, *refs = refs
    w_refs, refs = split_weight(refs, d.pieces)
    grad_two, q, coef_two, va, vb, count, mask, s, coef_one, *refs = refs
    gq_out, grad_out, sums_out, tot_out, weight, sems, pad = refs
    copies = start_weights(d, ids, w_refs, weight, sems)
    m = mask[...]
    total = va[...] + vb[...]
    tot_out[...] = total
    coef = coef_two[...]
    normed = normed_of(q[...].astype(F32), coef)
    grad_q = norm_back(grad_two[...], normed, coef, total, count[...], m).astype(BF)
    gq_out[...] = grad_q
    fill_time(d, pad, grad_q)
    for copy in copies:
        copy.wait()
    grad = dot(time_window(d, pad, TIME - 1), weight[0])
    for k in range(1, TIME):
        grad = grad + dot(time_window(d, pad, TIME - 1 - k), weight[k])
    grad = grad.astype(BF).astype(F32)
    coef = coef_one[...]
    normed = normed_of(s[...], coef)
    pre = coef[2:3] * normed + coef[3:4]
    grad_pre = grad * m * act_slope(pre)
    grad_out[...] = grad_pre
    sums_out[...] = sums_of(grad_pre, grad_pre * normed)


def space_back_kernel(d, *refs):
    ids, *refs = refs
    w_refs, refs = split_weight(refs, d.pieces)
    grad_pre, s, coef_one, va, vb, count, mask, *refs = refs
    gs_out, ga_out, tot_out, weight, sems, pad, acc = refs
    copies = start_weights(d, ids, w_refs, weight, sems)
    total = va[...] + vb[...]
    tot_out[...] = total
    coef = coef_one[...]
    normed = normed_of(s[...], coef)
    grad_s = norm_back(grad_pre[...], normed, coef, total, count[...], mask[...])
    gs_out[...] = grad_s.astype(BF)
    fill_space(d, pad, grad_s)
    for copy in copies:
        copy.wait()
    acc[...] = jnp.zeros_like(acc)

    @pl.loop(0, SPACE)
    def _(k):
        window = space_window(d, pad, 2 - lax.div(k, 3), 2 - lax.rem(k, 3))
        acc[...] += dot_nt(window, weight[k])

    ga_out[...] = acc[...].astype(BF)


def join_back_kernel(ga, gb, q, coef_two, mask, grad_out, sums_out):
    coef = coef_two[...]
    normed = normed_of(q[...].astype(F32), coef)
    pre = coef[2:3] * normed + coef[3:4]
    grad = ga[...].astype(F32) + gb[...].astype(F32)
    grad_pre = grad * mask[...] * act_slope(pre)
    grad_out[...] = grad_pre
    sums_out[...] = sums_of(grad_pre, grad_pre * normed)


def write_grad(d, ids, value, outs, held):
    if not d.pieces:
        outs[0][0] = value.astype(BF)
        return
    held[...] = value.astype(BF)
    for urel in range(2):
        for yy in range(d.ny):
            for z in range(d.nz):
                for srel in range(2):
                    row = d.row_base(yy, srel ^ ids[0], urel ^ ids[1], z)
                    row = pl.multiple_of(row, 16)
                    outs[urel][yy * d.nz + z, srel, 0] = held[pl.ds(row, d.rows), :]


def time_grad_kernel(d, *refs):
    ids, grad_q, act, *refs = refs
    outs, refs = split_weight(refs, d.pieces)
    pad, turned, held = refs
    k = pl.program_id(0)

    @pl.when(k == 0)
    def _():
        fill_time(d, pad, act[...])
        turned[...] = jnp.transpose(grad_q[...].astype(F32)).astype(BF)

    write_grad(d, ids, dot(turned[...], time_window(d, pad, k)), outs, held)


def space_grad_kernel(d, *refs):
    ids, a, grad_s, *refs = refs
    outs, refs = split_weight(refs, d.pieces)
    pad, turned, held = refs
    k = pl.program_id(0)

    @pl.when(k == 0)
    def _():
        fill_space(d, pad, grad_s[...].astype(F32))
        turned[...] = jnp.transpose(a[...].astype(F32)).astype(BF)

    window = space_window(d, pad, 2 - lax.div(k, 3), 2 - lax.rem(k, 3))
    write_grad(d, ids, dot(turned[...], window), outs, held)


def last_space_grad_kernel(d, *refs):
    ids, a, grad_pre, s, coef_one, va, vb, count, mask, tot_out, *refs = refs
    outs, refs = split_weight(refs, d.pieces)
    pad, turned, held = refs
    k = pl.program_id(0)

    @pl.when(k == 0)
    def _():
        total = va[...] + vb[...]
        tot_out[...] = total
        coef = coef_one[...]
        normed = normed_of(s[...], coef)
        grad_s = norm_back(grad_pre[...], normed, coef, total, count[...], mask[...])
        fill_space(d, pad, grad_s)
        turned[...] = jnp.transpose(a[...].astype(F32)).astype(BF)

    window = space_window(d, pad, 2 - lax.div(k, 3), 2 - lax.rem(k, 3))
    write_grad(d, ids, dot(turned[...], window), outs, held)


def sds(shape, dtype=F32):
    return jax.ShapeDtypeStruct(shape, dtype)


def call(body, name, ins, outs, scratch, flops, megabytes=40):
    return pl.pallas_call(
        body,
        name=name,
        out_shape=outs,
        in_specs=[spec for spec, _ in ins],
        out_specs=[whole()] * len(outs),
        scratch_shapes=scratch,
        compiler_params=pltpu.CompilerParams(vmem_limit_bytes=megabytes * MB),
        cost_estimate=pl.CostEstimate(flops=flops, bytes_accessed=8 * MB, transcendentals=0),
    )(*[value for _, value in ins])


def w_ins(weight):
    return [(anywhere(), piece) for piece in weight]


def v_ins(*values):
    return [(whole(), value) for value in values]


def grad_call(d, body, name, taps, ids, values, first_outs, scratch):
    if d.pieces:
        shape = (d.groups, 2, taps, d.rows, d.half)
        spec = pl.BlockSpec((d.groups, 2, 1, d.rows, d.half), lambda k: (0, 0, k, 0, 0))
        count = 2
    else:
        shape = (taps, d.channels, d.half)
        spec = pl.BlockSpec((1, d.channels, d.half), lambda k: (k, 0, 0))
        count = 1
    fixed = [pl.BlockSpec(out.shape, lambda k: (0, 0)) for out in first_outs]
    return pl.pallas_call(
        body,
        name=name,
        grid=(taps,),
        out_shape=list(first_outs) + [sds(shape, BF)] * count,
        in_specs=[smem()] + [whole()] * len(values),
        out_specs=fixed + [spec] * count,
        scratch_shapes=scratch
        + [pltpu.VMEM((d.channels, d.cells), BF), pltpu.VMEM((d.channels, d.half), BF)],
        compiler_params=pltpu.CompilerParams(vmem_limit_bytes=40 * MB),
        cost_estimate=pl.CostEstimate(
            flops=2 * taps * d.cells * d.channels * d.half,
            bytes_accessed=8 * MB,
            transcendentals=0,
        ),
    )(ids, *values)


def swap(value, axis, distance=1):
    size = lax.axis_size(axis)
    return lax.ppermute(value, axis, [(i, i ^ distance) for i in range(size)])


def data_hops():
    hops = []
    for axis in DATA:
        distance = 1
        while distance < lax.axis_size(axis):
            hops.append((axis, distance))
            distance *= 2
    return hops


def data_sums(values):
    hops = data_hops()
    for axis, distance in hops[:-1]:
        values = values + swap(values, axis, distance)
    return values, swap(values, *hops[-1])


def data_sums_gather(values):
    hops = data_hops()
    for axis, distance in hops[:-1]:
        other = swap(values, axis, distance)
        values = jnp.concatenate([values[:8] + other[:8], values[8:], other[8:]], axis=0)
    other = swap(values, *hops[-1])
    return values[:8], other[:8], jnp.concatenate([values[8:], other[8:]], axis=0)


def pick(index, first, second):
    return jnp.where(index == 0, first, second)


def gather_weight(d, s, u, both):
    own = lax.all_gather(both, DATA, axis=0, tiled=False)
    sibling = swap(own, "u")
    if d.pieces:
        return (own, sibling)
    taps = both.shape[1]
    parts = jnp.stack([own, sibling]).reshape(2, d.ny, d.nz, 2, taps, d.rows, d.half)
    parts = jnp.where(u == 0, parts, parts[::-1])
    parts = jnp.where(s == 0, parts, parts[:, :, :, ::-1])
    return (parts.transpose(4, 1, 3, 0, 2, 5, 6).reshape(taps, d.channels, d.half),)


def reduce_grad(d, s, u, outs):
    if d.pieces:
        keep, send = outs
    else:
        (natural,) = outs
        taps = natural.shape[0]
        parts = natural.reshape(taps, d.ny, 2, 2, d.nz, d.rows, d.half)
        parts = parts.transpose(3, 1, 4, 2, 0, 5, 6)
        parts = jnp.where(u == 0, parts, parts[::-1])
        parts = jnp.where(s == 0, parts, parts[:, :, :, ::-1])
        keep, send = parts.reshape(2, d.groups, 2, taps, d.rows, d.half)
    both = (keep.astype(F32) + swap(send, "u").astype(F32)).astype(BF)
    mine = lax.psum_scatter(both, DATA, scatter_dimension=0, tiled=False)
    other = swap(mine[1], "s")
    first = pick(s, mine[0], other)
    second = pick(s, other, mine[0])
    return jnp.concatenate([first, second[..., : d.mid - d.half]], axis=-1).astype(F32)


def halves(d, values):
    fill = [(0, 0)] * (values.ndim - 1) + [(0, 2 * d.half - d.mid)]
    return values[..., : d.half], jnp.pad(values[..., d.half :], fill)


def rows_of(gain, shift):
    return jnp.concatenate(
        [gain[None], shift[None], jnp.zeros((6, gain.shape[0]), F32)], axis=0
    )


def adam_part(weight, gradient, moment_one, moment_two, decay):
    new_one = BETA_ONE * moment_one + (1.0 - BETA_ONE) * gradient
    new_two = BETA_TWO * moment_two + (1.0 - BETA_TWO) * gradient * gradient
    direction = (
        new_one / (1.0 - BETA_ONE**STEP) / (jnp.sqrt(new_two / (1.0 - BETA_TWO**STEP)) + EPS_ADAM)
        + decay * weight
    )
    return (new_one, new_two, direction)


def on_device(
    clips_x,
    frames,
    labels,
    spatial_weight,
    temporal_weight,
    head_weight,
    affine,
    head_bias,
    spatial_first,
    spatial_second,
    temporal_first,
    temporal_second,
    head_first,
    head_second,
    affine_first,
    affine_second,
    bias_first,
    bias_second,
):
    s, u, z, yy = (lax.axis_index(axis) for axis in ("s", "u", "tm", "yy"))
    ny, nz = lax.axis_size("yy"), lax.axis_size("tm")
    micro, clips, _, height, width, channels = clips_x.shape
    mid = spatial_weight.shape[3]
    rows = spatial_weight.shape[0]
    classes = head_weight.shape[1]
    d = Dims(clips, nz, height, width, channels, mid, rows, ny, nz)
    assert nz == 4 and micro == 2
    ids = jnp.stack([s, u]).astype(jnp.int32)
    denominator = micro * clips * 4 * ny * nz // nz

    def prepared(weight, l):
        moved = weight[:, l].astype(BF).transpose(1, 0, 2)
        return halves(d, moved)

    head_slot = jnp.pad(head_weight.astype(BF), ((0, 0), (0, d.half - classes)))[None]
    space_parts = [prepared(spatial_weight, l) for l in range(2)]
    time_parts = [prepared(temporal_weight, l) for l in range(2)]

    def paired(parts):
        first = jnp.concatenate([part[0] for part in parts], axis=0)
        second = jnp.concatenate([part[1] for part in parts], axis=0)
        own = pick(s, first, second)
        return jnp.stack([own, swap(pick(s, second, first), "s")])

    space_w = [None, None]
    time_w = [None, None]
    space_w[0] = gather_weight(d, s, u, paired([space_parts[0]]))
    time_w[0] = gather_weight(d, s, u, paired([time_parts[0]]))
    space_w[1] = gather_weight(d, s, u, paired([space_parts[1]]))
    time_w[1] = gather_weight(d, s, u, paired([time_parts[1]]))
    head_w = gather_weight(d, s, u, paired([(head_slot, head_slot)]))
    if d.pieces:
        parts = jnp.stack(head_w).reshape(2, ny, nz, 2, rows, d.half)
        parts = jnp.where(u == 0, parts, parts[::-1])
        parts = jnp.where(s == 0, parts, parts[:, :, :, ::-1])
        head_full = parts.transpose(1, 3, 0, 2, 4, 5).reshape(channels, d.half)[:, :channels]
    else:
        head_full = head_w[0][0][:, :channels]

    def by_index(index, mine, other):
        return jnp.stack([pick(index, mine, other), pick(index, other, mine)])

    kept = pick(u, clips_x[0], clips_x[1])
    other = swap(pick(u, clips_x[1], clips_x[0]), "u")
    pair = by_index(u, kept, other)
    four = by_index(s, pair, swap(pair, "s"))
    four = four.reshape(nz, clips, height * width, channels)
    clip_all = lax.all_to_all(four, "tm", split_axis=0, concat_axis=0, tiled=True)
    x = clip_all.reshape(nz, clips, height * width, channels)
    x = x.transpose(0, 2, 1, 3).reshape(d.cells, channels)

    info = jnp.stack([frames, labels]).transpose(1, 0, 2)
    kept_info = pick(u, info[0], info[1])
    pair_info = by_index(u, kept_info, swap(pick(u, info[1], info[0]), "u"))
    four_info = by_index(s, pair_info, swap(pair_info, "s")).reshape(nz, 2, clips)
    mine_info = lax.dynamic_index_in_dim(four_info, z, 0, keepdims=False)
    my_frames, my_labels = mine_info[0], mine_info[1]
    valid = (jnp.arange(nz, dtype=jnp.int32)[:, None] * 8 < my_frames[None, :]).astype(F32)
    mask = jnp.broadcast_to(valid[:, None, :], (nz, height * width, clips)).reshape(d.cells, 1)
    divisor = (my_frames // 8).astype(F32) * (height * width)
    clip_info = jnp.broadcast_to(jnp.tile(divisor, 8 // clips)[:, None], (8, LANES))
    label_rows = jnp.broadcast_to(jnp.tile(my_labels, 8 // clips)[:, None], (8, LANES))
    bias_row = jnp.full((1, channels), -1e30, F32).at[0, :classes].set(head_bias)

    gains_one, gains_two = [], []
    for l in range(2):
        low, high = halves(d, affine[l, :, :mid])
        mine = pick(s, low, high)
        gains_one.append(rows_of(mine[0], mine[1]))
        gains_two.append(rows_of(affine[l, 0, mid:], affine[l, 1, mid:]))

    wide, narrow = (d.cells, d.half), (d.cells, channels)
    space_flops = 2 * d.cells * SPACE * channels * d.half
    time_flops = 2 * d.cells * TIME * channels * d.half

    def space_first(x_bf):
        return call(
            functools.partial(first_space_kernel, d),
            "space0",
            [(smem(), ids)] + w_ins(space_w[0]) + v_ins(x_bf, mask),
            [sds(wide), sds((8, d.half))],
            weight_scratch(d, SPACE) + [space_scratch(d, channels)],
            space_flops,
        )

    def space_next(q, va, vb, count):
        return call(
            functools.partial(second_space_kernel, d),
            "space1",
            [(smem(), ids)] + w_ins(space_w[1]) + v_ins(q, va, vb, count, gains_two[0], mask),
            [sds(narrow, BF), sds((8, channels)), sds(wide), sds((8, d.half))],
            weight_scratch(d, SPACE) + [space_scratch(d, channels)],
            space_flops,
        )

    def time_next(l, s_value, va, vb, count):
        return call(
            functools.partial(time_kernel, d),
            f"time{l}",
            [(smem(), ids)] + w_ins(time_w[l]) + v_ins(s_value, va, vb, count, gains_one[l], mask),
            [sds(wide, BF), sds(narrow, BF), sds((8, d.half))],
            weight_scratch(d, TIME) + [time_scratch(d, d.half)],
            time_flops,
        )

    def joined(q_part):
        return call(
            join_kernel,
            "join",
            v_ins(q_part, swap(q_part, "s"), mask),
            [sds(narrow, BF), sds((8, channels))],
            [],
            d.cells * channels,
        )

    s0, sums = space_first(x)
    va, vb = data_sums(sums)
    count = va[2:3, 0:1] + vb[2:3, 0:1]
    act0, q_part, coef_one0 = time_next(0, s0, va, vb, count)
    q0, sums = joined(q_part)
    va, vb = data_sums(sums)
    a_mid, coef_two0, s1, sums = space_next(q0, va, vb, count)
    va, vb = data_sums(sums)
    act1, q_part, coef_one1 = time_next(1, s1, va, vb, count)
    q1, sums = joined(q_part)
    va, vb = data_sums(sums)
    coef_two1, grad_two, sums = call(
        functools.partial(head_kernel, d, float(denominator), classes),
        "head",
        v_ins(
            q1, va, vb, count, gains_two[1], mask, x, head_full, bias_row, clip_info, label_rows
        ),
        [sds((8, channels)), sds(narrow), sds((16, channels))],
        [],
        4 * d.cells * channels,
    )
    va, vb, carried = data_sums_gather(sums)

    def time_back(l, grad, q, coef_two, va, vb, s_value, coef_one):
        return call(
            functools.partial(time_back_kernel, d),
            f"time_back{l}",
            [(smem(), ids)]
            + w_ins(time_w[l])
            + v_ins(grad, q, coef_two, va, vb, count, mask, s_value, coef_one),
            [sds(narrow, BF), sds(wide), sds((8, d.half)), sds((8, channels))],
            weight_scratch(d, TIME) + [time_scratch(d, channels)],
            time_flops,
        )

    def time_grad(l, grad_q, act):
        return grad_call(
            d,
            functools.partial(time_grad_kernel, d),
            f"time_grad{l}",
            TIME,
            ids,
            (grad_q, act),
            [],
            [time_scratch(d, d.half)],
        )

    grad_q1, grad_one, sums, tot_two1 = time_back(
        1, grad_two, q1, coef_two1, va, vb, s1, coef_one1
    )
    va, vb = data_sums(sums)
    time_outs1 = time_grad(1, grad_q1, act1)
    grad_s1, ga_part, tot_one1 = call(
        functools.partial(space_back_kernel, d),
        "space_back",
        [(smem(), ids)] + w_ins(space_w[1]) + v_ins(grad_one, s1, coef_one1, va, vb, count, mask),
        [sds(wide, BF), sds(narrow, BF), sds((8, d.half))],
        weight_scratch(d, SPACE)
        + [space_scratch(d, d.half), pltpu.VMEM((d.cells, channels), F32)],
        space_flops,
    )
    ga_other = swap(ga_part, "s")
    space_outs1 = grad_call(
        d,
        functools.partial(space_grad_kernel, d),
        "space_grad1",
        SPACE,
        ids,
        (a_mid, grad_s1),
        [],
        [space_scratch(d, d.half)],
    )
    grad_two, sums = call(
        join_back_kernel,
        "join_back",
        v_ins(ga_part, ga_other, q0, coef_two0, mask),
        [sds(narrow), sds((8, channels))],
        [],
        4 * d.cells * channels,
    )
    va, vb = data_sums(sums)
    grad_q0, grad_one, sums, tot_two0 = time_back(
        0, grad_two, q0, coef_two0, va, vb, s0, coef_one0
    )
    va, vb = data_sums(sums)
    time_outs0 = time_grad(0, grad_q0, act0)
    tot_one0, *space_outs0 = grad_call(
        d,
        functools.partial(last_space_grad_kernel, d),
        "space_grad0",
        SPACE,
        ids,
        (x, grad_one, s0, coef_one0, va, vb, count, mask),
        [sds((8, d.half))],
        [space_scratch(d, d.half)],
    )

    time_g1 = reduce_grad(d, s, u, time_outs1)
    space_g1 = reduce_grad(d, s, u, space_outs1)
    time_g0 = reduce_grad(d, s, u, time_outs0)
    space_g0 = reduce_grad(d, s, u, space_outs0)
    spatial_grad = jnp.stack([space_g0, space_g1]).transpose(2, 0, 1, 3)
    temporal_grad = jnp.stack([time_g0, time_g1]).transpose(2, 0, 1, 3)

    carried = jnp.concatenate([carried, swap(carried, "u")], axis=0).reshape(-1, 8, channels)
    pooled_all = carried[:, :clips].reshape(-1, channels)
    logit_all = carried[:, clips : 2 * clips].reshape(-1, channels)
    loss_sum = jnp.sum(logit_all[:, classes])
    logit_all = logit_all[:, :classes]
    bias_grad = jnp.sum(logit_all, axis=0)
    base = d.row_base(yy, s, u, z)
    pooled_mine = lax.dynamic_slice_in_dim(pooled_all, base, rows, 1)
    head_grad = lax.dot_general(
        pooled_mine.astype(BF),
        logit_all.astype(BF),
        (((0,), (0,)), ((), ())),
        preferred_element_type=F32,
    )

    ones = jnp.stack([tot_one0[:2], tot_one1[:2]])
    twos = jnp.stack([tot_two0[:2], tot_two1[:2]])
    small = jnp.concatenate([ones, twos], axis=-1)
    small = small + swap(small, "u")
    ones, twos = small[..., : d.half], small[..., d.half :]
    ones_other = swap(ones, "s")
    low, high = pick(s, ones, ones_other), pick(s, ones_other, ones)
    affine_grad = jnp.concatenate([low, high[..., : mid - d.half], twos], axis=-1)[:, ::-1]

    space_one, space_two, space_dir = adam_part(
        spatial_weight, spatial_grad, spatial_first, spatial_second, DECAY
    )
    time_one, time_two, time_dir = adam_part(
        temporal_weight, temporal_grad, temporal_first, temporal_second, DECAY
    )
    head_one, head_two, head_dir = adam_part(head_weight, head_grad, head_first, head_second, DECAY)
    affine_one, affine_two, affine_dir = adam_part(
        affine, affine_grad, affine_first, affine_second, 0.0
    )
    bias_one, bias_two, bias_dir = adam_part(head_bias, bias_grad, bias_first, bias_second, 0.0)

    def squares(a, b, c):
        return jnp.concatenate(
            [
                jnp.sum(a * a, axis=(0, 2, 3)),
                jnp.sum(b * b, axis=(0, 2, 3)),
                jnp.sum(c * c)[None],
            ]
        )

    both_squares = jnp.stack(
        [squares(spatial_weight, temporal_weight, head_weight), squares(space_dir, time_dir, head_dir)]
    )
    padded = jnp.pad(both_squares, ((0, 6), (0, LANES - 5)))
    padded = padded + swap(padded, "u")
    padded = padded + swap(padded, "s")
    padded = sum(data_sums(padded))
    norms = jnp.sqrt(padded[:2, :5])
    trust = norms[0] / norms[1]
    new_space = spatial_weight - RATE * trust[0:2][None, :, None, None] * space_dir
    new_time = temporal_weight - RATE * trust[2:4][None, :, None, None] * time_dir
    new_head = head_weight - RATE * trust[4] * head_dir
    new_affine = affine - RATE_SMALL * affine_dir
    new_bias = head_bias - RATE_SMALL * bias_dir
    return (
        loss_sum,
        space_one,
        space_two,
        new_space,
        time_one,
        time_two,
        new_time,
        head_one,
        head_two,
        new_head,
        affine_one,
        affine_two,
        new_affine,
        bias_one,
        bias_two,
        new_bias,
        norms,
    )


def solution(mesh):
    dp, tm = mesh.shape["dp"], mesh.shape["tm"]
    fine = Mesh(mesh.devices.reshape(dp // 4, 2, 2, tm), ALL)
    dp_axes = ("yy", "s", "u")
    owner = P(ALL)
    return jax.shard_map(
        on_device,
        mesh=fine,
        in_specs=(
            P(None, dp_axes, "tm"),
            P(None, dp_axes),
            P(None, dp_axes),
            owner,
            owner,
            owner,
            P(),
            P(),
            owner,
            owner,
            owner,
            owner,
            owner,
            owner,
            P(),
            P(),
            P(),
            P(),
        ),
        out_specs=(P(),) + (owner,) * 9 + (P(),) * 7,
        check_vma=False,
    )
```

```python
import functools

import jax
import jax.numpy as jnp
from jax import lax
from jax.experimental import pallas as pl
from jax.experimental.pallas import tpu as pltpu
from jax.sharding import Mesh
from jax.sharding import PartitionSpec as P

STEP = 5
EPS_NORM = 1e-05
EPS_ADAM = 1e-06
BETA_ONE = 0.5
BETA_TWO = 0.5
DECAY = 0.01
RATE = 0.3
RATE_SMALL = 0.1

F32 = jnp.float32
BF = jnp.bfloat16
LANES = 128
SPACE, TIME = 9, 3
ALL = ("yy", "s", "u", "tm")
DATA = ("yy", "tm")
MB = 1 << 20


def whole():
    return pl.BlockSpec(memory_space=pltpu.VMEM)


def anywhere():
    return pl.BlockSpec(memory_space=pl.ANY)


def smem():
    return pl.BlockSpec(memory_space=pltpu.SMEM)


def dot(a, b):
    return jnp.dot(a, b, preferred_element_type=F32)


def dot_nt(a, b):
    return lax.dot_general(a, b, (((1,), (1,)), ((), ())), preferred_element_type=F32)


class Dims:
    def __init__(self, clips, frames, height, width, channels, mid, rows, ny, nz):
        self.clips, self.frames, self.height, self.width = clips, frames, height, width
        self.channels, self.mid, self.rows, self.ny, self.nz = channels, mid, rows, ny, nz
        self.line = width * clips
        self.plane = height * self.line
        self.cells = frames * self.plane
        tiles = mid // LANES
        self.half = (tiles + 1) // 2 * LANES
        self.groups = ny * nz
        self.pieces = rows % 16 == 0 and ny == 2

    def row_base(self, yy, s, u, z):
        return (((yy * 2 + s) * 2 + u) * self.nz + z) * self.rows


class Weight:
    def __init__(self, kind, arrays, first, taps):
        self.kind, self.arrays, self.first, self.taps = kind, arrays, first, taps

    def part(self, first, taps):
        return Weight(self.kind, self.arrays, self.first + first, taps)

    def copies_needed(self, d):
        return 1 if self.kind == "natural" else 4 * d.groups

    def scratch(self, d):
        return [
            pltpu.VMEM((self.taps, d.channels, d.half), BF),
            pltpu.SemaphoreType.DMA((self.copies_needed(d),)),
        ]

    def places(self, d, ids):
        s, u, yy, z = (ids[i] for i in range(4))
        for urel in range(2):
            for i in range(d.groups):
                for srel in range(2):
                    if self.kind == "ring":
                        yrel, k = i // d.nz, i % d.nz
                        row = d.row_base(
                            yrel ^ yy, srel ^ s, urel ^ u, lax.rem(z + (d.nz - k), d.nz)
                        )
                        yield urel * d.groups + i, (srel,), row
                    else:
                        row = d.row_base(i // d.nz, srel ^ s, urel ^ u, i % d.nz)
                        yield urel, (i, srel), row

    def start(self, d, ids, refs, scratch, sems):
        taps = pl.ds(self.first, self.taps)
        copies = []
        if self.kind == "natural":
            copies.append(pltpu.make_async_copy(refs[0].at[taps], scratch, sems.at[0]))
        else:
            for operand, index, row in self.places(d, ids):
                copies.append(
                    pltpu.make_async_copy(
                        refs[operand].at[(*index, taps)],
                        scratch.at[:, pl.ds(pl.multiple_of(row, 16), d.rows), :],
                        sems.at[len(copies)],
                    )
                )
        for copy in copies:
            copy.start()
        return copies


def space_scratch(d, width):
    return pltpu.VMEM((3, d.frames, (d.height + 2) * d.line, width), BF)


def time_scratch(d, width):
    return pltpu.VMEM(((d.frames + 2) * d.plane, width), BF)


def fill_space(d, pad, values):
    cells, width = values.shape
    place = lax.broadcasted_iota(jnp.int32, (cells, width), 0)
    column = lax.rem(lax.div(place, d.clips), d.width)
    edge = jnp.zeros((3, d.frames, d.line, width), BF)
    pad[:, :, 0 : d.line, :] = edge
    pad[:, :, d.line + d.plane :, :] = edge
    left = jnp.where(column > 0, pltpu.roll(values, d.clips, 0), 0.0)
    right = jnp.where(column < d.width - 1, pltpu.roll(values, cells - d.clips, 0), 0.0)
    for j, moved in enumerate((left, values, right)):
        pad[j, :, d.line : d.line + d.plane, :] = moved.astype(BF).reshape(
            d.frames, d.plane, width
        )


def space_window(d, pad, i, j):
    start = pl.multiple_of(i * d.line, d.line)
    block = pad[j, :, pl.ds(start, d.plane), :]
    return block.reshape(d.cells, block.shape[-1])


def fill_time(d, pad, values):
    width = values.shape[1]
    edge = jnp.zeros((d.plane, width), BF)
    pad[0 : d.plane, :] = edge
    pad[d.plane + d.cells :, :] = edge
    pad[d.plane : d.plane + d.cells, :] = values


def time_window(d, pad, k):
    return pad[pl.ds(pl.multiple_of(k * d.plane, d.plane), d.cells), :]


def sums_of(first, second, extra=None):
    width = first.shape[1]
    rows = [jnp.sum(first, axis=0, keepdims=True), jnp.sum(second, axis=0, keepdims=True)]
    if extra is not None:
        rows.append(extra)
    rows.append(jnp.zeros((8 - len(rows), width), F32))
    return jnp.concatenate(rows, axis=0)


def coefs_of(total, count, gains):
    average = total[0:1] / count
    scale = lax.rsqrt(total[1:2] / count - average * average + EPS_NORM)
    return jnp.concatenate(
        [average, scale, gains[0:2], jnp.zeros((4, total.shape[1]), F32)], axis=0
    )


def normed_of(values, coef):
    return (values - coef[0:1]) * coef[1:2]


def act_slope(pre):
    sigma = jax.nn.sigmoid(pre)
    return sigma * (1.0 + pre * (1.0 - sigma))


def norm_back(grad_pre, normed, coef, total, count, mask):
    scale = coef[2:3] * coef[1:2]
    return mask * (scale * (grad_pre - (total[0:1] + normed * total[1:2]) / count))


def conv_space_into(d, acc, pad, weight):
    acc[...] = jnp.zeros_like(acc)

    @pl.loop(0, SPACE)
    def _(k):
        window = space_window(d, pad, lax.div(k, 3), lax.rem(k, 3))
        acc[...] += dot(window, weight[k])


def first_space_kernel(d, w, *refs):
    ids, *refs = refs
    w_refs, refs = refs[: len(w.arrays)], refs[len(w.arrays) :]
    x, mask, s_out, sums_out, weight, sems, pad = refs
    copies = w.start(d, ids, w_refs, weight, sems)
    fill_space(d, pad, x[...].astype(F32))
    for copy in copies:
        copy.wait()
    conv_space_into(d, s_out, pad, weight)
    m = mask[...]
    values = s_out[...]
    count = jnp.sum(m, axis=0, keepdims=True) + jnp.zeros((1, d.half), F32)
    sums_out[...] = sums_of(values * m, values * values * m, count)


def second_space_kernel(d, w, *refs):
    ids, *refs = refs
    w_refs, refs = refs[: len(w.arrays)], refs[len(w.arrays) :]
    q, va, vb, count, gains, mask, a_out, coef_out, s_out, sums_out, weight, sems, pad = refs
    copies = w.start(d, ids, w_refs, weight, sems)
    m = mask[...]
    coef = coefs_of(va[...] + vb[...], count[...], gains[...])
    coef_out[...] = coef
    pre = coef[2:3] * normed_of(q[...].astype(F32), coef) + coef[3:4]
    act = jax.nn.silu(pre) * m
    a_out[...] = act.astype(BF)
    fill_space(d, pad, act)
    for copy in copies:
        copy.wait()
    conv_space_into(d, s_out, pad, weight)
    values = s_out[...]
    sums_out[...] = sums_of(values * m, values * values * m)


def time_kernel(d, w, *refs):
    ids, *refs = refs
    w_refs, refs = refs[: len(w.arrays)], refs[len(w.arrays) :]
    s, va, vb, count, gains, mask, a_out, q_out, coef_out, weight, sems, pad = refs
    copies = w.start(d, ids, w_refs, weight, sems)
    coef = coefs_of(va[...] + vb[...], count[...], gains[...])
    coef_out[...] = coef
    pre = coef[2:3] * normed_of(s[...], coef) + coef[3:4]
    act = (jax.nn.silu(pre) * mask[...]).astype(BF)
    a_out[...] = act
    fill_time(d, pad, act)
    for copy in copies:
        copy.wait()
    total = dot_nt(time_window(d, pad, 0), weight[0])
    for k in range(1, TIME):
        total = total + dot_nt(time_window(d, pad, k), weight[k])
    q_out[...] = total.astype(BF)


def join_kernel(qa, qb, mask, q_out, sums_out):
    total = (qa[...].astype(F32) + qb[...].astype(F32)).astype(BF)
    q_out[...] = total
    values = total.astype(F32)
    m = mask[...]
    sums_out[...] = sums_of(values * m, values * values * m)


def head_kernel(d, w, denominator, classes, *refs):
    ids, *refs = refs
    w_refs, refs = refs[: len(w.arrays)], refs[len(w.arrays) :]
    q, va, vb, count, gains, mask, x, bias, clip_info, labels, *refs = refs
    coef_out, grad_out, sums_out, head, sems = refs
    copies = w.start(d, ids, w_refs, head, sems)
    m = mask[...]
    coef = coefs_of(va[...] + vb[...], count[...], gains[...])
    coef_out[...] = coef
    normed = normed_of(q[...].astype(F32), coef)
    pre = coef[2:3] * normed + coef[3:4] + x[...].astype(F32)
    sigma = jax.nn.sigmoid(pre)
    y = pre * sigma * m
    folded = jnp.sum(y.reshape(d.cells // 8, 8, d.channels), axis=0)
    step = d.clips
    total = folded
    for k in range(1, 8 // step):
        total = total + pltpu.roll(folded, k * step, 0)
    inverse = 1.0 / clip_info[:, 0:1]
    pooled = total * inverse
    pooled_bf = pooled.astype(BF)
    for copy in copies:
        copy.wait()
    weight = head[0, :, : d.channels]
    logits = dot(pooled_bf, weight) + bias[...]
    largest = jnp.max(logits, axis=1, keepdims=True)
    shifted = jnp.exp(logits - largest)
    log_total = largest + jnp.log(jnp.sum(shifted, axis=1, keepdims=True))
    lane = lax.broadcasted_iota(jnp.int32, logits.shape, 1)
    onehot = jnp.where(lane == labels[:, 0:1], 1.0, 0.0)
    inside = lane < classes
    kept = jnp.where(inside, logits, 0.0)
    loss = log_total - jnp.sum(kept * onehot, axis=1, keepdims=True)
    grad_logits = jnp.where(inside, (jnp.exp(logits - log_total) - onehot) / denominator, 0.0)
    grad_pooled = dot_nt(grad_logits.astype(BF), weight) * inverse
    grad_y = jnp.broadcast_to(grad_pooled[None], (d.cells // 8, 8, d.channels)).reshape(
        d.cells, d.channels
    )
    grad_pre = grad_y * m * (sigma * (1.0 + pre * (1.0 - sigma)))
    grad_out[...] = grad_pre
    sums_out[0:8, :] = sums_of(grad_pre, grad_pre * normed)
    carried = jnp.where(lane == classes, loss, grad_logits)
    sums_out[8:16, :] = jnp.concatenate(
        [
            pooled_bf.astype(F32)[0 : d.clips],
            carried[0 : d.clips],
            jnp.zeros((8 - 2 * d.clips, d.channels), F32),
        ],
        axis=0,
    )


def time_back_kernel(d, w, *refs):
    ids, *refs = refs
    w_refs, refs = refs[: len(w.arrays)], refs[len(w.arrays) :]
    grad_two, q, coef_two, va, vb, count, mask, s, coef_one, *refs = refs
    gq_out, grad_out, sums_out, tot_out, weight, sems, pad = refs
    copies = w.start(d, ids, w_refs, weight, sems)
    m = mask[...]
    total = va[...] + vb[...]
    tot_out[...] = total
    coef = coef_two[...]
    normed = normed_of(q[...].astype(F32), coef)
    grad_q = norm_back(grad_two[...], normed, coef, total, count[...], m).astype(BF)
    gq_out[...] = grad_q
    fill_time(d, pad, grad_q)
    for copy in copies:
        copy.wait()
    grad = dot(time_window(d, pad, TIME - 1), weight[0])
    for k in range(1, TIME):
        grad = grad + dot(time_window(d, pad, TIME - 1 - k), weight[k])
    grad = grad.astype(BF).astype(F32)
    coef = coef_one[...]
    normed = normed_of(s[...], coef)
    pre = coef[2:3] * normed + coef[3:4]
    grad_pre = grad * m * act_slope(pre)
    grad_out[...] = grad_pre
    sums_out[...] = sums_of(grad_pre, grad_pre * normed)


def space_back_kernel(d, w, *refs):
    ids, *refs = refs
    w_refs, refs = refs[: len(w.arrays)], refs[len(w.arrays) :]
    grad_pre, s, coef_one, va, vb, count, mask, *refs = refs
    gs_out, ga_out, tot_out, weight, sems, pad, acc = refs
    copies = w.start(d, ids, w_refs, weight, sems)
    total = va[...] + vb[...]
    tot_out[...] = total
    coef = coef_one[...]
    normed = normed_of(s[...], coef)
    grad_s = norm_back(grad_pre[...], normed, coef, total, count[...], mask[...])
    gs_out[...] = grad_s.astype(BF)
    fill_space(d, pad, grad_s)
    for copy in copies:
        copy.wait()
    acc[...] = jnp.zeros_like(acc)

    @pl.loop(0, SPACE)
    def _(k):
        window = space_window(d, pad, 2 - lax.div(k, 3), 2 - lax.rem(k, 3))
        acc[...] += dot_nt(window, weight[k])

    ga_out[...] = acc[...].astype(BF)


def join_back_kernel(ga, gb, q, coef_two, mask, grad_out, sums_out):
    coef = coef_two[...]
    normed = normed_of(q[...].astype(F32), coef)
    pre = coef[2:3] * normed + coef[3:4]
    grad = ga[...].astype(F32) + gb[...].astype(F32)
    grad_pre = grad * mask[...] * act_slope(pre)
    grad_out[...] = grad_pre
    sums_out[...] = sums_of(grad_pre, grad_pre * normed)


def write_grad(d, w, ids, value, outs, held):
    if w.kind == "natural":
        outs[0][0] = value.astype(BF)
        return
    held[...] = value.astype(BF)
    for operand, index, row in w.places(d, ids):
        block = held[pl.ds(pl.multiple_of(row, 16), d.rows), :]
        outs[operand][(*index, 0)] = block


def time_grad_kernel(d, w, *refs):
    ids, grad_q, act, *refs = refs
    outs, (pad, turned, held) = refs[:-3], refs[-3:]
    k = pl.program_id(0)

    @pl.when(k == 0)
    def _():
        fill_time(d, pad, act[...])
        turned[...] = jnp.transpose(grad_q[...].astype(F32)).astype(BF)

    write_grad(d, w, ids, dot(turned[...], time_window(d, pad, k)), outs, held)


def space_grad_kernel(d, w, *refs):
    ids, a, grad_s, *refs = refs
    outs, (pad, turned, held) = refs[:-3], refs[-3:]
    k = pl.program_id(0)

    @pl.when(k == 0)
    def _():
        fill_space(d, pad, grad_s[...].astype(F32))
        turned[...] = jnp.transpose(a[...].astype(F32)).astype(BF)

    window = space_window(d, pad, 2 - lax.div(k, 3), 2 - lax.rem(k, 3))
    write_grad(d, w, ids, dot(turned[...], window), outs, held)


def last_space_grad_kernel(d, w, *refs):
    ids, a, grad_pre, s, coef_one, va, vb, count, mask, tot_out, *refs = refs
    outs, (pad, turned, held) = refs[:-3], refs[-3:]
    k = pl.program_id(0)

    @pl.when(k == 0)
    def _():
        total = va[...] + vb[...]
        tot_out[...] = total
        coef = coef_one[...]
        normed = normed_of(s[...], coef)
        grad_s = norm_back(grad_pre[...], normed, coef, total, count[...], mask[...])
        fill_space(d, pad, grad_s)
        turned[...] = jnp.transpose(a[...].astype(F32)).astype(BF)

    window = space_window(d, pad, 2 - lax.div(k, 3), 2 - lax.rem(k, 3))
    write_grad(d, w, ids, dot(turned[...], window), outs, held)


def sds(shape, dtype=F32):
    return jax.ShapeDtypeStruct(shape, dtype)


def call(body, name, ins, outs, scratch, flops, megabytes=40):
    return pl.pallas_call(
        body,
        name=name,
        out_shape=outs,
        in_specs=[spec for spec, _ in ins],
        out_specs=[whole()] * len(outs),
        scratch_shapes=scratch,
        compiler_params=pltpu.CompilerParams(vmem_limit_bytes=megabytes * MB),
        cost_estimate=pl.CostEstimate(flops=flops, bytes_accessed=8 * MB, transcendentals=0),
    )(*[value for _, value in ins])


def w_ins(weight):
    return [(anywhere(), piece) for piece in weight.arrays]


def v_ins(*values):
    return [(whole(), value) for value in values]


def grad_call(d, body, name, kind, taps, ids, values, first_outs, scratch):
    if kind == "ring":
        shape, count = (2, taps, d.rows, d.half), 2 * d.groups
        spec = pl.BlockSpec((2, 1, d.rows, d.half), lambda k: (0, k, 0, 0))
    elif kind == "all":
        shape, count = (d.groups, 2, taps, d.rows, d.half), 2
        spec = pl.BlockSpec((d.groups, 2, 1, d.rows, d.half), lambda k: (0, 0, k, 0, 0))
    else:
        shape, count = (taps, d.channels, d.half), 1
        spec = pl.BlockSpec((1, d.channels, d.half), lambda k: (k, 0, 0))
    fixed = [pl.BlockSpec(out.shape, lambda k: (0, 0)) for out in first_outs]
    outs = pl.pallas_call(
        functools.partial(body, d, Weight(kind, (), 0, 1)),
        name=name,
        grid=(taps,),
        out_shape=list(first_outs) + [sds(shape, BF)] * count,
        in_specs=[smem()] + [whole()] * len(values),
        out_specs=fixed + [spec] * count,
        scratch_shapes=scratch
        + [pltpu.VMEM((d.channels, d.cells), BF), pltpu.VMEM((d.channels, d.half), BF)],
        compiler_params=pltpu.CompilerParams(vmem_limit_bytes=40 * MB),
        cost_estimate=pl.CostEstimate(
            flops=2 * taps * d.cells * d.channels * d.half,
            bytes_accessed=8 * MB,
            transcendentals=0,
        ),
    )(ids, *values)
    return outs[: len(first_outs)], outs[len(first_outs) :]


def swap(value, axis, distance=1):
    size = lax.axis_size(axis)
    return lax.ppermute(value, axis, [(i, i ^ distance) for i in range(size)])


def data_hops():
    hops = []
    for axis in DATA:
        distance = 1
        while distance < lax.axis_size(axis):
            hops.append((axis, distance))
            distance *= 2
    return hops


def data_sums(values):
    hops = data_hops()
    for axis, distance in hops[:-1]:
        values = values + swap(values, axis, distance)
    return values, swap(values, *hops[-1])


def data_sums_gather(values):
    hops = data_hops()
    for axis, distance in hops[:-1]:
        other = swap(values, axis, distance)
        values = jnp.concatenate([values[:8] + other[:8], values[8:], other[8:]], axis=0)
    other = swap(values, *hops[-1])
    return values[:8], other[:8], jnp.concatenate([values[8:], other[8:]], axis=0)


def pick(index, first, second):
    return jnp.where(index == 0, first, second)


def after(value, *earlier):
    return lax.optimization_barrier((value, *earlier))[0]


def turn(value):
    size = lax.axis_size("tm")
    return lax.ppermute(value, "tm", [(i, (i + 1) % size) for i in range(size)])


def gather_ring(both):
    held, across = [both], [swap(both, "yy")]
    for _ in range(lax.axis_size("tm") - 1):
        held.append(turn(held[-1]))
        across.append(swap(held[-1], "yy"))
    own = held + across
    return Weight("ring", own + [swap(block, "u") for block in own], 0, both.shape[1])


def gather_all(d, s, u, both, *earlier):
    own = lax.all_gather(both, DATA, axis=0, tiled=False)
    own = after(own, *earlier) if earlier else own
    sibling = swap(own, "u")
    taps = both.shape[1]
    if d.pieces:
        return Weight("all", (own, sibling), 0, taps)
    parts = jnp.stack([own, sibling]).reshape(2, d.ny, d.nz, 2, taps, d.rows, d.half)
    parts = jnp.where(u == 0, parts, parts[::-1])
    parts = jnp.where(s == 0, parts, parts[:, :, :, ::-1])
    natural = parts.transpose(4, 1, 3, 0, 2, 5, 6).reshape(taps, d.channels, d.half)
    return Weight("natural", (natural,), 0, taps)


def added(*values):
    total = values[0].astype(F32)
    for value in values[1:]:
        total = total + value.astype(F32)
    return total.astype(BF)


def reduce_ring(d, outs):
    n = d.nz
    keep, send = outs[: d.groups], outs[d.groups :]
    moving = None
    for k in list(range(1, n)) + [0]:
        across = swap(added(keep[n + k], swap(send[n + k], "u")), "yy")
        terms = [keep[k], swap(send[k], "u"), across]
        if moving is not None:
            terms.append(turn(moving))
        moving = added(*terms)
    return moving


def reduce_all(d, s, u, kind, out_lists):
    if kind == "all":
        both = jnp.concatenate(
            [added(keep, swap(send, "u")) for keep, send in out_lists], axis=2
        )
    else:
        natural = jnp.concatenate([outs[0] for outs in out_lists], axis=0)
        taps = natural.shape[0]
        parts = natural.reshape(taps, d.ny, 2, 2, d.nz, d.rows, d.half)
        parts = parts.transpose(3, 1, 4, 2, 0, 5, 6)
        parts = jnp.where(u == 0, parts, parts[::-1])
        parts = jnp.where(s == 0, parts, parts[:, :, :, ::-1])
        keep, send = parts.reshape(2, d.groups, 2, taps, d.rows, d.half)
        both = added(keep, swap(send, "u"))
    return lax.psum_scatter(both, DATA, scatter_dimension=0, tiled=False)


def own_rows(d, s, mine):
    other = swap(mine[1], "s")
    first = pick(s, mine[0], other)
    second = pick(s, other, mine[0])
    return jnp.concatenate([first, second[..., : d.mid - d.half]], axis=-1).astype(F32)


def halves(d, values):
    fill = [(0, 0)] * (values.ndim - 1) + [(0, 2 * d.half - d.mid)]
    return values[..., : d.half], jnp.pad(values[..., d.half :], fill)


def rows_of(gain, shift):
    return jnp.concatenate(
        [gain[None], shift[None], jnp.zeros((6, gain.shape[0]), F32)], axis=0
    )


def adam_part(weight, gradient, moment_one, moment_two, decay):
    new_one = BETA_ONE * moment_one + (1.0 - BETA_ONE) * gradient
    new_two = BETA_TWO * moment_two + (1.0 - BETA_TWO) * gradient * gradient
    direction = (
        new_one / (1.0 - BETA_ONE**STEP) / (jnp.sqrt(new_two / (1.0 - BETA_TWO**STEP)) + EPS_ADAM)
        + decay * weight
    )
    return (new_one, new_two, direction)


def on_device(
    clips_x,
    frames,
    labels,
    spatial_weight,
    temporal_weight,
    head_weight,
    affine,
    head_bias,
    spatial_first,
    spatial_second,
    temporal_first,
    temporal_second,
    head_first,
    head_second,
    affine_first,
    affine_second,
    bias_first,
    bias_second,
):
    s, u, z, yy = (lax.axis_index(axis) for axis in ("s", "u", "tm", "yy"))
    ny, nz = lax.axis_size("yy"), lax.axis_size("tm")
    micro, clips, _, height, width, channels = clips_x.shape
    mid = spatial_weight.shape[3]
    rows = spatial_weight.shape[0]
    classes = head_weight.shape[1]
    d = Dims(clips, nz, height, width, channels, mid, rows, ny, nz)
    assert nz == 4 and micro == 2
    ids = jnp.stack([s, u, yy, z]).astype(jnp.int32)
    denominator = micro * clips * 4 * ny

    def prepared(weight, l):
        moved = weight[:, l].astype(BF).transpose(1, 0, 2)
        return halves(d, moved)

    head_slot = jnp.pad(head_weight.astype(BF), ((0, 0), (0, d.half - classes)))[None]
    space_parts = [prepared(spatial_weight, l) for l in range(2)]
    time_parts = [prepared(temporal_weight, l) for l in range(2)]

    def paired(parts):
        first = jnp.concatenate([part[0] for part in parts], axis=0)
        second = jnp.concatenate([part[1] for part in parts], axis=0)
        own = pick(s, first, second)
        return jnp.stack([own, swap(pick(s, second, first), "s")])

    early = paired([space_parts[0], time_parts[0]])
    late = paired([space_parts[1], time_parts[1], (head_slot, head_slot)])
    if d.pieces:
        early_w = gather_ring(early)
    else:
        early_w = gather_all(d, s, u, early)

    def by_index(index, mine, other):
        return jnp.stack([pick(index, mine, other), pick(index, other, mine)])

    kept = pick(u, clips_x[0], clips_x[1])
    other = swap(pick(u, clips_x[1], clips_x[0]), "u")
    pair = by_index(u, kept, other)
    four = by_index(s, pair, swap(pair, "s"))
    four = four.reshape(nz, clips, height * width, channels)
    clip_all = lax.all_to_all(four, "tm", split_axis=0, concat_axis=0, tiled=True)
    x = clip_all.reshape(nz, clips, height * width, channels)
    x = x.transpose(0, 2, 1, 3).reshape(d.cells, channels)

    info = jnp.stack([frames, labels]).transpose(1, 0, 2)
    kept_info = pick(u, info[0], info[1])
    pair_info = by_index(u, kept_info, swap(pick(u, info[1], info[0]), "u"))
    four_info = by_index(s, pair_info, swap(pair_info, "s")).reshape(nz, 2, clips)
    mine_info = lax.dynamic_index_in_dim(four_info, z, 0, keepdims=False)
    my_frames, my_labels = mine_info[0], mine_info[1]
    valid = (jnp.arange(nz, dtype=jnp.int32)[:, None] * 8 < my_frames[None, :]).astype(F32)
    mask = jnp.broadcast_to(valid[:, None, :], (nz, height * width, clips)).reshape(d.cells, 1)
    divisor = (my_frames // 8).astype(F32) * (height * width)
    clip_info = jnp.broadcast_to(jnp.tile(divisor, 8 // clips)[:, None], (8, LANES))
    label_rows = jnp.broadcast_to(jnp.tile(my_labels, 8 // clips)[:, None], (8, LANES))
    bias_row = jnp.full((1, channels), -1e30, F32).at[0, :classes].set(head_bias)

    gains_one, gains_two = [], []
    for l in range(2):
        low, high = halves(d, affine[l, :, :mid])
        mine = pick(s, low, high)
        gains_one.append(rows_of(mine[0], mine[1]))
        gains_two.append(rows_of(affine[l, 0, mid:], affine[l, 1, mid:]))

    wide, narrow = (d.cells, d.half), (d.cells, channels)
    space_flops = 2 * d.cells * SPACE * channels * d.half
    time_flops = 2 * d.cells * TIME * channels * d.half

    space_w = [early_w.part(0, SPACE), None]
    time_w = [early_w.part(SPACE, TIME), None]

    def space_first(x_bf):
        return call(
            functools.partial(first_space_kernel, d, space_w[0]),
            "space0",
            [(smem(), ids)] + w_ins(space_w[0]) + v_ins(x_bf, mask),
            [sds(wide), sds((8, d.half))],
            space_w[0].scratch(d) + [space_scratch(d, channels)],
            space_flops,
        )

    def space_next(q, va, vb, count):
        return call(
            functools.partial(second_space_kernel, d, space_w[1]),
            "space1",
            [(smem(), ids)] + w_ins(space_w[1]) + v_ins(q, va, vb, count, gains_two[0], mask),
            [sds(narrow, BF), sds((8, channels)), sds(wide), sds((8, d.half))],
            space_w[1].scratch(d) + [space_scratch(d, channels)],
            space_flops,
        )

    def time_next(l, s_value, va, vb, count):
        return call(
            functools.partial(time_kernel, d, time_w[l]),
            f"time{l}",
            [(smem(), ids)] + w_ins(time_w[l]) + v_ins(s_value, va, vb, count, gains_one[l], mask),
            [sds(wide, BF), sds(narrow, BF), sds((8, d.half))],
            time_w[l].scratch(d) + [time_scratch(d, d.half)],
            time_flops,
        )

    def joined(q_part):
        return call(
            join_kernel,
            "join",
            v_ins(q_part, swap(q_part, "s"), mask),
            [sds(narrow, BF), sds((8, channels))],
            [],
            d.cells * channels,
        )

    s0, sums = space_first(x)
    va, vb = data_sums(sums)
    count = va[2:3, 0:1] + vb[2:3, 0:1]
    late_w = gather_all(d, s, u, late, va)
    space_w[1] = late_w.part(0, SPACE)
    time_w[1] = late_w.part(SPACE, TIME)
    head_w = late_w.part(SPACE + TIME, 1)
    act0, q_part, coef_one0 = time_next(0, s0, va, vb, count)
    q0, sums = joined(q_part)
    va, vb = data_sums(sums)
    a_mid, coef_two0, s1, sums = space_next(q0, va, vb, count)
    va, vb = data_sums(sums)
    act1, q_part, coef_one1 = time_next(1, s1, va, vb, count)
    q1, sums = joined(q_part)
    va, vb = data_sums(sums)
    coef_two1, grad_two, sums = call(
        functools.partial(head_kernel, d, head_w, float(denominator), classes),
        "head",
        [(smem(), ids)]
        + w_ins(head_w)
        + v_ins(q1, va, vb, count, gains_two[1], mask, x, bias_row, clip_info, label_rows),
        [sds((8, channels)), sds(narrow), sds((16, channels))],
        head_w.scratch(d),
        4 * d.cells * channels,
    )
    va, vb, carried = data_sums_gather(sums)

    def time_back(l, grad, q, coef_two, va, vb, s_value, coef_one):
        return call(
            functools.partial(time_back_kernel, d, time_w[l]),
            f"time_back{l}",
            [(smem(), ids)]
            + w_ins(time_w[l])
            + v_ins(grad, q, coef_two, va, vb, count, mask, s_value, coef_one),
            [sds(narrow, BF), sds(wide), sds((8, d.half)), sds((8, channels))],
            time_w[l].scratch(d) + [time_scratch(d, channels)],
            time_flops,
        )

    late_kind = "all" if d.pieces else "natural"
    early_kind = "ring" if d.pieces else "natural"

    def time_grad(l, grad_q, act):
        return grad_call(
            d,
            time_grad_kernel,
            f"time_grad{l}",
            late_kind if l else early_kind,
            TIME,
            ids,
            (grad_q, act),
            [],
            [time_scratch(d, d.half)],
        )[1]

    grad_q1, grad_one, sums, tot_two1 = time_back(
        1, grad_two, q1, coef_two1, va, vb, s1, coef_one1
    )
    va, vb = data_sums(sums)
    time_outs1 = time_grad(1, grad_q1, act1)
    grad_s1, ga_part, tot_one1 = call(
        functools.partial(space_back_kernel, d, space_w[1]),
        "space_back",
        [(smem(), ids)] + w_ins(space_w[1]) + v_ins(grad_one, s1, coef_one1, va, vb, count, mask),
        [sds(wide, BF), sds(narrow, BF), sds((8, d.half))],
        space_w[1].scratch(d)
        + [space_scratch(d, d.half), pltpu.VMEM((d.cells, channels), F32)],
        space_flops,
    )
    ga_other = swap(ga_part, "s")
    _, space_outs1 = grad_call(
        d,
        space_grad_kernel,
        "space_grad1",
        late_kind,
        SPACE,
        ids,
        (a_mid, grad_s1),
        [],
        [space_scratch(d, d.half)],
    )
    grad_two, sums = call(
        join_back_kernel,
        "join_back",
        v_ins(ga_part, after(ga_other, *space_outs1), q0, coef_two0, mask),
        [sds(narrow), sds((8, channels))],
        [],
        4 * d.cells * channels,
    )
    va, vb = data_sums(sums)
    grad_q0, grad_one, sums, tot_two0 = time_back(
        0, grad_two, q0, coef_two0, va, vb, s0, coef_one0
    )
    va, vb = data_sums(sums)
    time_outs0 = time_grad(0, grad_q0, act0)
    (tot_one0,), space_outs0 = grad_call(
        d,
        last_space_grad_kernel,
        "space_grad0",
        early_kind,
        SPACE,
        ids,
        (x, grad_one, s0, coef_one0, va, vb, count, mask),
        [sds((8, d.half))],
        [space_scratch(d, d.half)],
    )

    late_sum = reduce_all(d, s, u, late_kind, [space_outs1, time_outs1])
    late_sum = own_rows(d, s, after(late_sum, *space_outs0))
    if d.pieces:
        early_sum = reduce_ring(
            d, [jnp.concatenate(pair, axis=1) for pair in zip(space_outs0, time_outs0)]
        )
    else:
        early_sum = reduce_all(d, s, u, early_kind, [space_outs0, time_outs0])
    early_sum = own_rows(d, s, early_sum)

    carried = jnp.concatenate([carried, swap(carried, "u")], axis=0).reshape(-1, 8, channels)
    pooled_all = carried[:, :clips].reshape(-1, channels)
    logit_all = carried[:, clips : 2 * clips].reshape(-1, channels)
    loss_sum = jnp.sum(logit_all[:, classes])
    logit_all = logit_all[:, :classes]
    bias_grad = jnp.sum(logit_all, axis=0)
    base = d.row_base(yy, s, u, z)
    pooled_mine = lax.dynamic_slice_in_dim(pooled_all, base, rows, 1)
    head_grad = lax.dot_general(
        pooled_mine.astype(BF),
        logit_all.astype(BF),
        (((0,), (0,)), ((), ())),
        preferred_element_type=F32,
    )

    ones = jnp.stack([tot_one0[:2], tot_one1[:2]])
    twos = jnp.stack([tot_two0[:2], tot_two1[:2]])
    small = jnp.concatenate([ones, twos], axis=-1)
    small = small + swap(small, "u")
    ones, twos = small[..., : d.half], small[..., d.half :]
    ones_other = swap(ones, "s")
    low, high = pick(s, ones, ones_other), pick(s, ones_other, ones)
    both = jnp.concatenate([low, high[..., : mid - d.half], twos], axis=-1)
    affine_grad = jnp.stack([both[:, 1], both[:, 0]], axis=1)

    def step(weight, first, second, gradients):
        return [
            (moved[0],) + adam_part(moved[0], gradient, moved[1], moved[2], DECAY)
            for l, gradient in enumerate(gradients)
            for moved in [[v[:, l].transpose(1, 0, 2) for v in (weight, first, second)]]
        ]

    def joined_units(parts):
        return jnp.stack(parts).transpose(2, 0, 1, 3)

    space_steps = step(
        spatial_weight, spatial_first, spatial_second, (early_sum[:SPACE], late_sum[:SPACE])
    )
    time_steps = step(
        temporal_weight, temporal_first, temporal_second, (early_sum[SPACE:], late_sum[SPACE:])
    )
    head_one, head_two, head_dir = adam_part(head_weight, head_grad, head_first, head_second, DECAY)
    affine_one, affine_two, affine_dir = adam_part(
        affine, affine_grad, affine_first, affine_second, 0.0
    )
    bias_one, bias_two, bias_dir = adam_part(head_bias, bias_grad, bias_first, bias_second, 0.0)

    steps = space_steps + time_steps
    dir_squares = [jnp.sum(part[3] * part[3]) for part in steps] + [jnp.sum(head_dir * head_dir)]
    weight_squares = [jnp.sum(part[0] * part[0]) for part in steps]
    weight_squares.append(jnp.sum(head_weight * head_weight))
    both_squares = jnp.stack([jnp.stack(weight_squares), jnp.stack(dir_squares)])
    padded = jnp.pad(both_squares, ((0, 6), (0, LANES - 5)))
    padded = padded + swap(padded, "u")
    padded = padded + swap(padded, "s")
    padded = sum(data_sums(padded))
    norms = jnp.sqrt(padded[:2, :5])
    trust = norms[0] / norms[1]
    new = [part[0] - RATE * trust[i] * part[3] for i, part in enumerate(steps)]
    space_one, space_two = (joined_units([part[i] for part in space_steps]) for i in (1, 2))
    time_one, time_two = (joined_units([part[i] for part in time_steps]) for i in (1, 2))
    new_space, new_time = joined_units(new[:2]), joined_units(new[2:])
    new_head = head_weight - RATE * trust[4] * head_dir
    new_affine = affine - RATE_SMALL * affine_dir
    new_bias = head_bias - RATE_SMALL * bias_dir
    return (
        loss_sum,
        space_one,
        space_two,
        new_space,
        time_one,
        time_two,
        new_time,
        head_one,
        head_two,
        new_head,
        affine_one,
        affine_two,
        new_affine,
        bias_one,
        bias_two,
        new_bias,
        norms,
    )


def solution(mesh):
    dp, tm = mesh.shape["dp"], mesh.shape["tm"]
    fine = Mesh(mesh.devices.reshape(dp // 4, 2, 2, tm), ALL)
    dp_axes = ("yy", "s", "u")
    owner = P(ALL)
    return jax.shard_map(
        on_device,
        mesh=fine,
        in_specs=(
            P(None, dp_axes, "tm"),
            P(None, dp_axes),
            P(None, dp_axes),
            owner,
            owner,
            owner,
            P(),
            P(),
            owner,
            owner,
            owner,
            owner,
            owner,
            owner,
            P(),
            P(),
            P(),
            P(),
        ),
        out_specs=(P(),) + (owner,) * 9 + (P(),) * 7,
        check_vma=False,
    )
```

```python
import functools

import jax
import jax.numpy as jnp
from jax import lax
from jax.experimental import pallas as pl
from jax.experimental.layout import Layout, with_layout_constraint
from jax.experimental.pallas import tpu as pltpu
from jax.sharding import Mesh
from jax.sharding import PartitionSpec as P

STEP = 5
EPS_NORM = 1e-05
EPS_ADAM = 1e-06
BETA_ONE = 0.5
BETA_TWO = 0.5
DECAY = 0.01
RATE = 0.3
RATE_SMALL = 0.1

F32 = jnp.float32
BF = jnp.bfloat16
LANES = 128
SPACE, TIME = 9, 3
ALL = ("yy", "s", "u", "tm")
DATA = ("yy", "tm")
MB = 1 << 20


def whole():
    return pl.BlockSpec(memory_space=pltpu.VMEM)


def in_hbm():
    return pl.BlockSpec(memory_space=pltpu.HBM)


def smem():
    return pl.BlockSpec(memory_space=pltpu.SMEM)


def dot(a, b):
    return jnp.dot(a, b, preferred_element_type=F32)


def dot_nt(a, b):
    return lax.dot_general(a, b, (((1,), (1,)), ((), ())), preferred_element_type=F32)


class Dims:
    def __init__(self, clips, frames, height, width, channels, mid, rows, ny, nz):
        self.clips, self.frames, self.height, self.width = clips, frames, height, width
        self.channels, self.mid, self.rows, self.ny, self.nz = channels, mid, rows, ny, nz
        self.line = width * clips
        self.plane = height * self.line
        self.cells = frames * self.plane
        tiles = mid // LANES
        self.half = (tiles + 1) // 2 * LANES
        self.groups = ny * nz
        self.pieces = rows % 16 == 0 and ny == 2

    def row_base(self, yy, s, u, z):
        return (((yy * 2 + s) * 2 + u) * self.nz + z) * self.rows


class Weight:
    def __init__(self, kind, arrays, first, taps):
        self.kind, self.arrays, self.first, self.taps = kind, arrays, first, taps

    def part(self, first, taps):
        return Weight(self.kind, self.arrays, self.first + first, taps)

    def copies_needed(self, d):
        return 1 if self.kind == "natural" else 4 * d.groups

    def scratch(self, d):
        return [
            pltpu.VMEM((self.taps, d.channels, d.half), BF),
            pltpu.SemaphoreType.DMA((self.copies_needed(d),)),
        ]

    def places(self, d, ids):
        s, u, yy, z = (ids[i] for i in range(4))
        for urel in range(2):
            for i in range(d.groups):
                for srel in range(2):
                    if self.kind in ("blocks", "ring"):
                        yrel, k = i // d.nz, i % d.nz
                        row = d.row_base(
                            yrel ^ yy, srel ^ s, urel ^ u, lax.rem(z + (d.nz - k), d.nz)
                        )
                        if self.kind == "blocks":
                            yield urel * d.groups + i, (srel,), row
                        else:
                            yield urel * 2 + yrel, (k, srel), row
                    else:
                        row = d.row_base(i // d.nz, srel ^ s, urel ^ u, i % d.nz)
                        if self.kind == "all" or urel == 0:
                            yield urel, (i, srel), row
                        else:
                            yield 1 + i // 2, (i % 2, srel), row

    def start(self, d, ids, refs, scratch, sems):
        taps = pl.ds(self.first, self.taps)
        copies = []
        if self.kind == "natural":
            copies.append(pltpu.make_async_copy(refs[0].at[taps], scratch, sems.at[0]))
        else:
            for operand, index, row in self.places(d, ids):
                copies.append(
                    pltpu.make_async_copy(
                        refs[operand].at[(*index, taps)],
                        scratch.at[:, pl.ds(pl.multiple_of(row, 16), d.rows), :],
                        sems.at[len(copies)],
                    )
                )
        for copy in copies:
            copy.start()
        return copies


def space_scratch(d, width):
    return pltpu.VMEM((d.frames, (d.height + 2) * d.line, 3 * width), BF)


def time_scratch(d, width):
    return pltpu.VMEM(((d.frames + 2) * d.plane, width), BF)


def fill_space(d, pad, values):
    cells, width = values.shape
    place = lax.broadcasted_iota(jnp.int32, (cells, width), 0)
    column = lax.rem(lax.div(place, d.clips), d.width)
    edge = jnp.zeros((d.frames, d.line, 3 * width), BF)
    pad[:, 0 : d.line, :] = edge
    pad[:, d.line + d.plane :, :] = edge
    left = jnp.where(column > 0, pltpu.roll(values, d.clips, 0), 0.0)
    right = jnp.where(column < d.width - 1, pltpu.roll(values, cells - d.clips, 0), 0.0)
    for j, moved in enumerate((left, values, right)):
        block = moved.astype(BF).reshape(d.frames, d.plane, width)
        pad[:, d.line : d.line + d.plane, j * width : (j + 1) * width] = block


def space_window(d, pad, i, j=None):
    rows = pl.ds(pl.multiple_of(i * d.line, d.line), d.plane)
    if j is None:
        block = pad[:, rows, :]
    else:
        width = pad.shape[-1] // 3
        block = pad[:, rows, pl.ds(pl.multiple_of(j * width, LANES), width)]
    return block.reshape(d.cells, block.shape[-1])


def fill_time(d, pad, values):
    width = values.shape[1]
    edge = jnp.zeros((d.plane, width), BF)
    pad[0 : d.plane, :] = edge
    pad[d.plane + d.cells :, :] = edge
    pad[d.plane : d.plane + d.cells, :] = values


def time_window(d, pad, k):
    return pad[pl.ds(pl.multiple_of(k * d.plane, d.plane), d.cells), :]


def sums_of(first, second, extra=None):
    width = first.shape[1]
    rows = [jnp.sum(first, axis=0, keepdims=True), jnp.sum(second, axis=0, keepdims=True)]
    if extra is not None:
        rows.append(extra)
    rows.append(jnp.zeros((8 - len(rows), width), F32))
    return jnp.concatenate(rows, axis=0)


def total_of(d, ids, terms):
    z = ids[3]
    values = [term[...] for term in terms]
    total = None
    for place in range(d.nz):
        here = values[0]
        for k in range(1, d.nz):
            here = jnp.where(lax.rem(z + (d.nz - k), d.nz) == place, values[k], here)
        total = here if total is None else total + here
    return total


def coefs_of(total, count, gains):
    average = total[0:1] / count
    scale = lax.rsqrt(total[1:2] / count - average * average + EPS_NORM)
    return jnp.concatenate(
        [
            average,
            scale,
            gains[0:2],
            jnp.broadcast_to(count, average.shape),
            jnp.zeros((3, total.shape[1]), F32),
        ],
        axis=0,
    )


def normed_of(values, coef):
    return (values - coef[0:1]) * coef[1:2]


def act_slope(pre):
    sigma = jax.nn.sigmoid(pre)
    return sigma * (1.0 + pre * (1.0 - sigma))


def norm_back(grad_pre, normed, coef, total, count, mask):
    scale = coef[2:3] * coef[1:2]
    return mask * (scale * (grad_pre - (total[0:1] + normed * total[1:2]) / count))


def conv_space_into(d, acc, pad, weight):
    for i in range(3):
        three = weight[3 * i : 3 * i + 3].reshape(3 * d.channels, d.half)
        part = dot(space_window(d, pad, i), three)
        acc[...] = part if i == 0 else acc[...] + part


def first_space_kernel(d, w, *refs):
    ids, *refs = refs
    w_refs, refs = refs[: len(w.arrays)], refs[len(w.arrays) :]
    x, mask, s_out, sums_out, weight, sems, pad = refs
    copies = w.start(d, ids, w_refs, weight, sems)
    fill_space(d, pad, x[...].astype(F32))
    for copy in copies:
        copy.wait()
    conv_space_into(d, s_out, pad, weight)
    m = mask[...]
    values = s_out[...]
    count = jnp.sum(m, axis=0, keepdims=True) + jnp.zeros((1, d.half), F32)
    sums_out[...] = sums_of(values * m, values * values * m, count)


def second_space_kernel(d, w, *refs):
    ids, *refs = refs
    w_refs, refs = refs[: len(w.arrays)], refs[len(w.arrays) :]
    terms, refs = refs[: d.nz], refs[d.nz :]
    q, count, gains, mask, a_out, coef_out, s_out, sums_out, weight, sems, pad = refs
    copies = w.start(d, ids, w_refs, weight, sems)
    m = mask[...]
    coef = coefs_of(total_of(d, ids, terms), count[4:5, 0:1], gains[...])
    coef_out[...] = coef
    pre = coef[2:3] * normed_of(q[...].astype(F32), coef) + coef[3:4]
    act = jax.nn.silu(pre) * m
    a_out[...] = act.astype(BF)
    fill_space(d, pad, act)
    for copy in copies:
        copy.wait()
    conv_space_into(d, s_out, pad, weight)
    values = s_out[...]
    sums_out[...] = sums_of(values * m, values * values * m)


def time_kernel(d, w, *refs):
    ids, *refs = refs
    w_refs, refs = refs[: len(w.arrays)], refs[len(w.arrays) :]
    terms, refs = refs[: d.nz], refs[d.nz :]
    s, *counts, gains, mask, a_out, q_out, coef_out, weight, sems, pad = refs
    copies = w.start(d, ids, w_refs, weight, sems)
    total = total_of(d, ids, terms)
    count = counts[0][4:5, 0:1] if counts else total[2:3, 0:1]
    coef = coefs_of(total, count, gains[...])
    coef_out[...] = coef
    pre = coef[2:3] * normed_of(s[...], coef) + coef[3:4]
    act = (jax.nn.silu(pre) * mask[...]).astype(BF)
    a_out[...] = act
    fill_time(d, pad, act)
    for copy in copies:
        copy.wait()
    total = dot_nt(time_window(d, pad, 0), weight[0])
    for k in range(1, TIME):
        total = total + dot_nt(time_window(d, pad, k), weight[k])
    q_out[...] = total.astype(BF)


def join_kernel(qa, qb, mask, q_out, sums_out):
    total = (qa[...].astype(F32) + qb[...].astype(F32)).astype(BF)
    q_out[...] = total
    values = total.astype(F32)
    m = mask[...]
    sums_out[...] = sums_of(values * m, values * values * m)


def head_kernel(d, w, denominator, classes, *refs):
    ids, *refs = refs
    w_refs, refs = refs[: len(w.arrays)], refs[len(w.arrays) :]
    terms, refs = refs[: d.nz], refs[d.nz :]
    q, count, gains, mask, x, bias, clip_info, labels, *refs = refs
    coef_out, grad_out, sums_out, head, sems = refs
    copies = w.start(d, ids, w_refs, head, sems)
    m = mask[...]
    coef = coefs_of(total_of(d, ids, terms), count[4:5, 0:1], gains[...])
    coef_out[...] = coef
    normed = normed_of(q[...].astype(F32), coef)
    pre = coef[2:3] * normed + coef[3:4] + x[...].astype(F32)
    sigma = jax.nn.sigmoid(pre)
    y = pre * sigma * m
    folded = jnp.sum(y.reshape(d.cells // 8, 8, d.channels), axis=0)
    step = d.clips
    total = folded
    for k in range(1, 8 // step):
        total = total + pltpu.roll(folded, k * step, 0)
    inverse = 1.0 / clip_info[:, 0:1]
    pooled = total * inverse
    pooled_bf = pooled.astype(BF)
    for copy in copies:
        copy.wait()
    weight = head[0, :, : d.channels]
    logits = dot(pooled_bf, weight) + bias[...]
    largest = jnp.max(logits, axis=1, keepdims=True)
    shifted = jnp.exp(logits - largest)
    log_total = largest + jnp.log(jnp.sum(shifted, axis=1, keepdims=True))
    lane = lax.broadcasted_iota(jnp.int32, logits.shape, 1)
    onehot = jnp.where(lane == labels[:, 0:1], 1.0, 0.0)
    inside = lane < classes
    kept = jnp.where(inside, logits, 0.0)
    loss = log_total - jnp.sum(kept * onehot, axis=1, keepdims=True)
    grad_logits = jnp.where(inside, (jnp.exp(logits - log_total) - onehot) / denominator, 0.0)
    grad_pooled = dot_nt(grad_logits.astype(BF), weight) * inverse
    grad_y = jnp.broadcast_to(grad_pooled[None], (d.cells // 8, 8, d.channels)).reshape(
        d.cells, d.channels
    )
    grad_pre = grad_y * m * (sigma * (1.0 + pre * (1.0 - sigma)))
    grad_out[...] = grad_pre
    sums_out[0:8, :] = sums_of(grad_pre, grad_pre * normed)
    carried = jnp.where(lane == classes, loss, grad_logits)
    sums_out[8:16, :] = jnp.concatenate(
        [
            pooled_bf.astype(F32)[0 : d.clips],
            carried[0 : d.clips],
            jnp.zeros((8 - 2 * d.clips, d.channels), F32),
        ],
        axis=0,
    )


def time_back_kernel(d, w, *refs):
    ids, *refs = refs
    w_refs, refs = refs[: len(w.arrays)], refs[len(w.arrays) :]
    terms, refs = refs[: d.nz], refs[d.nz :]
    grad_two, q, coef_two, count, mask, s, coef_one, *refs = refs
    gq_out, grad_out, sums_out, tot_out, weight, sems, pad = refs
    copies = w.start(d, ids, w_refs, weight, sems)
    m = mask[...]
    total = total_of(d, ids, terms)
    tot_out[...] = total
    coef = coef_two[...]
    normed = normed_of(q[...].astype(F32), coef)
    grad_q = norm_back(grad_two[...], normed, coef, total, count[4:5, 0:1], m).astype(BF)
    gq_out[...] = grad_q
    fill_time(d, pad, grad_q)
    for copy in copies:
        copy.wait()
    grad = dot(time_window(d, pad, TIME - 1), weight[0])
    for k in range(1, TIME):
        grad = grad + dot(time_window(d, pad, TIME - 1 - k), weight[k])
    grad = grad.astype(BF).astype(F32)
    coef = coef_one[...]
    normed = normed_of(s[...], coef)
    pre = coef[2:3] * normed + coef[3:4]
    grad_pre = grad * m * act_slope(pre)
    grad_out[...] = grad_pre
    sums_out[...] = sums_of(grad_pre, grad_pre * normed)


def space_back_kernel(d, w, *refs):
    ids, *refs = refs
    w_refs, refs = refs[: len(w.arrays)], refs[len(w.arrays) :]
    terms, refs = refs[: d.nz], refs[d.nz :]
    grad_pre, s, coef_one, count, mask, *refs = refs
    gs_out, ga_out, tot_out, weight, sems, pad, acc = refs
    copies = w.start(d, ids, w_refs, weight, sems)
    total = total_of(d, ids, terms)
    tot_out[...] = total
    coef = coef_one[...]
    normed = normed_of(s[...], coef)
    grad_s = norm_back(grad_pre[...], normed, coef, total, count[4:5, 0:1], mask[...])
    gs_out[...] = grad_s.astype(BF)
    fill_space(d, pad, grad_s)
    for copy in copies:
        copy.wait()
    for i in range(3):
        part = sum(dot_nt(space_window(d, pad, 2 - i, 2 - j), weight[3 * i + j]) for j in range(3))
        acc[...] = part if i == 0 else acc[...] + part
    ga_out[...] = acc[...].astype(BF)


def join_back_kernel(ga, gb, q, coef_two, mask, grad_out, sums_out):
    coef = coef_two[...]
    normed = normed_of(q[...].astype(F32), coef)
    pre = coef[2:3] * normed + coef[3:4]
    grad = ga[...].astype(F32) + gb[...].astype(F32)
    grad_pre = grad * mask[...] * act_slope(pre)
    grad_out[...] = grad_pre
    sums_out[...] = sums_of(grad_pre, grad_pre * normed)


def write_grad(d, w, ids, value, outs, held):
    if w.kind == "natural":
        outs[0][0] = value.astype(BF)
        return
    held[...] = value.astype(BF)
    for operand, index, row in w.places(d, ids):
        block = held[pl.ds(pl.multiple_of(row, 16), d.rows), :]
        outs[operand][(*index, 0)] = block


def time_grad_kernel(d, w, *refs):
    ids, grad_q, act, *refs = refs
    outs, (pad, turned, held) = refs[:-3], refs[-3:]
    k = pl.program_id(0)

    @pl.when(k == 0)
    def _():
        fill_time(d, pad, act[...])
        turned[...] = jnp.transpose(grad_q[...].astype(F32)).astype(BF)

    write_grad(d, w, ids, dot(turned[...], time_window(d, pad, k)), outs, held)


def unit_grad_kernel(d, w, *refs):
    ids, a, grad_s, grad_q, act, *refs = refs
    outs, (pad, time_pad, time_turned, turned, held) = refs[:-5], refs[-5:]
    k = pl.program_id(0)

    @pl.when(k == 0)
    def _():
        fill_space(d, pad, grad_s[...].astype(F32))
        turned[...] = jnp.transpose(a[...].astype(F32)).astype(BF)
        fill_time(d, time_pad, act[...])
        time_turned[...] = jnp.transpose(grad_q[...].astype(F32)).astype(BF)

    @pl.when(k < SPACE)
    def _():
        window = space_window(d, pad, 2 - lax.div(k, 3), 2 - lax.rem(k, 3))
        write_grad(d, w, ids, dot(turned[...], window), outs, held)

    @pl.when(k >= SPACE)
    def _():
        window = time_window(d, time_pad, k - SPACE)
        write_grad(d, w, ids, dot(time_turned[...], window), outs, held)


def last_space_grad_kernel(d, w, *refs):
    ids, *refs = refs
    terms, refs = refs[: d.nz], refs[d.nz :]
    a, grad_pre, s, coef_one, count, mask, tot_out, *refs = refs
    outs, (pad, turned, held) = refs[:-3], refs[-3:]
    k = pl.program_id(0)

    @pl.when(k == 0)
    def _():
        total = total_of(d, ids, terms)
        tot_out[...] = total
        coef = coef_one[...]
        normed = normed_of(s[...], coef)
        grad_s = norm_back(grad_pre[...], normed, coef, total, count[4:5, 0:1], mask[...])
        fill_space(d, pad, grad_s)
        turned[...] = jnp.transpose(a[...].astype(F32)).astype(BF)

    window = space_window(d, pad, 2 - lax.div(k, 3), 2 - lax.rem(k, 3))
    write_grad(d, w, ids, dot(turned[...], window), outs, held)


def squares_kernel(*refs):
    *values, out = refs
    row = lax.broadcasted_iota(jnp.int32, (8, LANES), 0)
    lane = lax.broadcasted_iota(jnp.int32, (8, LANES), 1)
    total = jnp.zeros((8, LANES), F32)
    for i, value in enumerate(values):
        here = (row == i // 5) & (lane == i % 5)
        lanes = jnp.sum(value[...], axis=0, keepdims=True)
        total = jnp.where(here, jnp.sum(lanes, axis=1, keepdims=True), total)
    out[...] = total


def sds(shape, dtype=F32):
    return jax.ShapeDtypeStruct(shape, dtype)


def call(body, name, ins, outs, scratch, flops, megabytes=40):
    return pl.pallas_call(
        body,
        name=name,
        out_shape=outs,
        in_specs=[spec for spec, _ in ins],
        out_specs=[whole()] * len(outs),
        scratch_shapes=scratch,
        compiler_params=pltpu.CompilerParams(vmem_limit_bytes=megabytes * MB),
        cost_estimate=pl.CostEstimate(flops=flops, bytes_accessed=8 * MB, transcendentals=0),
    )(*[value for _, value in ins])


def w_ins(weight):
    return [
        (in_hbm(), pltpu.with_memory_space_constraint(piece, pltpu.HBM))
        for piece in weight.arrays
    ]


def v_ins(*values):
    return [(whole(), value) for value in values]


def grad_call(d, body, name, kind, taps, ids, values, first_outs, scratch):
    if kind == "ring":
        shape, count = (d.nz, 2, taps, d.rows, d.half), 4
        spec = pl.BlockSpec((d.nz, 2, 1, d.rows, d.half), lambda k: (0, 0, k, 0, 0))
    elif kind == "parts":
        shape, count = (2, 2, taps, d.rows, d.half), d.groups // 2
        spec = pl.BlockSpec((2, 2, 1, d.rows, d.half), lambda k: (0, 0, k, 0, 0))
        first_outs = [*first_outs, sds((d.groups, *shape[1:]), BF)]
    else:
        shape, count = (taps, d.channels, d.half), 1
        spec = pl.BlockSpec((1, d.channels, d.half), lambda k: (k, 0, 0))
    fixed = [pl.BlockSpec(out.shape, lambda k: (0, 0)) for out in first_outs]
    if kind == "parts":
        fixed[-1] = pl.BlockSpec((d.groups, 2, 1, d.rows, d.half), lambda k: (0, 0, k, 0, 0))
    outs = pl.pallas_call(
        functools.partial(body, d, Weight(kind, (), 0, 1)),
        name=name,
        grid=(taps,),
        out_shape=list(first_outs) + [sds(shape, BF)] * count,
        in_specs=[smem()] + [whole()] * len(values),
        out_specs=fixed + [spec] * count,
        scratch_shapes=scratch
        + [pltpu.VMEM((d.channels, d.cells), BF), pltpu.VMEM((d.channels, d.half), BF)],
        compiler_params=pltpu.CompilerParams(vmem_limit_bytes=40 * MB),
        cost_estimate=pl.CostEstimate(flops=1, bytes_accessed=1, transcendentals=0),
    )(ids, *values)
    return outs[: len(first_outs)], outs[len(first_outs) :]


def swap(value, axis, distance=1):
    size = lax.axis_size(axis)
    return lax.ppermute(value, axis, [(i, i ^ distance) for i in range(size)])


def across_yy(values, *besides):
    size = lax.axis_size("yy")
    distance = 1
    while distance < size:
        other = swap(values, "yy", distance)
        distance *= 2
        values = values + (after(other, *besides) if distance >= size else other)
    return values


def around_tm(values):
    size = lax.axis_size("tm")
    return [values] + [
        lax.ppermute(values, "tm", [(i, (i + k) % size) for i in range(size)])
        for k in range(1, size)
    ]


def data_sums(values, last=(), first=()):
    terms = around_tm(across_yy(values, *first))
    return [after(term, *last) if k == len(terms) - 1 else term for k, term in enumerate(terms)]


def data_sums_gather(values):
    distance = 1
    while distance < lax.axis_size("yy"):
        other = swap(values, "yy", distance)
        values = jnp.concatenate([values[:8] + other[:8], values[8:], other[8:]], axis=0)
        distance *= 2
    terms = around_tm(values)
    return [term[:8] for term in terms], jnp.concatenate([term[8:] for term in terms], axis=0)


def pick(index, first, second):
    return jnp.where(index == 0, first, second)


def after(value, *earlier):
    if not earlier:
        return value
    return lax.optimization_barrier((value, *earlier))[0]


def turn(value):
    size = lax.axis_size("tm")
    return lax.ppermute(value, "tm", [(i, (i + 1) % size) for i in range(size)])


def together(*values):
    return lax.optimization_barrier(values)


def gather_ring(both, besides):
    held, across, made = [both], [], []
    for beside in besides:
        moves = [swap(held[-1], "yy")]
        if len(held) < lax.axis_size("tm"):
            moves.append(turn(held[-1]))
        extra = beside(held[-1], made[-1] if made else None)
        results = together(*moves, *extra)
        across.append(results[0])
        held += results[1 : len(moves)]
        made.append(results[len(moves) :])
    own = held + across
    return Weight("blocks", own + [swap(block, "u") for block in own], 0, both.shape[1]), made


def gather_all(d, s, u, both, *earlier):
    own = after(lax.all_gather(both, DATA, axis=0, tiled=False), *earlier)
    sibling = swap(own, "u")
    taps = both.shape[1]
    if d.pieces:
        return Weight("all", (own, sibling), 0, taps)
    parts = jnp.stack([own, sibling]).reshape(2, d.ny, d.nz, 2, taps, d.rows, d.half)
    parts = jnp.where(u == 0, parts, parts[::-1])
    parts = jnp.where(s == 0, parts, parts[:, :, :, ::-1])
    natural = parts.transpose(4, 1, 3, 0, 2, 5, 6).reshape(taps, d.channels, d.half)
    return Weight("natural", (natural,), 0, taps)


def added(*values):
    total = values[0].astype(F32)
    for value in values[1:]:
        total = total + value.astype(F32)
    return total.astype(BF)


def reduce_ring(d, gradients):
    def joined(yrel, k, *others):
        parts = [outs[yrel][k].astype(F32) + outs[2 + yrel][k].astype(F32) for outs in gradients]
        total = jnp.concatenate(parts, axis=1)
        for other in others:
            total = total + other.astype(F32)
        return total.astype(BF)

    moving = None
    for k in list(range(1, d.nz)) + [0]:
        terms = [swap(joined(1, k), "yy")]
        if moving is not None:
            terms.append(turn(moving))
        moving = joined(0, k, *terms)
    return moving


def reduce_all(d, s, u, kind, outs, *earlier):
    if kind == "parts":
        keep, *sends = outs
        theirs = [swap(send, "u") for send in sends]
    else:
        (natural,) = outs
        taps = natural.shape[0]
        parts = natural.reshape(taps, d.ny, 2, 2, d.nz, d.rows, d.half)
        parts = parts.transpose(3, 1, 4, 2, 0, 5, 6)
        parts = jnp.where(u == 0, parts, parts[::-1])
        parts = jnp.where(s == 0, parts, parts[:, :, :, ::-1])
        keep, send = parts.reshape(2, d.groups, 2, taps, d.rows, d.half)
        theirs = [swap(send, "u")]
    keep, theirs = after((keep, theirs), *earlier)
    both = added(keep, jnp.concatenate(theirs, axis=0))
    return both, lax.psum_scatter(both, DATA, scatter_dimension=0, tiled=False)


def own_rows(d, s, mine):
    other = swap(mine[1], "s")
    first = pick(s, mine[0], other)
    second = pick(s, other, mine[0])
    return jnp.concatenate([first, second[..., : d.mid - d.half]], axis=-1).astype(F32)


def halves(d, values):
    fill = [(0, 0)] * (values.ndim - 1) + [(0, 2 * d.half - d.mid)]
    return values[..., : d.half], jnp.pad(values[..., d.half :], fill)


def rows_of(gain, shift):
    return jnp.concatenate(
        [gain[None], shift[None], jnp.zeros((6, gain.shape[0]), F32)], axis=0
    )


def square_rows(values):
    return jnp.sum(values * values, axis=tuple(range(1, values.ndim - 1)))


def adam_part(weight, gradient, moment_one, moment_two, decay):
    new_one = BETA_ONE * moment_one + (1.0 - BETA_ONE) * gradient
    new_two = BETA_TWO * moment_two + (1.0 - BETA_TWO) * gradient * gradient
    direction = (
        new_one / (1.0 - BETA_ONE**STEP) / (jnp.sqrt(new_two / (1.0 - BETA_TWO**STEP)) + EPS_ADAM)
        + decay * weight
    )
    return (new_one, new_two, direction)


def on_device(
    clips_x,
    frames,
    labels,
    spatial_weight,
    temporal_weight,
    head_weight,
    affine,
    head_bias,
    spatial_first,
    spatial_second,
    temporal_first,
    temporal_second,
    head_first,
    head_second,
    affine_first,
    affine_second,
    bias_first,
    bias_second,
):
    s, u, z, yy = (lax.axis_index(axis) for axis in ("s", "u", "tm", "yy"))
    ny, nz = lax.axis_size("yy"), lax.axis_size("tm")
    micro, clips, _, height, width, channels = clips_x.shape
    mid = spatial_weight.shape[3]
    rows = spatial_weight.shape[0]
    classes = head_weight.shape[1]
    d = Dims(clips, nz, height, width, channels, mid, rows, ny, nz)
    assert nz == 4 and micro == 2
    ids = jnp.stack([s, u, yy, z]).astype(jnp.int32)
    denominator = micro * clips * 4 * ny

    def prepared(weight, l):
        return halves(d, weight[:, l].astype(BF).transpose(1, 0, 2))

    def paired(parts):
        first = jnp.concatenate([part[0] for part in parts], axis=0)
        second = jnp.concatenate([part[1] for part in parts], axis=0)
        return jnp.stack([pick(s, first, second), swap(pick(s, second, first), "s")])

    def by_index(index, mine, other):
        return jnp.stack([pick(index, mine, other), pick(index, other, mine)])

    def beside_first(block, _):
        moved = []
        for value in (clips_x, jnp.stack([frames, labels]).transpose(1, 0, 2)):
            kept = pick(u, value[0], value[1])
            pair = by_index(u, kept, swap(pick(u, value[1], value[0]), "u"))
            moved.append(by_index(s, pair, swap(pair, "s")))
        return moved

    def clips_home(four):
        return lax.all_to_all(four, "tm", split_axis=0, concat_axis=0, tiled=True)

    def beside_second(block, first):
        weights = after((spatial_weight, temporal_weight, head_weight), block)
        late = paired([prepared(weights[0], 1)])
        slot = jnp.pad(weights[2].astype(BF), ((0, 0), (0, d.half - classes)))[None]
        four = first[0].reshape(nz, clips, height * width, channels)
        return late, paired([prepared(weights[1], 1), (slot, slot)]), clips_home(four)

    def beside_third(block, _):
        weights = after((spatial_weight, temporal_weight, head_weight), block)
        gains, bias = after((affine, head_bias), block)
        bias_row = jnp.full((1, channels), -1e30, F32).at[0, :classes].set(bias)
        rows_one, rows_two = [], []
        for l in range(2):
            low, high = halves(d, gains[l, :, :mid])
            mine = pick(s, low, high)
            rows_one.append(rows_of(mine[0], mine[1]))
            rows_two.append(rows_of(gains[l, 0, mid:], gains[l, 1, mid:]))
        squares = [square_rows(weight[:, l]) for weight in weights[:2] for l in range(2)]
        return [bias_row, *rows_one, *rows_two, *squares, square_rows(weights[2])]

    early = paired([prepared(spatial_weight, 0), prepared(temporal_weight, 0)])
    if d.pieces:
        early_w, made = gather_ring(
            early, [beside_first, beside_second, beside_third, lambda *_: []]
        )
        first, second, small, _ = made
    else:
        early_w = gather_all(d, s, u, early)
        first = beside_first(early, None)
        second, small = beside_second(early, first), beside_third(early, None)
    info_four = first[1]
    late, last, clip_all = second
    bias_row, *small = small
    gains_one, gains_two, weight_squares = small[:2], small[2:4], small[4:]

    x = clip_all.reshape(nz, clips, height * width, channels)
    x = x.transpose(0, 2, 1, 3).reshape(d.cells, channels)

    mine_info = lax.dynamic_index_in_dim(
        info_four.reshape(nz, 2, clips), z, 0, keepdims=False
    )
    my_frames, my_labels = mine_info[0], mine_info[1]
    valid = (jnp.arange(nz, dtype=jnp.int32)[:, None] * 8 < my_frames[None, :]).astype(F32)
    mask = jnp.broadcast_to(valid[:, None, :], (nz, height * width, clips)).reshape(d.cells, 1)
    divisor = (my_frames // 8).astype(F32) * (height * width)
    clip_info = jnp.broadcast_to(jnp.tile(divisor, 8 // clips)[:, None], (8, LANES))
    label_rows = jnp.broadcast_to(jnp.tile(my_labels, 8 // clips)[:, None], (8, LANES))
    x, mask, clip_info, label_rows = together(x, mask, clip_info, label_rows)

    wide, narrow = (d.cells, d.half), (d.cells, channels)
    space_flops = 2 * d.cells * SPACE * channels * d.half
    time_flops = 2 * d.cells * TIME * channels * d.half

    space_w = [early_w.part(0, SPACE), None]
    time_w = [early_w.part(SPACE, TIME), None]

    def space_first(x_bf):
        return call(
            functools.partial(first_space_kernel, d, space_w[0]),
            "space0",
            [(smem(), ids)] + w_ins(space_w[0]) + v_ins(x_bf, mask),
            [sds(wide), sds((8, d.half))],
            space_w[0].scratch(d) + [space_scratch(d, channels)],
            space_flops,
        )

    def space_next(q, terms, count):
        return call(
            functools.partial(second_space_kernel, d, space_w[1]),
            "space1",
            [(smem(), ids)] + w_ins(space_w[1]) + v_ins(*terms, q, count, gains_two[0], mask),
            [sds(narrow, BF), sds((8, channels)), sds(wide), sds((8, d.half))],
            space_w[1].scratch(d) + [space_scratch(d, channels)],
            space_flops,
        )

    def time_next(l, s_value, terms, *count):
        return call(
            functools.partial(time_kernel, d, time_w[l]),
            f"time{l}",
            [(smem(), ids)] + w_ins(time_w[l]) + v_ins(*terms, s_value, *count, gains_one[l], mask),
            [sds(wide, BF), sds(narrow, BF), sds((8, d.half))],
            time_w[l].scratch(d) + [time_scratch(d, d.half)],
            time_flops,
        )

    def joined(q_part):
        return call(
            join_kernel,
            "join",
            v_ins(q_part, swap(q_part, "s"), mask),
            [sds(narrow, BF), sds((8, channels))],
            [],
            d.cells * channels,
        )

    s0, sums = space_first(x)
    terms = data_sums(sums)
    act0, q_part, coef_one0 = time_next(0, s0, terms)
    count = coef_one0
    space_w[1] = gather_all(d, s, u, late, q_part)
    q0, sums = joined(q_part)
    terms = data_sums(sums)
    a_mid, coef_two0, s1, sums = space_next(q0, terms, count)
    late_w = gather_all(d, s, u, last, s1)
    time_w[1] = late_w.part(0, TIME)
    head_w = late_w.part(TIME, 1)
    terms = data_sums(sums)
    act1, q_part, coef_one1 = time_next(1, s1, terms, count)
    q1, sums = joined(q_part)
    terms = data_sums(sums)
    coef_two1, grad_two, sums = call(
        functools.partial(head_kernel, d, head_w, float(denominator), classes),
        "head",
        [(smem(), ids)]
        + w_ins(head_w)
        + v_ins(*terms, q1, count, gains_two[1], mask, x, bias_row, clip_info, label_rows),
        [sds((8, channels)), sds(narrow), sds((16, channels))],
        head_w.scratch(d),
        4 * d.cells * channels,
    )
    terms, carried = data_sums_gather(sums)

    def time_back(l, grad, q, coef_two, terms, s_value, coef_one):
        return call(
            functools.partial(time_back_kernel, d, time_w[l]),
            f"time_back{l}",
            [(smem(), ids)]
            + w_ins(time_w[l])
            + v_ins(*terms, grad, q, coef_two, count, mask, s_value, coef_one),
            [sds(narrow, BF), sds(wide), sds((8, d.half)), sds((8, channels))],
            time_w[l].scratch(d) + [time_scratch(d, channels)],
            time_flops,
        )

    late_kind = "parts" if d.pieces else "natural"
    early_kind = "ring" if d.pieces else "natural"

    grad_q1, grad_one, sums, tot_two1 = time_back(
        1, grad_two, q1, coef_two1, terms, s1, coef_one1
    )
    terms = data_sums(sums)
    grad_s1, ga_part, tot_one1 = call(
        functools.partial(space_back_kernel, d, space_w[1]),
        "space_back",
        [(smem(), ids)] + w_ins(space_w[1]) + v_ins(*terms, grad_one, s1, coef_one1, count, mask),
        [sds(wide, BF), sds(narrow, BF), sds((8, d.half))],
        space_w[1].scratch(d)
        + [space_scratch(d, d.half), pltpu.VMEM((d.cells, channels), F32)],
        space_flops,
    )
    ga_other = swap(ga_part, "s")
    late_first, late_outs = grad_call(
        d,
        unit_grad_kernel,
        "unit_grad1",
        late_kind,
        SPACE + TIME,
        ids,
        (a_mid, grad_s1, grad_q1, act1),
        [],
        [
            space_scratch(d, d.half),
            time_scratch(d, d.half),
            pltpu.VMEM((d.channels, d.cells), BF),
        ],
    )
    late_outs = [*late_first, *late_outs]
    grad_two, sums = call(
        join_back_kernel,
        "join_back",
        v_ins(ga_part, after(ga_other, *late_outs), q0, coef_two0, mask),
        [sds(narrow), sds((8, channels))],
        [],
        20 * 10**9,
    )
    late_both, late_sum = reduce_all(d, s, u, late_kind, late_outs, sums)

    carried = jnp.concatenate([carried, swap(carried, "u")], axis=0).reshape(-1, 8, channels)
    pooled_all = carried[:, :clips].reshape(-1, channels)
    logit_all = carried[:, clips : 2 * clips].reshape(-1, channels)
    loss_sum = jnp.sum(logit_all[:, classes])
    logit_all = logit_all[:, :classes]
    bias_grad = jnp.sum(logit_all, axis=0)
    base = d.row_base(yy, s, u, z)
    pooled_mine = lax.dynamic_slice_in_dim(pooled_all, base, rows, 1)
    head_grad = lax.dot_general(
        pooled_mine.astype(BF),
        logit_all.astype(BF),
        (((0,), (0,)), ((), ())),
        preferred_element_type=F32,
    )
    head_one, head_two, head_dir = adam_part(head_weight, head_grad, head_first, head_second, DECAY)
    bias_one, bias_two, bias_dir = adam_part(head_bias, bias_grad, bias_first, bias_second, 0.0)
    head_squares = square_rows(head_dir)

    terms = data_sums(
        sums,
        (late_both, head_one, head_two, head_dir, head_squares),
        (loss_sum, bias_one, bias_two),
    )
    grad_q0, grad_one, sums, tot_two0 = time_back(
        0, grad_two, q0, coef_two0, terms, s0, coef_one0
    )
    _, time_outs0 = grad_call(
        d,
        time_grad_kernel,
        "time_grad0",
        early_kind,
        TIME,
        ids,
        (grad_q0, act0),
        [],
        [time_scratch(d, d.half)],
    )
    if d.pieces:
        time_outs0 = [*time_outs0[:2], *(swap(send, "u") for send in time_outs0[2:])]
    terms = data_sums(sums, time_outs0[2:], time_outs0[:2])
    (tot_one0,), space_outs0 = grad_call(
        d,
        last_space_grad_kernel,
        "space_grad0",
        early_kind,
        SPACE,
        ids,
        (*terms, x, grad_one, s0, coef_one0, count, mask),
        [sds((8, d.half))],
        [space_scratch(d, d.half)],
    )

    late_sum = own_rows(d, s, after(late_sum, *space_outs0))
    if d.pieces:
        early_sum = reduce_ring(
            d,
            [[*space_outs0[:2], *(swap(send, "u") for send in space_outs0[2:])], time_outs0],
        )
    else:
        early_outs = [jnp.concatenate([space_outs0[0], time_outs0[0]], axis=0)]
        _, early_sum = reduce_all(d, s, u, early_kind, early_outs)
    early_sum, late_sum = together(early_sum, late_sum)
    early_sum = own_rows(d, s, early_sum)

    ones = jnp.stack([tot_one0[:2], tot_one1[:2]])
    twos = jnp.stack([tot_two0[:2], tot_two1[:2]])
    small = jnp.concatenate([ones, twos], axis=-1)
    small = small + swap(small, "u")
    ones, twos = small[..., : d.half], small[..., d.half :]
    ones_other = swap(ones, "s")
    low, high = pick(s, ones, ones_other), pick(s, ones_other, ones)
    both = jnp.concatenate([low, high[..., : mid - d.half], twos], axis=-1)
    affine_grad = jnp.stack([both[:, 1], both[:, 0]], axis=1)

    def units(first, second):
        return jnp.stack([first, second]).transpose(2, 0, 1, 3)

    spatial_grad = units(early_sum[:SPACE], late_sum[:SPACE])
    temporal_grad = units(early_sum[SPACE:], late_sum[SPACE:])
    space_one, space_two, space_dir = adam_part(
        spatial_weight, spatial_grad, spatial_first, spatial_second, DECAY
    )
    time_one, time_two, time_dir = adam_part(
        temporal_weight, temporal_grad, temporal_first, temporal_second, DECAY
    )
    affine_one, affine_two, affine_dir = adam_part(
        affine, affine_grad, affine_first, affine_second, 0.0
    )
    dir_squares = [square_rows(v[:, l]) for v in (space_dir, time_dir) for l in range(2)]
    dir_squares.append(head_squares)
    padded = pl.pallas_call(
        squares_kernel,
        name="squares",
        out_shape=sds((8, LANES)),
        in_specs=[whole()] * 10,
        out_specs=whole(),
    )(*weight_squares, *dir_squares)
    native = Layout(major_to_minor=(0, 2, 1, 3))
    moments = [
        with_layout_constraint(value, native)
        for value in together(space_one, space_two, time_one, time_two)
    ]
    space_one, space_two, time_one, time_two = moments
    padded = padded + swap(padded, "u")
    padded = padded + after(swap(padded, "s"), affine_one, affine_two, affine_dir)
    terms = data_sums(padded, moments[1:3], (moments[0], moments[3]))
    terms = jnp.stack(terms)
    padded = sum(terms[lax.rem(z + (nz - place), nz)] for place in range(nz))
    norms = jnp.sqrt(padded[:2, :5])
    trust = norms[0] / norms[1]
    new_space = spatial_weight - RATE * trust[0:2][None, :, None, None] * space_dir
    new_time = temporal_weight - RATE * trust[2:4][None, :, None, None] * time_dir
    new_head = head_weight - RATE * trust[4] * head_dir
    new_affine = affine - RATE_SMALL * affine_dir
    new_bias = head_bias - RATE_SMALL * bias_dir
    return (
        loss_sum,
        space_one,
        space_two,
        new_space,
        time_one,
        time_two,
        new_time,
        head_one,
        head_two,
        new_head,
        affine_one,
        affine_two,
        new_affine,
        bias_one,
        bias_two,
        new_bias,
        norms,
    )


def solution(mesh):
    dp, tm = mesh.shape["dp"], mesh.shape["tm"]
    fine = Mesh(mesh.devices.reshape(dp // 4, 2, 2, tm), ALL)
    dp_axes = ("yy", "s", "u")
    owner = P(ALL)
    return jax.shard_map(
        on_device,
        mesh=fine,
        in_specs=(
            P(None, dp_axes, "tm"),
            P(None, dp_axes),
            P(None, dp_axes),
            owner,
            owner,
            owner,
            P(),
            P(),
            owner,
            owner,
            owner,
            owner,
            owner,
            owner,
            P(),
            P(),
            P(),
            P(),
        ),
        out_specs=(P(),) + (owner,) * 9 + (P(),) * 7,
        check_vma=False,
    )
```

```python
import functools

import jax
import jax.numpy as jnp
from jax import lax
from jax.experimental import pallas as pl
from jax.experimental.layout import Layout, with_layout_constraint
from jax.experimental.pallas import tpu as pltpu
from jax.sharding import Mesh
from jax.sharding import PartitionSpec as P

STEP = 5
EPS_NORM = 1e-05
EPS_ADAM = 1e-06
BETA_ONE = 0.5
BETA_TWO = 0.5
DECAY = 0.01
RATE = 0.3
RATE_SMALL = 0.1

F32 = jnp.float32
BF = jnp.bfloat16
LANES = 128
SPACE, TIME = 9, 3
ALL = ("yy", "s", "u", "tm")
DATA = ("yy", "tm")
MB = 1 << 20


def whole():
    return pl.BlockSpec(memory_space=pltpu.VMEM)


def in_hbm():
    return pl.BlockSpec(memory_space=pltpu.HBM)


def smem():
    return pl.BlockSpec(memory_space=pltpu.SMEM)


def dot(a, b):
    return jnp.dot(a, b, preferred_element_type=F32)


def dot_nt(a, b):
    return lax.dot_general(a, b, (((1,), (1,)), ((), ())), preferred_element_type=F32)


class Dims:
    def __init__(self, clips, frames, height, width, channels, mid, rows, ny, nz):
        self.clips, self.frames, self.height, self.width = clips, frames, height, width
        self.channels, self.mid, self.rows, self.ny, self.nz = channels, mid, rows, ny, nz
        self.line = width * clips
        self.plane = height * self.line
        self.cells = frames * self.plane
        tiles = mid // LANES
        self.half = (tiles + 1) // 2 * LANES
        self.groups = ny * nz
        self.pieces = rows % 16 == 0 and ny == 2

    def row_base(self, yy, s, u, z):
        return (((yy * 2 + s) * 2 + u) * self.nz + z) * self.rows


class Weight:
    def __init__(self, kind, arrays, first, taps):
        self.kind, self.arrays, self.first, self.taps = kind, arrays, first, taps

    def part(self, first, taps):
        return Weight(self.kind, self.arrays, self.first + first, taps)

    def copies_needed(self, d):
        return 1 if self.kind == "natural" else 4 * d.groups

    def scratch(self, d):
        return [
            pltpu.VMEM((self.taps, d.channels, d.half), BF),
            pltpu.SemaphoreType.DMA((self.copies_needed(d),)),
        ]

    def places(self, d, ids):
        s, u, yy, z = (ids[i] for i in range(4))
        for urel in range(2):
            for i in range(d.groups):
                for srel in range(2):
                    if self.kind in ("blocks", "ring"):
                        yrel, k = i // d.nz, i % d.nz
                        row = d.row_base(
                            yrel ^ yy, srel ^ s, urel ^ u, lax.rem(z + (d.nz - k), d.nz)
                        )
                        if self.kind == "blocks":
                            yield urel * d.groups + i, (srel,), row
                        else:
                            yield urel * 2 + yrel, (k, srel), row
                    else:
                        row = d.row_base(i // d.nz, srel ^ s, urel ^ u, i % d.nz)
                        if self.kind == "all" or urel == 0:
                            yield urel, (i, srel), row
                        else:
                            yield 1 + i // 2, (i % 2, srel), row

    def start(self, d, ids, refs, scratch, sems):
        taps = pl.ds(self.first, self.taps)
        copies = []
        if self.kind == "natural":
            copies.append(pltpu.make_async_copy(refs[0].at[taps], scratch, sems.at[0]))
        else:
            for operand, index, row in self.places(d, ids):
                copies.append(
                    pltpu.make_async_copy(
                        refs[operand].at[(*index, taps)],
                        scratch.at[:, pl.ds(pl.multiple_of(row, 16), d.rows), :],
                        sems.at[len(copies)],
                    )
                )
        for copy in copies:
            copy.start()
        return copies


def space_scratch(d, width):
    return pltpu.VMEM((d.frames, (d.height + 2) * d.line, 3 * width), BF)


def time_scratch(d, width):
    return pltpu.VMEM(((d.frames + 2) * d.plane, width), BF)


def fill_space(d, pad, values):
    cells, width = values.shape
    place = lax.broadcasted_iota(jnp.int32, (cells, width), 0)
    column = lax.rem(lax.div(place, d.clips), d.width)
    edge = jnp.zeros((d.frames, d.line, 3 * width), BF)
    pad[:, 0 : d.line, :] = edge
    pad[:, d.line + d.plane :, :] = edge
    left = jnp.where(column > 0, pltpu.roll(values, d.clips, 0), 0.0)
    right = jnp.where(column < d.width - 1, pltpu.roll(values, cells - d.clips, 0), 0.0)
    for j, moved in enumerate((left, values, right)):
        block = moved.astype(BF).reshape(d.frames, d.plane, width)
        pad[:, d.line : d.line + d.plane, j * width : (j + 1) * width] = block


def space_window(d, pad, i, j=None):
    rows = pl.ds(pl.multiple_of(i * d.line, d.line), d.plane)
    if j is None:
        block = pad[:, rows, :]
    else:
        width = pad.shape[-1] // 3
        block = pad[:, rows, pl.ds(pl.multiple_of(j * width, LANES), width)]
    return block.reshape(d.cells, block.shape[-1])


def fill_time(d, pad, values):
    width = values.shape[1]
    edge = jnp.zeros((d.plane, width), BF)
    pad[0 : d.plane, :] = edge
    pad[d.plane + d.cells :, :] = edge
    pad[d.plane : d.plane + d.cells, :] = values


def time_window(d, pad, k):
    return pad[pl.ds(pl.multiple_of(k * d.plane, d.plane), d.cells), :]


def sums_of(first, second, extra=None):
    width = first.shape[1]
    rows = [jnp.sum(first, axis=0, keepdims=True), jnp.sum(second, axis=0, keepdims=True)]
    if extra is not None:
        rows.append(extra)
    rows.append(jnp.zeros((8 - len(rows), width), F32))
    return jnp.concatenate(rows, axis=0)


def total_of(d, ids, terms):
    z = ids[3]
    values = [term[...] for term in terms]
    total = None
    for place in range(d.nz):
        here = values[0]
        for k in range(1, d.nz):
            here = jnp.where(lax.rem(z + (d.nz - k), d.nz) == place, values[k], here)
        total = here if total is None else total + here
    return total


def coefs_of(total, count, gains):
    average = total[0:1] / count
    scale = lax.rsqrt(total[1:2] / count - average * average + EPS_NORM)
    return jnp.concatenate(
        [
            average,
            scale,
            gains[0:2],
            jnp.broadcast_to(count, average.shape),
            jnp.zeros((3, total.shape[1]), F32),
        ],
        axis=0,
    )


def normed_of(values, coef):
    return (values - coef[0:1]) * coef[1:2]


def act_slope(pre):
    sigma = jax.nn.sigmoid(pre)
    return sigma * (1.0 + pre * (1.0 - sigma))


def norm_back(grad_pre, normed, coef, total, count, mask):
    scale = coef[2:3] * coef[1:2]
    return mask * (scale * (grad_pre - (total[0:1] + normed * total[1:2]) / count))


def conv_space_into(d, acc, pad, weight):
    for i in range(3):
        three = weight[3 * i : 3 * i + 3].reshape(3 * d.channels, d.half)
        part = dot(space_window(d, pad, i), three)
        acc[...] = part if i == 0 else acc[...] + part


def first_space_kernel(d, w, *refs):
    ids, *refs = refs
    w_refs, refs = refs[: len(w.arrays)], refs[len(w.arrays) :]
    x, mask, s_out, sums_out, weight, sems, pad = refs
    copies = w.start(d, ids, w_refs, weight, sems)
    fill_space(d, pad, x[...].astype(F32))
    for copy in copies:
        copy.wait()
    conv_space_into(d, s_out, pad, weight)
    m = mask[...]
    values = s_out[...]
    count = jnp.sum(m, axis=0, keepdims=True) + jnp.zeros((1, d.half), F32)
    sums_out[...] = sums_of(values * m, values * values * m, count)


def second_space_kernel(d, w, *refs):
    ids, *refs = refs
    w_refs, refs = refs[: len(w.arrays)], refs[len(w.arrays) :]
    terms, refs = refs[: d.nz], refs[d.nz :]
    q, count, gains, mask, a_out, coef_out, s_out, sums_out, weight, sems, pad = refs
    copies = w.start(d, ids, w_refs, weight, sems)
    m = mask[...]
    coef = coefs_of(total_of(d, ids, terms), count[4:5, 0:1], gains[...])
    coef_out[...] = coef
    pre = coef[2:3] * normed_of(q[...].astype(F32), coef) + coef[3:4]
    act = jax.nn.silu(pre) * m
    a_out[...] = act.astype(BF)
    fill_space(d, pad, act)
    for copy in copies:
        copy.wait()
    conv_space_into(d, s_out, pad, weight)
    values = s_out[...]
    sums_out[...] = sums_of(values * m, values * values * m)


def time_kernel(d, w, *refs):
    ids, *refs = refs
    w_refs, refs = refs[: len(w.arrays)], refs[len(w.arrays) :]
    terms, refs = refs[: d.nz], refs[d.nz :]
    s, *counts, gains, mask, a_out, q_out, coef_out, weight, sems, pad = refs
    copies = w.start(d, ids, w_refs, weight, sems)
    total = total_of(d, ids, terms)
    count = counts[0][4:5, 0:1] if counts else total[2:3, 0:1]
    coef = coefs_of(total, count, gains[...])
    coef_out[...] = coef
    pre = coef[2:3] * normed_of(s[...], coef) + coef[3:4]
    act = (jax.nn.silu(pre) * mask[...]).astype(BF)
    a_out[...] = act
    fill_time(d, pad, act)
    for copy in copies:
        copy.wait()
    total = dot_nt(time_window(d, pad, 0), weight[0])
    for k in range(1, TIME):
        total = total + dot_nt(time_window(d, pad, k), weight[k])
    q_out[...] = total.astype(BF)


def join_kernel(qa, qb, mask, q_out, sums_out):
    total = (qa[...].astype(F32) + qb[...].astype(F32)).astype(BF)
    q_out[...] = total
    values = total.astype(F32)
    m = mask[...]
    sums_out[...] = sums_of(values * m, values * values * m)


def head_kernel(d, w, denominator, classes, *refs):
    ids, *refs = refs
    w_refs, refs = refs[: len(w.arrays)], refs[len(w.arrays) :]
    terms, refs = refs[: d.nz], refs[d.nz :]
    q, count, gains, mask, x, bias, clip_info, labels, *refs = refs
    coef_out, grad_out, sums_out, head, sems = refs
    copies = w.start(d, ids, w_refs, head, sems)
    m = mask[...]
    coef = coefs_of(total_of(d, ids, terms), count[4:5, 0:1], gains[...])
    coef_out[...] = coef
    normed = normed_of(q[...].astype(F32), coef)
    pre = coef[2:3] * normed + coef[3:4] + x[...].astype(F32)
    sigma = jax.nn.sigmoid(pre)
    y = pre * sigma * m
    folded = jnp.sum(y.reshape(d.cells // 8, 8, d.channels), axis=0)
    step = d.clips
    total = folded
    for k in range(1, 8 // step):
        total = total + pltpu.roll(folded, k * step, 0)
    inverse = 1.0 / clip_info[:, 0:1]
    pooled = total * inverse
    pooled_bf = pooled.astype(BF)
    for copy in copies:
        copy.wait()
    weight = head[0, :, : d.channels]
    logits = dot(pooled_bf, weight) + bias[...]
    largest = jnp.max(logits, axis=1, keepdims=True)
    shifted = jnp.exp(logits - largest)
    log_total = largest + jnp.log(jnp.sum(shifted, axis=1, keepdims=True))
    lane = lax.broadcasted_iota(jnp.int32, logits.shape, 1)
    onehot = jnp.where(lane == labels[:, 0:1], 1.0, 0.0)
    inside = lane < classes
    kept = jnp.where(inside, logits, 0.0)
    loss = log_total - jnp.sum(kept * onehot, axis=1, keepdims=True)
    grad_logits = jnp.where(inside, (jnp.exp(logits - log_total) - onehot) / denominator, 0.0)
    grad_pooled = dot_nt(grad_logits.astype(BF), weight) * inverse
    grad_y = jnp.broadcast_to(grad_pooled[None], (d.cells // 8, 8, d.channels)).reshape(
        d.cells, d.channels
    )
    grad_pre = grad_y * m * (sigma * (1.0 + pre * (1.0 - sigma)))
    grad_out[...] = grad_pre
    sums_out[0:8, :] = sums_of(grad_pre, grad_pre * normed)
    carried = jnp.where(lane == classes, loss, grad_logits)
    sums_out[8:16, :] = jnp.concatenate(
        [
            pooled_bf.astype(F32)[0 : d.clips],
            carried[0 : d.clips],
            jnp.zeros((8 - 2 * d.clips, d.channels), F32),
        ],
        axis=0,
    )


def time_back_kernel(d, w, *refs):
    ids, *refs = refs
    w_refs, refs = refs[: len(w.arrays)], refs[len(w.arrays) :]
    terms, refs = refs[: d.nz], refs[d.nz :]
    grad_two, q, coef_two, count, mask, s, coef_one, *refs = refs
    gq_out, grad_out, sums_out, tot_out, weight, sems, pad = refs
    copies = w.start(d, ids, w_refs, weight, sems)
    m = mask[...]
    total = total_of(d, ids, terms)
    tot_out[...] = total
    coef = coef_two[...]
    normed = normed_of(q[...].astype(F32), coef)
    grad_q = norm_back(grad_two[...], normed, coef, total, count[4:5, 0:1], m).astype(BF)
    gq_out[...] = grad_q
    fill_time(d, pad, grad_q)
    for copy in copies:
        copy.wait()
    grad = dot(time_window(d, pad, TIME - 1), weight[0])
    for k in range(1, TIME):
        grad = grad + dot(time_window(d, pad, TIME - 1 - k), weight[k])
    grad = grad.astype(BF).astype(F32)
    coef = coef_one[...]
    normed = normed_of(s[...], coef)
    pre = coef[2:3] * normed + coef[3:4]
    grad_pre = grad * m * act_slope(pre)
    grad_out[...] = grad_pre
    sums_out[...] = sums_of(grad_pre, grad_pre * normed)


def space_back_kernel(d, w, *refs):
    ids, *refs = refs
    w_refs, refs = refs[: len(w.arrays)], refs[len(w.arrays) :]
    terms, refs = refs[: d.nz], refs[d.nz :]
    grad_pre, s, coef_one, count, mask, *refs = refs
    gs_out, ga_out, tot_out, weight, sems, pad, acc = refs
    copies = w.start(d, ids, w_refs, weight, sems)
    total = total_of(d, ids, terms)
    tot_out[...] = total
    coef = coef_one[...]
    normed = normed_of(s[...], coef)
    grad_s = norm_back(grad_pre[...], normed, coef, total, count[4:5, 0:1], mask[...])
    gs_out[...] = grad_s.astype(BF)
    fill_space(d, pad, grad_s)
    for copy in copies:
        copy.wait()
    for i in range(3):
        part = sum(dot_nt(space_window(d, pad, 2 - i, 2 - j), weight[3 * i + j]) for j in range(3))
        acc[...] = part if i == 0 else acc[...] + part
    ga_out[...] = acc[...].astype(BF)


def join_back_kernel(ga, gb, q, coef_two, mask, grad_out, sums_out):
    coef = coef_two[...]
    normed = normed_of(q[...].astype(F32), coef)
    pre = coef[2:3] * normed + coef[3:4]
    grad = ga[...].astype(F32) + gb[...].astype(F32)
    grad_pre = grad * mask[...] * act_slope(pre)
    grad_out[...] = grad_pre
    sums_out[...] = sums_of(grad_pre, grad_pre * normed)


def write_grad(d, w, ids, value, outs, held):
    if w.kind == "natural":
        outs[0][0] = value.astype(BF)
        return
    held[...] = value.astype(BF)
    for operand, index, row in w.places(d, ids):
        block = held[pl.ds(pl.multiple_of(row, 16), d.rows), :]
        outs[operand][(*index, 0)] = block


def time_grad_kernel(d, w, *refs):
    ids, grad_q, act, *refs = refs
    outs, (pad, turned, held) = refs[:-3], refs[-3:]
    k = pl.program_id(0)

    @pl.when(k == 0)
    def _():
        fill_time(d, pad, act[...])
        turned[...] = jnp.transpose(grad_q[...].astype(F32)).astype(BF)

    write_grad(d, w, ids, dot(turned[...], time_window(d, pad, k)), outs, held)


def unit_grad_kernel(d, w, *refs):
    ids, a, grad_s, grad_q, act, *refs = refs
    outs, (pad, time_pad, time_turned, turned, held) = refs[:-5], refs[-5:]
    k = pl.program_id(0)

    @pl.when(k == 0)
    def _():
        fill_space(d, pad, grad_s[...].astype(F32))
        turned[...] = jnp.transpose(a[...].astype(F32)).astype(BF)
        fill_time(d, time_pad, act[...])
        time_turned[...] = jnp.transpose(grad_q[...].astype(F32)).astype(BF)

    @pl.when(k < SPACE)
    def _():
        window = space_window(d, pad, 2 - lax.div(k, 3), 2 - lax.rem(k, 3))
        write_grad(d, w, ids, dot(turned[...], window), outs, held)

    @pl.when(k >= SPACE)
    def _():
        window = time_window(d, time_pad, k - SPACE)
        write_grad(d, w, ids, dot(time_turned[...], window), outs, held)


def last_space_grad_kernel(d, w, *refs):
    ids, *refs = refs
    terms, refs = refs[: d.nz], refs[d.nz :]
    a, grad_pre, s, coef_one, count, mask, tot_out, *refs = refs
    outs, (pad, turned, held) = refs[:-3], refs[-3:]
    k = pl.program_id(0)

    @pl.when(k == 0)
    def _():
        total = total_of(d, ids, terms)
        tot_out[...] = total
        coef = coef_one[...]
        normed = normed_of(s[...], coef)
        grad_s = norm_back(grad_pre[...], normed, coef, total, count[4:5, 0:1], mask[...])
        fill_space(d, pad, grad_s)
        turned[...] = jnp.transpose(a[...].astype(F32)).astype(BF)

    window = space_window(d, pad, 2 - lax.div(k, 3), 2 - lax.rem(k, 3))
    write_grad(d, w, ids, dot(turned[...], window), outs, held)


def squares_kernel(*refs):
    *values, out = refs
    row = lax.broadcasted_iota(jnp.int32, (8, LANES), 0)
    lane = lax.broadcasted_iota(jnp.int32, (8, LANES), 1)
    total = jnp.zeros((8, LANES), F32)
    for i, value in enumerate(values):
        here = (row == i // 5) & (lane == i % 5)
        lanes = jnp.sum(value[...], axis=0, keepdims=True)
        total = jnp.where(here, jnp.sum(lanes, axis=1, keepdims=True), total)
    out[...] = total


def sds(shape, dtype=F32):
    return jax.ShapeDtypeStruct(shape, dtype)


def call(body, name, ins, outs, scratch, flops, megabytes=40):
    return pl.pallas_call(
        body,
        name=name,
        out_shape=outs,
        in_specs=[spec for spec, _ in ins],
        out_specs=[whole()] * len(outs),
        scratch_shapes=scratch,
        compiler_params=pltpu.CompilerParams(vmem_limit_bytes=megabytes * MB),
        cost_estimate=pl.CostEstimate(flops=flops, bytes_accessed=8 * MB, transcendentals=0),
    )(*[value for _, value in ins])


def w_ins(weight):
    return [
        (in_hbm(), pltpu.with_memory_space_constraint(piece, pltpu.HBM))
        for piece in weight.arrays
    ]


def v_ins(*values):
    return [(whole(), value) for value in values]


def grad_call(d, body, name, kind, taps, ids, values, first_outs, scratch):
    if kind == "ring":
        shape, count = (d.nz, 2, taps, d.rows, d.half), 4
        spec = pl.BlockSpec((d.nz, 2, 1, d.rows, d.half), lambda k: (0, 0, k, 0, 0))
    elif kind == "parts":
        shape, count = (2, 2, taps, d.rows, d.half), d.groups // 2
        spec = pl.BlockSpec((2, 2, 1, d.rows, d.half), lambda k: (0, 0, k, 0, 0))
        first_outs = [*first_outs, sds((d.groups, *shape[1:]), BF)]
    else:
        shape, count = (taps, d.channels, d.half), 1
        spec = pl.BlockSpec((1, d.channels, d.half), lambda k: (k, 0, 0))
    fixed = [pl.BlockSpec(out.shape, lambda k: (0, 0)) for out in first_outs]
    if kind == "parts":
        fixed[-1] = pl.BlockSpec((d.groups, 2, 1, d.rows, d.half), lambda k: (0, 0, k, 0, 0))
    outs = pl.pallas_call(
        functools.partial(body, d, Weight(kind, (), 0, 1)),
        name=name,
        grid=(taps,),
        out_shape=list(first_outs) + [sds(shape, BF)] * count,
        in_specs=[smem()] + [whole()] * len(values),
        out_specs=fixed + [spec] * count,
        scratch_shapes=scratch
        + [pltpu.VMEM((d.channels, d.cells), BF), pltpu.VMEM((d.channels, d.half), BF)],
        compiler_params=pltpu.CompilerParams(vmem_limit_bytes=40 * MB),
        cost_estimate=pl.CostEstimate(flops=1, bytes_accessed=1, transcendentals=0),
    )(ids, *values)
    return outs[: len(first_outs)], outs[len(first_outs) :]


def swap(value, axis, distance=1):
    size = lax.axis_size(axis)
    return lax.ppermute(value, axis, [(i, i ^ distance) for i in range(size)])


def across_yy(values, *besides):
    size = lax.axis_size("yy")
    distance = 1
    while distance < size:
        other = swap(values, "yy", distance)
        distance *= 2
        values = values + (after(other, *besides) if distance >= size else other)
    return values


def around_tm(values):
    size = lax.axis_size("tm")
    return [values] + [
        lax.ppermute(values, "tm", [(i, (i + k) % size) for i in range(size)])
        for k in range(1, size)
    ]


def data_sums(values, last=(), first=()):
    terms = around_tm(across_yy(values, *first))
    return [after(term, *last) if k == len(terms) - 1 else term for k, term in enumerate(terms)]


def data_sums_gather(values):
    distance = 1
    while distance < lax.axis_size("yy"):
        other = swap(values, "yy", distance)
        values = jnp.concatenate([values[:8] + other[:8], values[8:], other[8:]], axis=0)
        distance *= 2
    terms = around_tm(values)
    return [term[:8] for term in terms], jnp.concatenate([term[8:] for term in terms], axis=0)


def pick(index, first, second):
    return jnp.where(index == 0, first, second)


def after(value, *earlier):
    if not earlier:
        return value
    return lax.optimization_barrier((value, *earlier))[0]


def turn(value):
    size = lax.axis_size("tm")
    return lax.ppermute(value, "tm", [(i, (i + 1) % size) for i in range(size)])


def together(*values):
    return lax.optimization_barrier(values)


def gather_ring(both, besides):
    held, across, made = [both], [], []
    for beside in besides:
        moves = [swap(held[-1], "yy")]
        if len(held) < lax.axis_size("tm"):
            moves.append(turn(held[-1]))
        extra = beside(held[-1], made[-1] if made else None)
        results = together(*moves, *extra)
        across.append(results[0])
        held += results[1 : len(moves)]
        made.append(results[len(moves) :])
    own = held + across
    return Weight("blocks", own + [swap(block, "u") for block in own], 0, both.shape[1]), made


def gather_all(d, s, u, both, *earlier):
    own = after(lax.all_gather(both, DATA, axis=0, tiled=False), *earlier)
    sibling = swap(own, "u")
    taps = both.shape[1]
    if d.pieces:
        return Weight("all", (own, sibling), 0, taps)
    parts = jnp.stack([own, sibling]).reshape(2, d.ny, d.nz, 2, taps, d.rows, d.half)
    parts = jnp.where(u == 0, parts, parts[::-1])
    parts = jnp.where(s == 0, parts, parts[:, :, :, ::-1])
    natural = parts.transpose(4, 1, 3, 0, 2, 5, 6).reshape(taps, d.channels, d.half)
    return Weight("natural", (natural,), 0, taps)


def added(*values):
    total = values[0].astype(F32)
    for value in values[1:]:
        total = total + value.astype(F32)
    return total.astype(BF)


def reduce_ring(d, gradients):
    def joined(yrel, k, *others):
        parts = [outs[yrel][k].astype(F32) + outs[2 + yrel][k].astype(F32) for outs in gradients]
        total = jnp.concatenate(parts, axis=1)
        for other in others:
            total = total + other.astype(F32)
        return total.astype(BF)

    moving = None
    for k in range(1, d.nz):
        terms = [swap(joined(1, k), "yy")]
        if moving is not None:
            terms.append(turn(moving))
        moving = joined(0, k, *terms)
    across = swap(joined(1, 0), "yy")
    last = joined(0, 0, across)
    theirs = added(last[1], turn(moving[1]))
    return added(last[0], turn(moving[0])), theirs


def reduce_all(d, s, u, kind, outs, *earlier):
    if kind == "parts":
        keep, *sends = outs
        theirs = [swap(send, "u") for send in sends]
    else:
        (natural,) = outs
        taps = natural.shape[0]
        parts = natural.reshape(taps, d.ny, 2, 2, d.nz, d.rows, d.half)
        parts = parts.transpose(3, 1, 4, 2, 0, 5, 6)
        parts = jnp.where(u == 0, parts, parts[::-1])
        parts = jnp.where(s == 0, parts, parts[:, :, :, ::-1])
        keep, send = parts.reshape(2, d.groups, 2, taps, d.rows, d.half)
        theirs = [swap(send, "u")]
    keep, theirs = after((keep, theirs), *earlier)
    both = added(keep, jnp.concatenate(theirs, axis=0))
    return both, lax.psum_scatter(both, DATA, scatter_dimension=0, tiled=False)


def own_rows(d, s, mine, theirs):
    other = swap(theirs, "s")
    return pick(s, mine, other), pick(s, other, mine)[..., : d.mid - d.half]


def whole_rows(halves_of_rows):
    return jnp.concatenate(halves_of_rows, axis=-1).astype(F32)


def halves(d, values):
    fill = [(0, 0)] * (values.ndim - 1) + [(0, 2 * d.half - d.mid)]
    return values[..., : d.half], jnp.pad(values[..., d.half :], fill)


def rows_of(gain, shift):
    return jnp.concatenate(
        [gain[None], shift[None], jnp.zeros((6, gain.shape[0]), F32)], axis=0
    )


def square_rows(values):
    return jnp.sum(values * values, axis=tuple(range(1, values.ndim - 1)))


def adam_part(weight, gradient, moment_one, moment_two, decay):
    new_one = BETA_ONE * moment_one + (1.0 - BETA_ONE) * gradient
    new_two = BETA_TWO * moment_two + (1.0 - BETA_TWO) * gradient * gradient
    direction = (
        new_one / (1.0 - BETA_ONE**STEP) / (jnp.sqrt(new_two / (1.0 - BETA_TWO**STEP)) + EPS_ADAM)
        + decay * weight
    )
    return (new_one, new_two, direction)


def on_device(
    clips_x,
    frames,
    labels,
    spatial_weight,
    temporal_weight,
    head_weight,
    affine,
    head_bias,
    spatial_first,
    spatial_second,
    temporal_first,
    temporal_second,
    head_first,
    head_second,
    affine_first,
    affine_second,
    bias_first,
    bias_second,
):
    s, u, z, yy = (lax.axis_index(axis) for axis in ("s", "u", "tm", "yy"))
    ny, nz = lax.axis_size("yy"), lax.axis_size("tm")
    micro, clips, _, height, width, channels = clips_x.shape
    mid = spatial_weight.shape[3]
    rows = spatial_weight.shape[0]
    classes = head_weight.shape[1]
    d = Dims(clips, nz, height, width, channels, mid, rows, ny, nz)
    assert nz == 4 and micro == 2
    ids = jnp.stack([s, u, yy, z]).astype(jnp.int32)
    denominator = micro * clips * 4 * ny

    def prepared(weight, l):
        return halves(d, weight[:, l].astype(BF).transpose(1, 0, 2))

    def paired(parts, *earlier):
        first = jnp.concatenate([part[0] for part in parts], axis=0)
        second = jnp.concatenate([part[1] for part in parts], axis=0)
        send = after(pick(s, second, first), *earlier)
        return jnp.stack([pick(s, first, second), swap(send, "s")])

    def by_index(index, mine, other):
        return jnp.stack([pick(index, mine, other), pick(index, other, mine)])

    pairs = []
    for value in (clips_x, jnp.stack([frames, labels]).transpose(1, 0, 2)):
        kept = pick(u, value[0], value[1])
        pairs.append(by_index(u, kept, swap(pick(u, value[1], value[0]), "u")))
    early = paired([prepared(spatial_weight, 0), prepared(temporal_weight, 0)])

    def beside_first(*_):
        four, info = (by_index(s, pair, swap(pair, "s")) for pair in pairs)
        return four.reshape(nz, clips, height * width, channels), info

    def clips_home(four):
        return lax.all_to_all(four, "tm", split_axis=0, concat_axis=0, tiled=True)

    def beside_second(block, first):
        weights = after((spatial_weight, temporal_weight, head_weight), block)
        slot = jnp.pad(weights[2].astype(BF), ((0, 0), (0, d.half - classes)))[None]
        parts = [prepared(weights[0], 1), prepared(weights[1], 1), (slot, slot)]
        return [paired(parts), clips_home(first[0])]

    def beside_third(block, _):
        weights = after((spatial_weight, temporal_weight, head_weight), block)
        gains, bias = after((affine, head_bias), block)
        bias_row = jnp.full((1, channels), -1e30, F32).at[0, :classes].set(bias)
        rows_one, rows_two = [], []
        for l in range(2):
            low, high = halves(d, gains[l, :, :mid])
            mine = pick(s, low, high)
            rows_one.append(rows_of(mine[0], mine[1]))
            rows_two.append(rows_of(gains[l, 0, mid:], gains[l, 1, mid:]))
        squares = [square_rows(weight[:, l]) for weight in weights[:2] for l in range(2)]
        return [bias_row, *rows_one, *rows_two, *squares, square_rows(weights[2])]

    if d.pieces:
        early_w, made = gather_ring(
            early, [beside_first, beside_second, beside_third, lambda *_: []]
        )
        (_, info_four), (late, clip_all), small, _ = made
    else:
        early_w = gather_all(d, s, u, early)
        first = beside_first()
        info_four = first[1]
        (late, clip_all), small = beside_second(early, first), beside_third(early, None)
    bias_row, *small = small
    gains_one, gains_two, weight_squares = small[:2], small[2:4], small[4:]

    x = clip_all.reshape(nz, clips, height * width, channels)
    x = x.transpose(0, 2, 1, 3).reshape(d.cells, channels)

    mine_info = lax.dynamic_index_in_dim(
        info_four.reshape(nz, 2, clips), z, 0, keepdims=False
    )
    my_frames, my_labels = mine_info[0], mine_info[1]
    valid = (jnp.arange(nz, dtype=jnp.int32)[:, None] * 8 < my_frames[None, :]).astype(F32)
    mask = jnp.broadcast_to(valid[:, None, :], (nz, height * width, clips)).reshape(d.cells, 1)
    divisor = (my_frames // 8).astype(F32) * (height * width)
    clip_info = jnp.broadcast_to(jnp.tile(divisor, 8 // clips)[:, None], (8, LANES))
    label_rows = jnp.broadcast_to(jnp.tile(my_labels, 8 // clips)[:, None], (8, LANES))
    x, mask, clip_info, label_rows = together(x, mask, clip_info, label_rows)

    wide, narrow = (d.cells, d.half), (d.cells, channels)
    space_flops = 2 * d.cells * SPACE * channels * d.half
    time_flops = 2 * d.cells * TIME * channels * d.half

    space_w = [early_w.part(0, SPACE), None]
    time_w = [early_w.part(SPACE, TIME), None]

    def space_first(x_bf):
        return call(
            functools.partial(first_space_kernel, d, space_w[0]),
            "space0",
            [(smem(), ids)] + w_ins(space_w[0]) + v_ins(x_bf, mask),
            [sds(wide), sds((8, d.half))],
            space_w[0].scratch(d) + [space_scratch(d, channels)],
            space_flops,
        )

    def space_next(q, terms, count):
        return call(
            functools.partial(second_space_kernel, d, space_w[1]),
            "space1",
            [(smem(), ids)] + w_ins(space_w[1]) + v_ins(*terms, q, count, gains_two[0], mask),
            [sds(narrow, BF), sds((8, channels)), sds(wide), sds((8, d.half))],
            space_w[1].scratch(d) + [space_scratch(d, channels)],
            space_flops,
        )

    def time_next(l, s_value, terms, *count):
        return call(
            functools.partial(time_kernel, d, time_w[l]),
            f"time{l}",
            [(smem(), ids)] + w_ins(time_w[l]) + v_ins(*terms, s_value, *count, gains_one[l], mask),
            [sds(wide, BF), sds(narrow, BF), sds((8, d.half))],
            time_w[l].scratch(d) + [time_scratch(d, d.half)],
            time_flops,
        )

    def joined(q_part):
        return call(
            join_kernel,
            "join",
            v_ins(q_part, swap(q_part, "s"), mask),
            [sds(narrow, BF), sds((8, channels))],
            [],
            d.cells * channels,
        )

    s0, sums = space_first(x)
    terms = data_sums(sums)
    act0, q_part, coef_one0 = time_next(0, s0, terms)
    count = coef_one0
    q0, sums = joined(q_part)
    terms = data_sums(sums)
    late_w = gather_all(d, s, u, late, terms[0])
    space_w[1] = late_w.part(0, SPACE)
    time_w[1] = late_w.part(SPACE, TIME)
    head_w = late_w.part(SPACE + TIME, 1)
    a_mid, coef_two0, s1, sums = space_next(q0, terms, count)
    terms = data_sums(sums)
    act1, q_part, coef_one1 = time_next(1, s1, terms, count)
    q1, sums = joined(q_part)
    terms = data_sums(sums)
    coef_two1, grad_two, sums = call(
        functools.partial(head_kernel, d, head_w, float(denominator), classes),
        "head",
        [(smem(), ids)]
        + w_ins(head_w)
        + v_ins(*terms, q1, count, gains_two[1], mask, x, bias_row, clip_info, label_rows),
        [sds((8, channels)), sds(narrow), sds((16, channels))],
        head_w.scratch(d),
        4 * d.cells * channels,
    )
    terms, carried = data_sums_gather(sums)

    def time_back(l, grad, q, coef_two, terms, s_value, coef_one):
        return call(
            functools.partial(time_back_kernel, d, time_w[l]),
            f"time_back{l}",
            [(smem(), ids)]
            + w_ins(time_w[l])
            + v_ins(*terms, grad, q, coef_two, count, mask, s_value, coef_one),
            [sds(narrow, BF), sds(wide), sds((8, d.half)), sds((8, channels))],
            time_w[l].scratch(d) + [time_scratch(d, channels)],
            time_flops,
        )

    late_kind = "parts" if d.pieces else "natural"
    early_kind = "ring" if d.pieces else "natural"

    grad_q1, grad_one, sums, tot_two1 = time_back(
        1, grad_two, q1, coef_two1, terms, s1, coef_one1
    )
    terms = data_sums(sums)
    grad_s1, ga_part, tot_one1 = call(
        functools.partial(space_back_kernel, d, space_w[1]),
        "space_back",
        [(smem(), ids)] + w_ins(space_w[1]) + v_ins(*terms, grad_one, s1, coef_one1, count, mask),
        [sds(wide, BF), sds(narrow, BF), sds((8, d.half))],
        space_w[1].scratch(d)
        + [space_scratch(d, d.half), pltpu.VMEM((d.cells, channels), F32)],
        space_flops,
    )
    ga_other = swap(ga_part, "s")
    late_first, late_outs = grad_call(
        d,
        unit_grad_kernel,
        "unit_grad1",
        late_kind,
        SPACE + TIME,
        ids,
        (a_mid, grad_s1, grad_q1, act1),
        [],
        [
            space_scratch(d, d.half),
            time_scratch(d, d.half),
            pltpu.VMEM((d.channels, d.cells), BF),
        ],
    )
    late_outs = [*late_first, *late_outs]
    grad_two, sums = call(
        join_back_kernel,
        "join_back",
        v_ins(ga_part, after(ga_other, *late_outs), q0, coef_two0, mask),
        [sds(narrow), sds((8, channels))],
        [],
        20 * 10**9,
    )
    late_both, late_sum = reduce_all(d, s, u, late_kind, late_outs, sums)

    carried = jnp.concatenate([carried, swap(carried, "u")], axis=0).reshape(-1, 8, channels)
    pooled_all = carried[:, :clips].reshape(-1, channels)
    logit_all = carried[:, clips : 2 * clips].reshape(-1, channels)
    loss_sum = jnp.sum(logit_all[:, classes])
    logit_all = logit_all[:, :classes]
    bias_grad = jnp.sum(logit_all, axis=0)
    base = d.row_base(yy, s, u, z)
    pooled_mine = lax.dynamic_slice_in_dim(pooled_all, base, rows, 1)
    head_grad = lax.dot_general(
        pooled_mine.astype(BF),
        logit_all.astype(BF),
        (((0,), (0,)), ((), ())),
        preferred_element_type=F32,
    )
    head_one, head_two, head_dir = adam_part(head_weight, head_grad, head_first, head_second, DECAY)
    bias_one, bias_two, bias_dir = adam_part(head_bias, bias_grad, bias_first, bias_second, 0.0)
    head_squares = square_rows(head_dir)

    terms = data_sums(
        sums,
        (late_both, head_one, head_two, head_dir, head_squares),
        (loss_sum, bias_one, bias_two),
    )
    grad_q0, grad_one, sums, tot_two0 = time_back(
        0, grad_two, q0, coef_two0, terms, s0, coef_one0
    )
    _, time_outs0 = grad_call(
        d,
        time_grad_kernel,
        "time_grad0",
        early_kind,
        TIME,
        ids,
        (grad_q0, act0),
        [],
        [time_scratch(d, d.half)],
    )
    if d.pieces:
        time_outs0 = [*time_outs0[:2], *(swap(send, "u") for send in time_outs0[2:])]
    terms = data_sums(sums, time_outs0[2:], time_outs0[:2])
    (tot_one0,), space_outs0 = grad_call(
        d,
        last_space_grad_kernel,
        "space_grad0",
        early_kind,
        SPACE,
        ids,
        (*terms, x, grad_one, s0, coef_one0, count, mask),
        [sds((8, d.half))],
        [space_scratch(d, d.half)],
    )

    late_sum = own_rows(d, s, *after((late_sum[0], late_sum[1]), *space_outs0))
    if d.pieces:
        early_sum = reduce_ring(
            d,
            [[*space_outs0[:2], *(swap(send, "u") for send in space_outs0[2:])], time_outs0],
        )
    else:
        early_outs = [jnp.concatenate([space_outs0[0], time_outs0[0]], axis=0)]
        _, early_sum = reduce_all(d, s, u, early_kind, early_outs)
    early_sum = whole_rows(own_rows(d, s, after(early_sum[0], *late_sum), early_sum[1]))
    late_sum = whole_rows(late_sum)

    ones = jnp.stack([tot_one0[:2], tot_one1[:2]])
    twos = jnp.stack([tot_two0[:2], tot_two1[:2]])
    small = jnp.concatenate([ones, twos], axis=-1)
    small = small + swap(small, "u")
    ones, twos = small[..., : d.half], small[..., d.half :]
    ones_other = swap(ones, "s")
    low, high = pick(s, ones, ones_other), pick(s, ones_other, ones)
    both = jnp.concatenate([low, high[..., : mid - d.half], twos], axis=-1)
    affine_grad = jnp.stack([both[:, 1], both[:, 0]], axis=1)

    def units(first, second):
        return jnp.stack([first, second]).transpose(2, 0, 1, 3)

    spatial_grad = units(early_sum[:SPACE], late_sum[:SPACE])
    temporal_grad = units(early_sum[SPACE:], late_sum[SPACE:])
    space_one, space_two, space_dir = adam_part(
        spatial_weight, spatial_grad, spatial_first, spatial_second, DECAY
    )
    time_one, time_two, time_dir = adam_part(
        temporal_weight, temporal_grad, temporal_first, temporal_second, DECAY
    )
    affine_one, affine_two, affine_dir = adam_part(
        affine, affine_grad, affine_first, affine_second, 0.0
    )
    dir_squares = [square_rows(v[:, l]) for v in (space_dir, time_dir) for l in range(2)]
    dir_squares.append(head_squares)
    padded = pl.pallas_call(
        squares_kernel,
        name="squares",
        out_shape=sds((8, LANES)),
        in_specs=[whole()] * 10,
        out_specs=whole(),
    )(*weight_squares, *dir_squares)
    native, by_tap = (Layout(major_to_minor=order) for order in ((0, 2, 1, 3), (1, 2, 0, 3)))
    moments = together(
        *(with_layout_constraint(v, by_tap) for v in (space_one, space_two, time_one, time_two))
    )
    moments = [with_layout_constraint(value, native) for value in moments]
    space_one, space_two, time_one, time_two = moments
    padded = padded + swap(padded, "u")
    padded = padded + after(swap(padded, "s"), affine_one, affine_two, affine_dir)
    terms = data_sums(padded, moments[1:3], (moments[0], moments[3]))
    terms = jnp.stack(terms)
    padded = sum(terms[lax.rem(z + (nz - place), nz)] for place in range(nz))
    norms = jnp.sqrt(padded[:2, :5])
    trust = norms[0] / norms[1]
    new_space = spatial_weight - RATE * trust[0:2][None, :, None, None] * space_dir
    new_time = temporal_weight - RATE * trust[2:4][None, :, None, None] * time_dir
    new_head = head_weight - RATE * trust[4] * head_dir
    new_affine = affine - RATE_SMALL * affine_dir
    new_bias = head_bias - RATE_SMALL * bias_dir
    return (
        loss_sum,
        space_one,
        space_two,
        new_space,
        time_one,
        time_two,
        new_time,
        head_one,
        head_two,
        new_head,
        affine_one,
        affine_two,
        new_affine,
        bias_one,
        bias_two,
        new_bias,
        norms,
    )


def solution(mesh):
    dp, tm = mesh.shape["dp"], mesh.shape["tm"]
    fine = Mesh(mesh.devices.reshape(dp // 4, 2, 2, tm), ALL)
    dp_axes = ("yy", "s", "u")
    owner = P(ALL)
    return jax.shard_map(
        on_device,
        mesh=fine,
        in_specs=(
            P(None, dp_axes, "tm"),
            P(None, dp_axes),
            P(None, dp_axes),
            owner,
            owner,
            owner,
            P(),
            P(),
            owner,
            owner,
            owner,
            owner,
            owner,
            owner,
            P(),
            P(),
            P(),
            P(),
        ),
        out_specs=(P(),) + (owner,) * 9 + (P(),) * 7,
        check_vma=False,
    )
```

```python
import functools

import jax
import jax.numpy as jnp
from jax import lax
from jax.experimental import pallas as pl
from jax.experimental.layout import Layout, with_layout_constraint
from jax.experimental.pallas import tpu as pltpu
from jax.sharding import Mesh
from jax.sharding import PartitionSpec as P

STEP = 5
EPS_NORM = 1e-05
EPS_ADAM = 1e-06
BETA_ONE = 0.5
BETA_TWO = 0.5
DECAY = 0.01
RATE = 0.3
RATE_SMALL = 0.1

F32 = jnp.float32
BF = jnp.bfloat16
LANES = 128
SPACE, TIME = 9, 3
ALL = ("yy", "s", "u", "tm")
DATA = ("yy", "tm")
MB = 1 << 20


def whole():
    return pl.BlockSpec(memory_space=pltpu.VMEM)


def in_hbm():
    return pl.BlockSpec(memory_space=pltpu.HBM)


def smem():
    return pl.BlockSpec(memory_space=pltpu.SMEM)


def dot(a, b):
    return jnp.dot(a, b, preferred_element_type=F32)


def dot_nt(a, b):
    return lax.dot_general(a, b, (((1,), (1,)), ((), ())), preferred_element_type=F32)


class Dims:
    def __init__(self, clips, frames, height, width, channels, mid, rows, ny, nz):
        self.clips, self.frames, self.height, self.width = clips, frames, height, width
        self.channels, self.mid, self.rows, self.ny, self.nz = channels, mid, rows, ny, nz
        self.line = width * clips
        self.plane = height * self.line
        self.cells = frames * self.plane
        tiles = mid // LANES
        self.half = (tiles + 1) // 2 * LANES
        self.groups = ny * nz
        self.pieces = rows % 16 == 0 and ny == 2

    def row_base(self, yy, s, u, z):
        return (((yy * 2 + s) * 2 + u) * self.nz + z) * self.rows


class Weight:
    def __init__(self, kind, arrays, first, taps):
        self.kind, self.arrays, self.first, self.taps = kind, arrays, first, taps

    def part(self, first, taps):
        return Weight(self.kind, self.arrays, self.first + first, taps)

    def copies_needed(self, d):
        return 1 if self.kind == "natural" else 4 * d.groups

    def scratch(self, d):
        return [
            pltpu.VMEM((self.taps, d.channels, d.half), BF),
            pltpu.SemaphoreType.DMA((self.copies_needed(d),)),
        ]

    def places(self, d, ids):
        s, u, yy, z = (ids[i] for i in range(4))
        for urel in range(2):
            for i in range(d.groups):
                for srel in range(2):
                    if self.kind == "all":
                        row = d.row_base(i // d.nz, srel ^ s, urel, i % d.nz)
                        yield 0, (urel, i, srel), row
                        continue
                    if self.kind in ("blocks", "ring"):
                        yrel, k = i // d.nz, i % d.nz
                        row = d.row_base(
                            yrel ^ yy, srel ^ s, urel ^ u, lax.rem(z + (d.nz - k), d.nz)
                        )
                        if self.kind == "blocks":
                            yield urel * d.groups + i, (srel,), row
                        else:
                            yield urel * 2 + yrel, (k, srel), row
                    else:
                        row = d.row_base(i // d.nz, srel ^ s, urel ^ u, i % d.nz)
                        if urel == 0:
                            yield 0, (i, srel), row
                        else:
                            yield 1 + i // 2, (i % 2, srel), row

    def start(self, d, ids, refs, scratch, sems):
        taps = pl.ds(self.first, self.taps)
        copies = []
        if self.kind == "natural":
            copies.append(pltpu.make_async_copy(refs[0].at[taps], scratch, sems.at[0]))
        else:
            for operand, index, row in self.places(d, ids):
                copies.append(
                    pltpu.make_async_copy(
                        refs[operand].at[(*index, taps)],
                        scratch.at[:, pl.ds(pl.multiple_of(row, 16), d.rows), :],
                        sems.at[len(copies)],
                    )
                )
        for copy in copies:
            copy.start()
        return copies


def space_scratch(d, width):
    return pltpu.VMEM((d.frames, (d.height + 2) * d.line, 3 * width), BF)


def time_scratch(d, width):
    return pltpu.VMEM(((d.frames + 2) * d.plane, width), BF)


def fill_space(d, pad, values):
    cells, width = values.shape
    place = lax.broadcasted_iota(jnp.int32, (cells, width), 0)
    column = lax.rem(lax.div(place, d.clips), d.width)
    edge = jnp.zeros((d.frames, d.line, 3 * width), BF)
    pad[:, 0 : d.line, :] = edge
    pad[:, d.line + d.plane :, :] = edge
    left = jnp.where(column > 0, pltpu.roll(values, d.clips, 0), 0.0)
    right = jnp.where(column < d.width - 1, pltpu.roll(values, cells - d.clips, 0), 0.0)
    for j, moved in enumerate((left, values, right)):
        block = moved.astype(BF).reshape(d.frames, d.plane, width)
        pad[:, d.line : d.line + d.plane, j * width : (j + 1) * width] = block


def space_window(d, pad, i, j=None):
    rows = pl.ds(pl.multiple_of(i * d.line, d.line), d.plane)
    if j is None:
        block = pad[:, rows, :]
    else:
        width = pad.shape[-1] // 3
        block = pad[:, rows, pl.ds(pl.multiple_of(j * width, LANES), width)]
    return block.reshape(d.cells, block.shape[-1])


def fill_time(d, pad, values):
    width = values.shape[1]
    edge = jnp.zeros((d.plane, width), BF)
    pad[0 : d.plane, :] = edge
    pad[d.plane + d.cells :, :] = edge
    pad[d.plane : d.plane + d.cells, :] = values


def time_window(d, pad, k):
    return pad[pl.ds(pl.multiple_of(k * d.plane, d.plane), d.cells), :]


def sums_of(first, second, extra=None):
    width = first.shape[1]
    rows = [jnp.sum(first, axis=0, keepdims=True), jnp.sum(second, axis=0, keepdims=True)]
    if extra is not None:
        rows.append(extra)
    rows.append(jnp.zeros((8 - len(rows), width), F32))
    return jnp.concatenate(rows, axis=0)


def total_of(d, ids, terms):
    z = ids[3]
    values = [term[...] for term in terms]
    total = None
    for place in range(d.nz):
        here = values[0]
        for k in range(1, d.nz):
            here = jnp.where(lax.rem(z + (d.nz - k), d.nz) == place, values[k], here)
        total = here if total is None else total + here
    return total


def coefs_of(total, count, gains):
    average = total[0:1] / count
    scale = lax.rsqrt(total[1:2] / count - average * average + EPS_NORM)
    return jnp.concatenate(
        [
            average,
            scale,
            gains[0:2],
            jnp.broadcast_to(count, average.shape),
            jnp.zeros((3, total.shape[1]), F32),
        ],
        axis=0,
    )


def normed_of(values, coef):
    return (values - coef[0:1]) * coef[1:2]


def act_slope(pre):
    sigma = jax.nn.sigmoid(pre)
    return sigma * (1.0 + pre * (1.0 - sigma))


def norm_back(grad_pre, normed, coef, total, count, mask):
    scale = coef[2:3] * coef[1:2]
    return mask * (scale * (grad_pre - (total[0:1] + normed * total[1:2]) / count))


def conv_space_into(d, acc, pad, weight):
    for i in range(3):
        three = weight[3 * i : 3 * i + 3].reshape(3 * d.channels, d.half)
        part = dot(space_window(d, pad, i), three)
        acc[...] = part if i == 0 else acc[...] + part


def first_space_kernel(d, w, *refs):
    ids, *refs = refs
    w_refs, refs = refs[: len(w.arrays)], refs[len(w.arrays) :]
    x, mask, s_out, sums_out, weight, sems, pad = refs
    copies = w.start(d, ids, w_refs, weight, sems)
    fill_space(d, pad, x[...].astype(F32))
    for copy in copies:
        copy.wait()
    conv_space_into(d, s_out, pad, weight)
    m = mask[...]
    values = s_out[...]
    count = jnp.sum(m, axis=0, keepdims=True) + jnp.zeros((1, d.half), F32)
    sums_out[...] = sums_of(values * m, values * values * m, count)


def second_space_kernel(d, w, *refs):
    ids, *refs = refs
    w_refs, refs = refs[: len(w.arrays)], refs[len(w.arrays) :]
    terms, refs = refs[: d.nz], refs[d.nz :]
    q, count, gains, mask, a_out, coef_out, s_out, sums_out, weight, sems, pad = refs
    copies = w.start(d, ids, w_refs, weight, sems)
    m = mask[...]
    coef = coefs_of(total_of(d, ids, terms), count[4:5, 0:1], gains[...])
    coef_out[...] = coef
    pre = coef[2:3] * normed_of(q[...].astype(F32), coef) + coef[3:4]
    act = jax.nn.silu(pre) * m
    a_out[...] = act.astype(BF)
    fill_space(d, pad, act)
    for copy in copies:
        copy.wait()
    conv_space_into(d, s_out, pad, weight)
    values = s_out[...]
    sums_out[...] = sums_of(values * m, values * values * m)


def time_kernel(d, w, *refs):
    ids, *refs = refs
    w_refs, refs = refs[: len(w.arrays)], refs[len(w.arrays) :]
    terms, refs = refs[: d.nz], refs[d.nz :]
    s, *counts, gains, mask, a_out, q_out, coef_out, weight, sems, pad = refs
    copies = w.start(d, ids, w_refs, weight, sems)
    total = total_of(d, ids, terms)
    count = counts[0][4:5, 0:1] if counts else total[2:3, 0:1]
    coef = coefs_of(total, count, gains[...])
    coef_out[...] = coef
    pre = coef[2:3] * normed_of(s[...], coef) + coef[3:4]
    act = (jax.nn.silu(pre) * mask[...]).astype(BF)
    a_out[...] = act
    fill_time(d, pad, act)
    for copy in copies:
        copy.wait()
    total = dot_nt(time_window(d, pad, 0), weight[0])
    for k in range(1, TIME):
        total = total + dot_nt(time_window(d, pad, k), weight[k])
    q_out[...] = total.astype(BF)


def join_kernel(qa, qb, mask, q_out, sums_out):
    total = (qa[...].astype(F32) + qb[...].astype(F32)).astype(BF)
    q_out[...] = total
    values = total.astype(F32)
    m = mask[...]
    sums_out[...] = sums_of(values * m, values * values * m)


def head_kernel(d, w, denominator, classes, *refs):
    ids, *refs = refs
    w_refs, refs = refs[: len(w.arrays)], refs[len(w.arrays) :]
    terms, refs = refs[: d.nz], refs[d.nz :]
    q, count, gains, mask, x, bias, clip_info, labels, *refs = refs
    coef_out, grad_out, sums_out, head, sems = refs
    copies = w.start(d, ids, w_refs, head, sems)
    m = mask[...]
    coef = coefs_of(total_of(d, ids, terms), count[4:5, 0:1], gains[...])
    coef_out[...] = coef
    normed = normed_of(q[...].astype(F32), coef)
    pre = coef[2:3] * normed + coef[3:4] + x[...].astype(F32)
    sigma = jax.nn.sigmoid(pre)
    y = pre * sigma * m
    folded = jnp.sum(y.reshape(d.cells // 8, 8, d.channels), axis=0)
    step = d.clips
    total = folded
    for k in range(1, 8 // step):
        total = total + pltpu.roll(folded, k * step, 0)
    inverse = 1.0 / clip_info[:, 0:1]
    pooled = total * inverse
    pooled_bf = pooled.astype(BF)
    for copy in copies:
        copy.wait()
    weight = head[0, :, : d.channels]
    logits = dot(pooled_bf, weight) + bias[...]
    largest = jnp.max(logits, axis=1, keepdims=True)
    shifted = jnp.exp(logits - largest)
    log_total = largest + jnp.log(jnp.sum(shifted, axis=1, keepdims=True))
    lane = lax.broadcasted_iota(jnp.int32, logits.shape, 1)
    onehot = jnp.where(lane == labels[:, 0:1], 1.0, 0.0)
    inside = lane < classes
    kept = jnp.where(inside, logits, 0.0)
    loss = log_total - jnp.sum(kept * onehot, axis=1, keepdims=True)
    grad_logits = jnp.where(inside, (jnp.exp(logits - log_total) - onehot) / denominator, 0.0)
    grad_pooled = dot_nt(grad_logits.astype(BF), weight) * inverse
    grad_y = jnp.broadcast_to(grad_pooled[None], (d.cells // 8, 8, d.channels)).reshape(
        d.cells, d.channels
    )
    grad_pre = grad_y * m * (sigma * (1.0 + pre * (1.0 - sigma)))
    grad_out[...] = grad_pre
    sums_out[0:8, :] = sums_of(grad_pre, grad_pre * normed)
    carried = jnp.where(lane == classes, loss, grad_logits)
    sums_out[8:16, :] = jnp.concatenate(
        [
            pooled_bf.astype(F32)[0 : d.clips],
            carried[0 : d.clips],
            jnp.zeros((8 - 2 * d.clips, d.channels), F32),
        ],
        axis=0,
    )


def time_back_kernel(d, w, *refs):
    ids, *refs = refs
    w_refs, refs = refs[: len(w.arrays)], refs[len(w.arrays) :]
    terms, refs = refs[: d.nz], refs[d.nz :]
    grad_two, q, coef_two, count, mask, s, coef_one, *refs = refs
    gq_out, grad_out, sums_out, tot_out, weight, sems, pad = refs
    copies = w.start(d, ids, w_refs, weight, sems)
    m = mask[...]
    total = total_of(d, ids, terms)
    tot_out[...] = total
    coef = coef_two[...]
    normed = normed_of(q[...].astype(F32), coef)
    grad_q = norm_back(grad_two[...], normed, coef, total, count[4:5, 0:1], m).astype(BF)
    gq_out[...] = grad_q
    fill_time(d, pad, grad_q)
    for copy in copies:
        copy.wait()
    grad = dot(time_window(d, pad, TIME - 1), weight[0])
    for k in range(1, TIME):
        grad = grad + dot(time_window(d, pad, TIME - 1 - k), weight[k])
    grad = grad.astype(BF).astype(F32)
    coef = coef_one[...]
    normed = normed_of(s[...], coef)
    pre = coef[2:3] * normed + coef[3:4]
    grad_pre = grad * m * act_slope(pre)
    grad_out[...] = grad_pre
    sums_out[...] = sums_of(grad_pre, grad_pre * normed)


def space_back_kernel(d, w, *refs):
    ids, *refs = refs
    w_refs, refs = refs[: len(w.arrays)], refs[len(w.arrays) :]
    terms, refs = refs[: d.nz], refs[d.nz :]
    grad_pre, s, coef_one, count, mask, *refs = refs
    gs_out, ga_out, tot_out, weight, sems, pad, acc = refs
    copies = w.start(d, ids, w_refs, weight, sems)
    total = total_of(d, ids, terms)
    tot_out[...] = total
    coef = coef_one[...]
    normed = normed_of(s[...], coef)
    grad_s = norm_back(grad_pre[...], normed, coef, total, count[4:5, 0:1], mask[...])
    gs_out[...] = grad_s.astype(BF)
    fill_space(d, pad, grad_s)
    for copy in copies:
        copy.wait()
    for i in range(3):
        part = sum(dot_nt(space_window(d, pad, 2 - i, 2 - j), weight[3 * i + j]) for j in range(3))
        acc[...] = part if i == 0 else acc[...] + part
    ga_out[...] = acc[...].astype(BF)


def join_back_kernel(ga, gb, q, coef_two, mask, grad_out, sums_out):
    coef = coef_two[...]
    normed = normed_of(q[...].astype(F32), coef)
    pre = coef[2:3] * normed + coef[3:4]
    grad = ga[...].astype(F32) + gb[...].astype(F32)
    grad_pre = grad * mask[...] * act_slope(pre)
    grad_out[...] = grad_pre
    sums_out[...] = sums_of(grad_pre, grad_pre * normed)


def write_grad(d, w, ids, value, outs, held):
    if w.kind == "natural":
        outs[0][0] = value.astype(BF)
        return
    held[...] = value.astype(BF)
    for operand, index, row in w.places(d, ids):
        block = held[pl.ds(pl.multiple_of(row, 16), d.rows), :]
        outs[operand][(*index, 0)] = block


def time_grad_kernel(d, w, *refs):
    ids, grad_q, act, *refs = refs
    outs, (pad, turned, held) = refs[:-3], refs[-3:]
    k = pl.program_id(0)

    @pl.when(k == 0)
    def _():
        fill_time(d, pad, act[...])
        turned[...] = jnp.transpose(grad_q[...].astype(F32)).astype(BF)

    write_grad(d, w, ids, dot(turned[...], time_window(d, pad, k)), outs, held)


def unit_grad_kernel(d, w, *refs):
    ids, a, grad_s, grad_q, act, *refs = refs
    outs, (pad, time_pad, time_turned, turned, held) = refs[:-5], refs[-5:]
    k = pl.program_id(0)

    @pl.when(k == 0)
    def _():
        fill_space(d, pad, grad_s[...].astype(F32))
        turned[...] = jnp.transpose(a[...].astype(F32)).astype(BF)
        fill_time(d, time_pad, act[...])
        time_turned[...] = jnp.transpose(grad_q[...].astype(F32)).astype(BF)

    @pl.when(k < SPACE)
    def _():
        window = space_window(d, pad, 2 - lax.div(k, 3), 2 - lax.rem(k, 3))
        write_grad(d, w, ids, dot(turned[...], window), outs, held)

    @pl.when(k >= SPACE)
    def _():
        window = time_window(d, time_pad, k - SPACE)
        write_grad(d, w, ids, dot(time_turned[...], window), outs, held)


def last_space_grad_kernel(d, w, *refs):
    ids, *refs = refs
    terms, refs = refs[: d.nz], refs[d.nz :]
    a, grad_pre, s, coef_one, count, mask, tot_out, *refs = refs
    outs, (pad, turned, held) = refs[:-3], refs[-3:]
    k = pl.program_id(0)

    @pl.when(k == 0)
    def _():
        total = total_of(d, ids, terms)
        tot_out[...] = total
        coef = coef_one[...]
        normed = normed_of(s[...], coef)
        grad_s = norm_back(grad_pre[...], normed, coef, total, count[4:5, 0:1], mask[...])
        fill_space(d, pad, grad_s)
        turned[...] = jnp.transpose(a[...].astype(F32)).astype(BF)

    window = space_window(d, pad, 2 - lax.div(k, 3), 2 - lax.rem(k, 3))
    write_grad(d, w, ids, dot(turned[...], window), outs, held)


def squares_kernel(*refs):
    *values, out = refs
    row = lax.broadcasted_iota(jnp.int32, (8, LANES), 0)
    lane = lax.broadcasted_iota(jnp.int32, (8, LANES), 1)
    total = jnp.zeros((8, LANES), F32)
    for i, value in enumerate(values):
        here = (row == i // 5) & (lane == i % 5)
        lanes = jnp.sum(value[...], axis=0, keepdims=True)
        total = jnp.where(here, jnp.sum(lanes, axis=1, keepdims=True), total)
    out[...] = total


def sds(shape, dtype=F32):
    return jax.ShapeDtypeStruct(shape, dtype)


def call(body, name, ins, outs, scratch, flops, megabytes=24):
    return pl.pallas_call(
        body,
        name=name,
        out_shape=outs,
        in_specs=[spec for spec, _ in ins],
        out_specs=[whole()] * len(outs),
        scratch_shapes=scratch,
        compiler_params=pltpu.CompilerParams(vmem_limit_bytes=megabytes * MB),
        cost_estimate=pl.CostEstimate(flops=flops, bytes_accessed=8 * MB, transcendentals=0),
    )(*[value for _, value in ins])


def w_ins(weight):
    return [
        (in_hbm(), pltpu.with_memory_space_constraint(piece, pltpu.HBM))
        for piece in weight.arrays
    ]


def v_ins(*values):
    return [(whole(), value) for value in values]


def grad_call(d, body, name, kind, taps, ids, values, first_outs, scratch):
    if kind == "ring":
        shape, count = (d.nz, 2, taps, d.rows, d.half), 4
        spec = pl.BlockSpec((d.nz, 2, 1, d.rows, d.half), lambda k: (0, 0, k, 0, 0))
    elif kind == "parts":
        shape, count = (2, 2, taps, d.rows, d.half), d.groups // 2
        spec = pl.BlockSpec((2, 2, 1, d.rows, d.half), lambda k: (0, 0, k, 0, 0))
        first_outs = [*first_outs, sds((d.groups, *shape[1:]), BF)]
    else:
        shape, count = (taps, d.channels, d.half), 1
        spec = pl.BlockSpec((1, d.channels, d.half), lambda k: (k, 0, 0))
    fixed = [pl.BlockSpec(out.shape, lambda k: (0, 0)) for out in first_outs]
    if kind == "parts":
        fixed[-1] = pl.BlockSpec((d.groups, 2, 1, d.rows, d.half), lambda k: (0, 0, k, 0, 0))
    outs = pl.pallas_call(
        functools.partial(body, d, Weight(kind, (), 0, 1)),
        name=name,
        grid=(taps,),
        out_shape=list(first_outs) + [sds(shape, BF)] * count,
        in_specs=[smem()] + [whole()] * len(values),
        out_specs=fixed + [spec] * count,
        scratch_shapes=scratch
        + [pltpu.VMEM((d.channels, d.cells), BF), pltpu.VMEM((d.channels, d.half), BF)],
        compiler_params=pltpu.CompilerParams(vmem_limit_bytes=24 * MB),
        cost_estimate=pl.CostEstimate(flops=1, bytes_accessed=1, transcendentals=0),
    )(ids, *values)
    return outs[: len(first_outs)], outs[len(first_outs) :]


def swap(value, axis, distance=1):
    size = lax.axis_size(axis)
    return lax.ppermute(value, axis, [(i, i ^ distance) for i in range(size)])


def across_yy(values, *besides):
    size = lax.axis_size("yy")
    distance = 1
    while distance < size:
        other = swap(values, "yy", distance)
        distance *= 2
        values = values + (after(other, *besides) if distance >= size else other)
    return values


def around_tm(values):
    size = lax.axis_size("tm")
    return [values] + [
        lax.ppermute(values, "tm", [(i, (i + k) % size) for i in range(size)])
        for k in range(1, size)
    ]


def data_sums(values, last=(), first=()):
    terms = around_tm(across_yy(values, *first))
    return [after(term, *last) if k == len(terms) - 1 else term for k, term in enumerate(terms)]


def data_sums_gather(values):
    distance = 1
    while distance < lax.axis_size("yy"):
        other = swap(values, "yy", distance)
        values = jnp.concatenate([values[:8] + other[:8], values[8:], other[8:]], axis=0)
        distance *= 2
    terms = around_tm(values)
    return [term[:8] for term in terms], terms


def pick(index, first, second):
    return jnp.where(index == 0, first, second)


def after(value, *earlier):
    if not earlier:
        return value
    return lax.optimization_barrier((value, *earlier))[0]


def turn(value):
    size = lax.axis_size("tm")
    return lax.ppermute(value, "tm", [(i, (i + 1) % size) for i in range(size)])


def together(*values):
    return lax.optimization_barrier(values)


def gather_ring(both, besides):
    held, across, made = [both], [], []
    for beside in besides:
        moves = [swap(held[-1], "yy")]
        if len(held) < lax.axis_size("tm"):
            moves.append(turn(held[-1]))
        extra = beside(held[-1], made[-1] if made else None)
        results = together(*moves, *extra)
        across.append(results[0])
        held += results[1 : len(moves)]
        made.append(results[len(moves) :])
    own = held + across
    return Weight("blocks", own + [swap(block, "u") for block in own], 0, both.shape[1]), made


def gather_all(d, s, both, *earlier):
    gathered = lax.all_gather(both, ("u",) + DATA, axis=0, tiled=False)
    gathered = after(gathered, *earlier).reshape(2, d.groups, *both.shape)
    taps = both.shape[1]
    if d.pieces:
        return Weight("all", (gathered,), 0, taps)
    parts = gathered.reshape(2, d.ny, d.nz, 2, taps, d.rows, d.half)
    parts = jnp.where(s == 0, parts, parts[:, :, :, ::-1])
    natural = parts.transpose(4, 1, 3, 0, 2, 5, 6).reshape(taps, d.channels, d.half)
    return Weight("natural", (natural,), 0, taps)


def added(*values):
    total = values[0].astype(F32)
    for value in values[1:]:
        total = total + value.astype(F32)
    return total.astype(BF)


def reduce_ring(d, gradients, beside):
    def joined(yrel, k, *others, second=None):
        parts = [outs[yrel][k].astype(F32) + outs[2 + yrel][k].astype(F32) for outs in gradients]
        total = jnp.concatenate(parts, axis=1)
        for other in others:
            total = total + other.astype(F32)
        if second is not None:
            total = jnp.stack([total[0], total[1] + second.astype(F32)])
        return total.astype(BF)

    first = joined(1, 1)
    by_y, by_z = swap(first[0], "yy"), turn(first[1])
    moving = joined(0, 1)
    moving = jnp.stack([added(moving[0], by_y), moving[1]])
    for k in list(range(2, d.nz)) + [0]:
        across = swap(joined(1, k, second=by_z if k == 2 else None), "yy")
        turned = turn(moving)
        if k == 3:
            turned, *made = together(turned, *beside(moving))
        moving = joined(0, k, across, turned)
    return moving, made


def reduce_all(d, s, u, kind, outs, *earlier):
    if kind == "parts":
        keep, *sends = outs
        theirs = [swap(send, "u") for send in sends]
    else:
        (natural,) = outs
        taps = natural.shape[0]
        parts = natural.reshape(taps, d.ny, 2, 2, d.nz, d.rows, d.half)
        parts = parts.transpose(3, 1, 4, 2, 0, 5, 6)
        parts = jnp.where(u == 0, parts, parts[::-1])
        parts = jnp.where(s == 0, parts, parts[:, :, :, ::-1])
        keep, send = parts.reshape(2, d.groups, 2, taps, d.rows, d.half)
        theirs = [swap(send, "u")]
    keep, theirs = after((keep, theirs), *earlier)
    both = added(keep, jnp.concatenate(theirs, axis=0))
    return both, lax.psum_scatter(both, DATA, scatter_dimension=0, tiled=False)


def own_rows(d, s, mine, theirs):
    other = swap(theirs, "s")
    return pick(s, mine, other), pick(s, other, mine)[..., : d.mid - d.half]


def whole_rows(halves_of_rows):
    return jnp.concatenate(halves_of_rows, axis=-1).astype(F32)


def halves(d, values):
    fill = [(0, 0)] * (values.ndim - 1) + [(0, 2 * d.half - d.mid)]
    return values[..., : d.half], jnp.pad(values[..., d.half :], fill)


def rows_of(gain, shift):
    return jnp.concatenate(
        [gain[None], shift[None], jnp.zeros((6, gain.shape[0]), F32)], axis=0
    )


def square_rows(values):
    return jnp.sum(values * values, axis=tuple(range(1, values.ndim - 1)))


def adam_part(weight, gradient, moment_one, moment_two, decay):
    new_one = BETA_ONE * moment_one + (1.0 - BETA_ONE) * gradient
    new_two = BETA_TWO * moment_two + (1.0 - BETA_TWO) * gradient * gradient
    direction = (
        new_one / (1.0 - BETA_ONE**STEP) / (jnp.sqrt(new_two / (1.0 - BETA_TWO**STEP)) + EPS_ADAM)
        + decay * weight
    )
    return (new_one, new_two, direction)


def on_device(
    clips_x,
    frames,
    labels,
    spatial_weight,
    temporal_weight,
    head_weight,
    affine,
    head_bias,
    spatial_first,
    spatial_second,
    temporal_first,
    temporal_second,
    head_first,
    head_second,
    affine_first,
    affine_second,
    bias_first,
    bias_second,
):
    s, u, z, yy = (lax.axis_index(axis) for axis in ("s", "u", "tm", "yy"))
    ny, nz = lax.axis_size("yy"), lax.axis_size("tm")
    micro, clips, _, height, width, channels = clips_x.shape
    mid = spatial_weight.shape[3]
    rows = spatial_weight.shape[0]
    classes = head_weight.shape[1]
    d = Dims(clips, nz, height, width, channels, mid, rows, ny, nz)
    assert nz == 4 and micro == 2
    ids = jnp.stack([s, u, yy, z]).astype(jnp.int32)
    denominator = micro * clips * 4 * ny

    def prepared(weight, l):
        return halves(d, weight[:, l].astype(BF).transpose(1, 0, 2))

    def paired(parts, *earlier):
        first = jnp.concatenate([part[0] for part in parts], axis=0)
        second = jnp.concatenate([part[1] for part in parts], axis=0)
        send = after(pick(s, second, first), *earlier)
        return jnp.stack([pick(s, first, second), swap(send, "s")])

    def by_index(index, mine, other):
        return jnp.stack([pick(index, mine, other), pick(index, other, mine)])

    pairs = []
    for value in (clips_x, jnp.stack([frames, labels]).transpose(1, 0, 2)):
        kept = pick(u, value[0], value[1])
        pairs.append(by_index(u, kept, swap(pick(u, value[1], value[0]), "u")))
    early = paired([prepared(spatial_weight, 0), prepared(temporal_weight, 0)])

    def beside_first(*_):
        four, info = (by_index(s, pair, swap(pair, "s")) for pair in pairs)
        return four.reshape(nz, clips, height * width, channels), info

    def clips_home(four):
        return lax.all_to_all(four, "tm", split_axis=0, concat_axis=0, tiled=True)

    def beside_second(block, first):
        weights = after((spatial_weight, temporal_weight, head_weight), block)
        slot = jnp.pad(weights[2].astype(BF), ((0, 0), (0, d.half - classes)))[None]
        parts = [prepared(weights[0], 1), prepared(weights[1], 1), (slot, slot)]
        return [paired(parts), clips_home(first[0])]

    def beside_third(block, _):
        weights = after((spatial_weight, temporal_weight, head_weight), block)
        gains, bias = after((affine, head_bias), block)
        bias_row = jnp.full((1, channels), -1e30, F32).at[0, :classes].set(bias)
        rows_one, rows_two = [], []
        for l in range(2):
            low, high = halves(d, gains[l, :, :mid])
            mine = pick(s, low, high)
            rows_one.append(rows_of(mine[0], mine[1]))
            rows_two.append(rows_of(gains[l, 0, mid:], gains[l, 1, mid:]))
        squares = [square_rows(weight[:, l]) for weight in weights[:2] for l in range(2)]
        return [bias_row, *rows_one, *rows_two, *squares, square_rows(weights[2])]

    if d.pieces:
        early_w, made = gather_ring(
            early, [beside_first, beside_second, beside_third, lambda *_: []]
        )
        (_, info_four), (late, clip_all), small, _ = made
    else:
        early_w = gather_all(d, s, early)
        first = beside_first()
        info_four = first[1]
        (late, clip_all), small = beside_second(early, first), beside_third(early, None)
    bias_row, *small = small
    gains_one, gains_two, weight_squares = small[:2], small[2:4], small[4:]

    x = clip_all.reshape(nz, clips, height * width, channels)
    x = x.transpose(0, 2, 1, 3).reshape(d.cells, channels)

    mine_info = lax.dynamic_index_in_dim(
        info_four.reshape(nz, 2, clips), z, 0, keepdims=False
    )
    my_frames, my_labels = mine_info[0], mine_info[1]
    valid = (jnp.arange(nz, dtype=jnp.int32)[:, None] * 8 < my_frames[None, :]).astype(F32)
    mask = jnp.broadcast_to(valid[:, None, :], (nz, height * width, clips)).reshape(d.cells, 1)
    divisor = (my_frames // 8).astype(F32) * (height * width)
    clip_info = jnp.broadcast_to(jnp.tile(divisor, 8 // clips)[:, None], (8, LANES))
    label_rows = jnp.broadcast_to(jnp.tile(my_labels, 8 // clips)[:, None], (8, LANES))
    x, mask, clip_info, label_rows = together(x, mask, clip_info, label_rows)

    wide, narrow = (d.cells, d.half), (d.cells, channels)
    space_flops = 2 * d.cells * SPACE * channels * d.half
    time_flops = 2 * d.cells * TIME * channels * d.half

    space_w = [early_w.part(0, SPACE), None]
    time_w = [early_w.part(SPACE, TIME), None]

    def space_first(x_bf):
        return call(
            functools.partial(first_space_kernel, d, space_w[0]),
            "space0",
            [(smem(), ids)] + w_ins(space_w[0]) + v_ins(x_bf, mask),
            [sds(wide), sds((8, d.half))],
            space_w[0].scratch(d) + [space_scratch(d, channels)],
            space_flops,
        )

    def space_next(q, terms, count):
        return call(
            functools.partial(second_space_kernel, d, space_w[1]),
            "space1",
            [(smem(), ids)] + w_ins(space_w[1]) + v_ins(*terms, q, count, gains_two[0], mask),
            [sds(narrow, BF), sds((8, channels)), sds(wide), sds((8, d.half))],
            space_w[1].scratch(d) + [space_scratch(d, channels)],
            space_flops,
        )

    def time_next(l, s_value, terms, *count):
        return call(
            functools.partial(time_kernel, d, time_w[l]),
            f"time{l}",
            [(smem(), ids)] + w_ins(time_w[l]) + v_ins(*terms, s_value, *count, gains_one[l], mask),
            [sds(wide, BF), sds(narrow, BF), sds((8, d.half))],
            time_w[l].scratch(d) + [time_scratch(d, d.half)],
            time_flops,
        )

    def joined(q_part):
        return call(
            join_kernel,
            "join",
            v_ins(q_part, swap(q_part, "s"), mask),
            [sds(narrow, BF), sds((8, channels))],
            [],
            d.cells * channels,
            12,
        )

    s0, sums = space_first(x)
    terms = data_sums(sums)
    act0, q_part, coef_one0 = time_next(0, s0, terms)
    count = coef_one0
    q0, sums = joined(q_part)
    terms = data_sums(sums)
    late_w = gather_all(d, s, late, terms[0])
    space_w[1] = late_w.part(0, SPACE)
    time_w[1] = late_w.part(SPACE, TIME)
    head_w = late_w.part(SPACE + TIME, 1)
    a_mid, coef_two0, s1, sums = space_next(q0, terms, count)
    terms = data_sums(sums)
    act1, q_part, coef_one1 = time_next(1, s1, terms, count)
    q1, sums = joined(q_part)
    terms = data_sums(sums)
    coef_two1, grad_two, sums = call(
        functools.partial(head_kernel, d, head_w, float(denominator), classes),
        "head",
        [(smem(), ids)]
        + w_ins(head_w)
        + v_ins(*terms, q1, count, gains_two[1], mask, x, bias_row, clip_info, label_rows),
        [sds((8, channels)), sds(narrow), sds((16, channels))],
        head_w.scratch(d),
        4 * d.cells * channels,
    )
    terms, carried = data_sums_gather(sums)

    def time_back(l, grad, q, coef_two, terms, s_value, coef_one):
        return call(
            functools.partial(time_back_kernel, d, time_w[l]),
            f"time_back{l}",
            [(smem(), ids)]
            + w_ins(time_w[l])
            + v_ins(*terms, grad, q, coef_two, count, mask, s_value, coef_one),
            [sds(narrow, BF), sds(wide), sds((8, d.half)), sds((8, channels))],
            time_w[l].scratch(d) + [time_scratch(d, channels)],
            time_flops,
        )

    late_kind = "parts" if d.pieces else "natural"
    early_kind = "ring" if d.pieces else "natural"

    grad_q1, grad_one, sums, tot_two1 = time_back(
        1, grad_two, q1, coef_two1, terms, s1, coef_one1
    )
    terms = data_sums(sums)
    grad_s1, ga_part, tot_one1 = call(
        functools.partial(space_back_kernel, d, space_w[1]),
        "space_back",
        [(smem(), ids)] + w_ins(space_w[1]) + v_ins(*terms, grad_one, s1, coef_one1, count, mask),
        [sds(wide, BF), sds(narrow, BF), sds((8, d.half))],
        space_w[1].scratch(d)
        + [space_scratch(d, d.half), pltpu.VMEM((d.cells, channels), F32)],
        space_flops,
    )
    ga_other = swap(ga_part, "s")
    late_first, late_outs = grad_call(
        d,
        unit_grad_kernel,
        "unit_grad1",
        late_kind,
        SPACE + TIME,
        ids,
        (a_mid, grad_s1, grad_q1, act1),
        [],
        [
            space_scratch(d, d.half),
            time_scratch(d, d.half),
            pltpu.VMEM((d.channels, d.cells), BF),
        ],
    )
    late_outs = [*late_first, *late_outs]
    grad_two, sums = call(
        join_back_kernel,
        "join_back",
        v_ins(ga_part, after(ga_other, *late_outs), q0, coef_two0, mask),
        [sds(narrow), sds((8, channels))],
        [],
        20 * 10**9,
        12,
    )
    late_both, late_sum = reduce_all(d, s, u, late_kind, late_outs, sums)

    terms = data_sums(sums, (late_both,))
    grad_q0, grad_one, sums, tot_two0 = time_back(
        0, grad_two, q0, coef_two0, terms, s0, coef_one0
    )
    _, time_outs0 = grad_call(
        d,
        time_grad_kernel,
        "time_grad0",
        early_kind,
        TIME,
        ids,
        (grad_q0, act0),
        [],
        [time_scratch(d, d.half)],
    )
    if d.pieces:
        time_outs0 = [*time_outs0[:2], *(swap(send, "u") for send in time_outs0[2:])]
    terms = data_sums(sums, time_outs0[2:], time_outs0[:2])
    (tot_one0,), space_outs0 = grad_call(
        d,
        last_space_grad_kernel,
        "space_grad0",
        early_kind,
        SPACE,
        ids,
        (*terms, x, grad_one, s0, coef_one0, count, mask),
        [sds((8, d.half))],
        [space_scratch(d, d.half)],
    )

    def head_steps(value):
        rows_all = jnp.concatenate([term[8:] for term in after(carried, value)], axis=0)
        rows_all = jnp.concatenate([rows_all, swap(rows_all, "u")], axis=0)
        rows_all = rows_all.reshape(-1, 8, channels)
        pooled_all = rows_all[:, :clips].reshape(-1, channels)
        logit_all = rows_all[:, clips : 2 * clips].reshape(-1, channels)
        loss_sum = jnp.sum(logit_all[:, classes])
        logit_all = logit_all[:, :classes]
        bias_grad = jnp.sum(logit_all, axis=0)
        base = d.row_base(yy, s, u, z)
        pooled_mine = lax.dynamic_slice_in_dim(pooled_all, base, rows, 1)
        head_grad = lax.dot_general(
            pooled_mine.astype(BF),
            logit_all.astype(BF),
            (((0,), (0,)), ((), ())),
            preferred_element_type=F32,
        )
        head_one, head_two, head_dir = adam_part(head_weight, head_grad, head_first, head_second, DECAY)
        bias_one, bias_two, bias_dir = adam_part(head_bias, bias_grad, bias_first, bias_second, 0.0)
        return (
            loss_sum, head_one, head_two, head_dir, square_rows(head_dir), bias_one, bias_two, bias_dir
        )

    late_sum = own_rows(d, s, *after((late_sum[0], late_sum[1]), *space_outs0))
    if d.pieces:
        early_sum, head_made = reduce_ring(
            d,
            [[*space_outs0[:2], *(swap(send, "u") for send in space_outs0[2:])], time_outs0],
            head_steps,
        )
    else:
        early_outs = [jnp.concatenate([space_outs0[0], time_outs0[0]], axis=0)]
        _, early_sum = reduce_all(d, s, u, early_kind, early_outs)
        head_made = head_steps(early_sum)
    loss_sum, head_one, head_two, head_dir, head_squares, bias_one, bias_two, bias_dir = head_made
    early_sum = whole_rows(own_rows(d, s, after(early_sum[0], *late_sum), early_sum[1]))
    late_sum = whole_rows(late_sum)

    ones = jnp.stack([tot_one0[:2], tot_one1[:2]])
    twos = jnp.stack([tot_two0[:2], tot_two1[:2]])
    small = jnp.concatenate([ones, twos], axis=-1)
    small = small + swap(small, "u")
    ones, twos = small[..., : d.half], small[..., d.half :]
    ones_other = swap(ones, "s")
    low, high = pick(s, ones, ones_other), pick(s, ones_other, ones)
    both = jnp.concatenate([low, high[..., : mid - d.half], twos], axis=-1)
    affine_grad = jnp.stack([both[:, 1], both[:, 0]], axis=1)

    def units(first, second):
        return jnp.stack([first, second]).transpose(2, 0, 1, 3)

    spatial_grad = units(early_sum[:SPACE], late_sum[:SPACE])
    temporal_grad = units(early_sum[SPACE:], late_sum[SPACE:])
    space_one, space_two, space_dir = adam_part(
        spatial_weight, spatial_grad, spatial_first, spatial_second, DECAY
    )
    time_one, time_two, time_dir = adam_part(
        temporal_weight, temporal_grad, temporal_first, temporal_second, DECAY
    )
    affine_one, affine_two, affine_dir = adam_part(
        affine, affine_grad, affine_first, affine_second, 0.0
    )
    dir_squares = [square_rows(v[:, l]) for v in (space_dir, time_dir) for l in range(2)]
    dir_squares.append(head_squares)
    padded = pl.pallas_call(
        squares_kernel,
        name="squares",
        out_shape=sds((8, LANES)),
        in_specs=[whole()] * 10,
        out_specs=whole(),
    )(*weight_squares, *dir_squares)
    native, by_tap = (Layout(major_to_minor=order) for order in ((0, 2, 1, 3), (1, 2, 0, 3)))
    moments = together(
        *(with_layout_constraint(v, by_tap) for v in (space_one, space_two, time_one, time_two))
    )
    moments = [with_layout_constraint(value, native) for value in moments]
    space_one, space_two, time_one, time_two = moments
    padded = padded + swap(padded, "u")
    padded = padded + after(swap(padded, "s"), affine_one, affine_two, affine_dir)
    terms = data_sums(padded, moments[1:3], (moments[0], moments[3]))
    terms = jnp.stack(terms)
    padded = sum(terms[lax.rem(z + (nz - place), nz)] for place in range(nz))
    norms = jnp.sqrt(padded[:2, :5])
    trust = norms[0] / norms[1]
    new_space = spatial_weight - RATE * trust[0:2][None, :, None, None] * space_dir
    new_time = temporal_weight - RATE * trust[2:4][None, :, None, None] * time_dir
    new_head = head_weight - RATE * trust[4] * head_dir
    new_affine = affine - RATE_SMALL * affine_dir
    new_bias = head_bias - RATE_SMALL * bias_dir
    return (
        loss_sum,
        space_one,
        space_two,
        new_space,
        time_one,
        time_two,
        new_time,
        head_one,
        head_two,
        new_head,
        affine_one,
        affine_two,
        new_affine,
        bias_one,
        bias_two,
        new_bias,
        norms,
    )


def solution(mesh):
    dp, tm = mesh.shape["dp"], mesh.shape["tm"]
    fine = Mesh(mesh.devices.reshape(dp // 4, 2, 2, tm), ALL)
    dp_axes = ("yy", "s", "u")
    owner = P(ALL)
    return jax.shard_map(
        on_device,
        mesh=fine,
        in_specs=(
            P(None, dp_axes, "tm"),
            P(None, dp_axes),
            P(None, dp_axes),
            owner,
            owner,
            owner,
            P(),
            P(),
            owner,
            owner,
            owner,
            owner,
            owner,
            owner,
            P(),
            P(),
            P(),
            P(),
        ),
        out_specs=(P(),) + (owner,) * 9 + (P(),) * 7,
        check_vma=False,
    )
```

```python
import functools

import jax
import jax.numpy as jnp
from jax import lax
from jax.experimental import pallas as pl
from jax.experimental.layout import Layout, with_layout_constraint
from jax.experimental.pallas import tpu as pltpu
from jax.sharding import Mesh
from jax.sharding import PartitionSpec as P

STEP = 5
EPS_NORM = 1e-05
EPS_ADAM = 1e-06
BETA_ONE = 0.5
BETA_TWO = 0.5
DECAY = 0.01
RATE = 0.3
RATE_SMALL = 0.1

F32 = jnp.float32
BF = jnp.bfloat16
LANES = 128
SPACE, TIME = 9, 3
ALL = ("yy", "s", "u", "tm")
DATA = ("yy", "tm")
MB = 1 << 20


def whole():
    return pl.BlockSpec(memory_space=pltpu.VMEM)


def in_hbm():
    return pl.BlockSpec(memory_space=pltpu.HBM)


def smem():
    return pl.BlockSpec(memory_space=pltpu.SMEM)


def dot(a, b):
    return jnp.dot(a, b, preferred_element_type=F32)


def dot_nt(a, b):
    return lax.dot_general(a, b, (((1,), (1,)), ((), ())), preferred_element_type=F32)


class Dims:
    def __init__(self, clips, frames, height, width, channels, mid, rows, ny, nz):
        self.clips, self.frames, self.height, self.width = clips, frames, height, width
        self.channels, self.mid, self.rows, self.ny, self.nz = channels, mid, rows, ny, nz
        self.line = width * clips
        self.plane = height * self.line
        self.cells = frames * self.plane
        tiles = mid // LANES
        self.half = (tiles + 1) // 2 * LANES
        self.groups = ny * nz
        self.pieces = rows % 16 == 0 and ny == 2

    def row_base(self, yy, s, u, z):
        return (((yy * 2 + s) * 2 + u) * self.nz + z) * self.rows


class Weight:
    def __init__(self, kind, arrays, first, taps):
        self.kind, self.arrays, self.first, self.taps = kind, arrays, first, taps

    def part(self, first, taps):
        return Weight(self.kind, self.arrays, self.first + first, taps)

    def copies_needed(self, d):
        return 1 if self.kind == "natural" else 4 * d.groups

    def natural(self, d):
        return sds((self.taps, d.channels, d.half), BF)

    def semaphores(self, d):
        return pltpu.SemaphoreType.DMA((self.copies_needed(d),))

    def places(self, d, ids):
        s, u, yy, z = (ids[i] for i in range(4))
        for urel in range(2):
            for i in range(d.groups):
                for srel in range(2):
                    if self.kind == "all":
                        row = d.row_base(i // d.nz, srel ^ s, urel, i % d.nz)
                        yield 0, (urel, i, srel), row
                        continue
                    if self.kind in ("blocks", "ring"):
                        yrel, k = i // d.nz, i % d.nz
                        row = d.row_base(
                            yrel ^ yy, srel ^ s, urel ^ u, lax.rem(z + (d.nz - k), d.nz)
                        )
                        if self.kind == "blocks":
                            yield urel * d.groups + i, (srel,), row
                        else:
                            yield urel * 2 + yrel, (k, srel), row
                    else:
                        row = d.row_base(i // d.nz, srel ^ s, urel ^ u, i % d.nz)
                        if urel == 0:
                            yield 0, (i, srel), row
                        else:
                            yield 1 + i // 2, (i % 2, srel), row

    def start(self, d, ids, refs, scratch, sems):
        taps = pl.ds(self.first, self.taps)
        copies = []
        if self.kind == "natural":
            copies.append(pltpu.make_async_copy(refs[0].at[taps], scratch, sems.at[0]))
        else:
            for operand, index, row in self.places(d, ids):
                copies.append(
                    pltpu.make_async_copy(
                        refs[operand].at[(*index, taps)],
                        scratch.at[:, pl.ds(pl.multiple_of(row, 16), d.rows), :],
                        sems.at[len(copies)],
                    )
                )
        for copy in copies:
            copy.start()
        return copies


def space_scratch(d, width):
    return pltpu.VMEM((d.frames, (d.height + 2) * d.line, 3 * width), BF)


def time_scratch(d, width):
    return pltpu.VMEM(((d.frames + 2) * d.plane, width), BF)


def fill_space(d, pad, values):
    cells, width = values.shape
    place = lax.broadcasted_iota(jnp.int32, (cells, width), 0)
    column = lax.rem(lax.div(place, d.clips), d.width)
    edge = jnp.zeros((d.frames, d.line, 3 * width), BF)
    pad[:, 0 : d.line, :] = edge
    pad[:, d.line + d.plane :, :] = edge
    left = jnp.where(column > 0, pltpu.roll(values, d.clips, 0), 0.0)
    right = jnp.where(column < d.width - 1, pltpu.roll(values, cells - d.clips, 0), 0.0)
    for j, moved in enumerate((left, values, right)):
        block = moved.astype(BF).reshape(d.frames, d.plane, width)
        pad[:, d.line : d.line + d.plane, j * width : (j + 1) * width] = block


def space_window(d, pad, i, j=None):
    rows = pl.ds(pl.multiple_of(i * d.line, d.line), d.plane)
    if j is None:
        block = pad[:, rows, :]
    else:
        width = pad.shape[-1] // 3
        block = pad[:, rows, pl.ds(pl.multiple_of(j * width, LANES), width)]
    return block.reshape(d.cells, block.shape[-1])


def fill_time(d, pad, values):
    width = values.shape[1]
    edge = jnp.zeros((d.plane, width), BF)
    pad[0 : d.plane, :] = edge
    pad[d.plane + d.cells :, :] = edge
    pad[d.plane : d.plane + d.cells, :] = values


def time_window(d, pad, k):
    return pad[pl.ds(pl.multiple_of(k * d.plane, d.plane), d.cells), :]


def sums_of(first, second, extra=None):
    width = first.shape[1]
    rows = [jnp.sum(first, axis=0, keepdims=True), jnp.sum(second, axis=0, keepdims=True)]
    if extra is not None:
        rows.append(extra)
    rows.append(jnp.zeros((8 - len(rows), width), F32))
    return jnp.concatenate(rows, axis=0)


def total_of(d, ids, terms):
    z = ids[3]
    values = [term[...] for term in terms]
    total = None
    for place in range(d.nz):
        here = values[0]
        for k in range(1, d.nz):
            here = jnp.where(lax.rem(z + (d.nz - k), d.nz) == place, values[k], here)
        total = here if total is None else total + here
    return total


def coefs_of(total, count, gains):
    average = total[0:1] / count
    scale = lax.rsqrt(total[1:2] / count - average * average + EPS_NORM)
    return jnp.concatenate(
        [
            average,
            scale,
            gains[0:2],
            jnp.broadcast_to(count, average.shape),
            jnp.zeros((3, total.shape[1]), F32),
        ],
        axis=0,
    )


def normed_of(values, coef):
    return (values - coef[0:1]) * coef[1:2]


def act_slope(pre):
    sigma = jax.nn.sigmoid(pre)
    return sigma * (1.0 + pre * (1.0 - sigma))


def norm_back(grad_pre, normed, coef, total, count, mask):
    scale = coef[2:3] * coef[1:2]
    return mask * (scale * (grad_pre - (total[0:1] + normed * total[1:2]) / count))


def conv_space_into(d, acc, pad, weight):
    for i in range(3):
        three = weight[3 * i : 3 * i + 3].reshape(3 * d.channels, d.half)
        part = dot(space_window(d, pad, i), three)
        acc[...] = part if i == 0 else acc[...] + part


def first_space_kernel(d, parts, *refs):
    ids, *refs = refs
    w_refs, refs = refs[: len(parts[0].arrays)], refs[len(parts[0].arrays) :]
    x, mask, s_out, sums_out, rest, weight, *sems, pad = refs
    copies = parts[0].start(d, ids, w_refs, weight, sems[0])
    later = parts[1].start(d, ids, w_refs, rest, sems[1])
    fill_space(d, pad, x[...].astype(F32))
    for copy in copies:
        copy.wait()
    conv_space_into(d, s_out, pad, weight)
    for copy in later:
        copy.wait()
    m = mask[...]
    values = s_out[...]
    count = jnp.sum(m, axis=0, keepdims=True) + jnp.zeros((1, d.half), F32)
    sums_out[...] = sums_of(values * m, values * values * m, count)


def second_space_kernel(d, parts, *refs):
    ids, *refs = refs
    w_refs, refs = refs[: len(parts[0].arrays)], refs[len(parts[0].arrays) :]
    terms, refs = refs[: d.nz], refs[d.nz :]
    q, count, gains, mask, a_out, coef_out, s_out, sums_out, weight, *rest, pad = refs
    rest, sems = rest[: len(parts) - 1], rest[len(parts) - 1 :]
    copies = parts[0].start(d, ids, w_refs, weight, sems[0])
    later = []
    for part, ref, sem in zip(parts[1:], rest, sems[1:]):
        later += part.start(d, ids, w_refs, ref, sem)
    m = mask[...]
    coef = coefs_of(total_of(d, ids, terms), count[4:5, 0:1], gains[...])
    coef_out[...] = coef
    pre = coef[2:3] * normed_of(q[...].astype(F32), coef) + coef[3:4]
    act = jax.nn.silu(pre) * m
    a_out[...] = act.astype(BF)
    fill_space(d, pad, act)
    for copy in copies:
        copy.wait()
    conv_space_into(d, s_out, pad, weight)
    for copy in later:
        copy.wait()
    values = s_out[...]
    sums_out[...] = sums_of(values * m, values * values * m)


def time_kernel(d, *refs):
    ids, weight, *refs = refs
    terms, refs = refs[: d.nz], refs[d.nz :]
    s, *counts, gains, mask, a_out, q_out, coef_out, pad = refs
    total = total_of(d, ids, terms)
    count = counts[0][4:5, 0:1] if counts else total[2:3, 0:1]
    coef = coefs_of(total, count, gains[...])
    coef_out[...] = coef
    pre = coef[2:3] * normed_of(s[...], coef) + coef[3:4]
    act = (jax.nn.silu(pre) * mask[...]).astype(BF)
    a_out[...] = act
    fill_time(d, pad, act)
    total = dot_nt(time_window(d, pad, 0), weight[0])
    for k in range(1, TIME):
        total = total + dot_nt(time_window(d, pad, k), weight[k])
    q_out[...] = total.astype(BF)


def join_kernel(qa, qb, mask, q_out, sums_out):
    total = (qa[...].astype(F32) + qb[...].astype(F32)).astype(BF)
    q_out[...] = total
    values = total.astype(F32)
    m = mask[...]
    sums_out[...] = sums_of(values * m, values * values * m)


def head_kernel(d, denominator, classes, *refs):
    ids, head, *refs = refs
    terms, refs = refs[: d.nz], refs[d.nz :]
    q, count, gains, mask, x, bias, clip_info, labels, *refs = refs
    coef_out, grad_out, sums_out = refs
    m = mask[...]
    coef = coefs_of(total_of(d, ids, terms), count[4:5, 0:1], gains[...])
    coef_out[...] = coef
    normed = normed_of(q[...].astype(F32), coef)
    pre = coef[2:3] * normed + coef[3:4] + x[...].astype(F32)
    sigma = jax.nn.sigmoid(pre)
    y = pre * sigma * m
    folded = jnp.sum(y.reshape(d.cells // 8, 8, d.channels), axis=0)
    step = d.clips
    total = folded
    for k in range(1, 8 // step):
        total = total + pltpu.roll(folded, k * step, 0)
    inverse = 1.0 / clip_info[:, 0:1]
    pooled = total * inverse
    pooled_bf = pooled.astype(BF)
    weight = head[0, :, : d.channels]
    logits = dot(pooled_bf, weight) + bias[...]
    largest = jnp.max(logits, axis=1, keepdims=True)
    shifted = jnp.exp(logits - largest)
    log_total = largest + jnp.log(jnp.sum(shifted, axis=1, keepdims=True))
    lane = lax.broadcasted_iota(jnp.int32, logits.shape, 1)
    onehot = jnp.where(lane == labels[:, 0:1], 1.0, 0.0)
    inside = lane < classes
    kept = jnp.where(inside, logits, 0.0)
    loss = log_total - jnp.sum(kept * onehot, axis=1, keepdims=True)
    grad_logits = jnp.where(inside, (jnp.exp(logits - log_total) - onehot) / denominator, 0.0)
    grad_pooled = dot_nt(grad_logits.astype(BF), weight) * inverse
    grad_y = jnp.broadcast_to(grad_pooled[None], (d.cells // 8, 8, d.channels)).reshape(
        d.cells, d.channels
    )
    grad_pre = grad_y * m * (sigma * (1.0 + pre * (1.0 - sigma)))
    grad_out[...] = grad_pre
    sums_out[0:8, :] = sums_of(grad_pre, grad_pre * normed)
    carried = jnp.where(lane == classes, loss, grad_logits)
    sums_out[8:16, :] = jnp.concatenate(
        [
            pooled_bf.astype(F32)[0 : d.clips],
            carried[0 : d.clips],
            jnp.zeros((8 - 2 * d.clips, d.channels), F32),
        ],
        axis=0,
    )


def time_back_kernel(d, *refs):
    ids, weight, *refs = refs
    terms, refs = refs[: d.nz], refs[d.nz :]
    grad_two, q, coef_two, count, mask, s, coef_one, *refs = refs
    gq_out, grad_out, sums_out, tot_out, pad = refs
    m = mask[...]
    total = total_of(d, ids, terms)
    tot_out[...] = total
    coef = coef_two[...]
    normed = normed_of(q[...].astype(F32), coef)
    grad_q = norm_back(grad_two[...], normed, coef, total, count[4:5, 0:1], m).astype(BF)
    gq_out[...] = grad_q
    fill_time(d, pad, grad_q)
    grad = dot(time_window(d, pad, TIME - 1), weight[0])
    for k in range(1, TIME):
        grad = grad + dot(time_window(d, pad, TIME - 1 - k), weight[k])
    grad = grad.astype(BF).astype(F32)
    coef = coef_one[...]
    normed = normed_of(s[...], coef)
    pre = coef[2:3] * normed + coef[3:4]
    grad_pre = grad * m * act_slope(pre)
    grad_out[...] = grad_pre
    sums_out[...] = sums_of(grad_pre, grad_pre * normed)


def space_back_kernel(d, *refs):
    ids, weight, *refs = refs
    terms, refs = refs[: d.nz], refs[d.nz :]
    grad_pre, s, coef_one, count, mask, *refs = refs
    gs_out, ga_out, tot_out, pad, acc = refs
    total = total_of(d, ids, terms)
    tot_out[...] = total
    coef = coef_one[...]
    normed = normed_of(s[...], coef)
    grad_s = norm_back(grad_pre[...], normed, coef, total, count[4:5, 0:1], mask[...])
    gs_out[...] = grad_s.astype(BF)
    fill_space(d, pad, grad_s)
    for i in range(3):
        part = sum(dot_nt(space_window(d, pad, 2 - i, 2 - j), weight[3 * i + j]) for j in range(3))
        acc[...] = part if i == 0 else acc[...] + part
    ga_out[...] = acc[...].astype(BF)


def join_back_kernel(ga, gb, q, coef_two, mask, grad_out, sums_out):
    coef = coef_two[...]
    normed = normed_of(q[...].astype(F32), coef)
    pre = coef[2:3] * normed + coef[3:4]
    grad = ga[...].astype(F32) + gb[...].astype(F32)
    grad_pre = grad * mask[...] * act_slope(pre)
    grad_out[...] = grad_pre
    sums_out[...] = sums_of(grad_pre, grad_pre * normed)


def write_grad(d, w, ids, value, outs, held):
    if w.kind == "natural":
        outs[0][0] = value.astype(BF)
        return
    held[...] = value.astype(BF)
    for operand, index, row in w.places(d, ids):
        block = held[pl.ds(pl.multiple_of(row, 16), d.rows), :]
        outs[operand][(*index, 0)] = block


def time_grad_kernel(d, w, *refs):
    ids, grad_q, act, *refs = refs
    outs, (pad, turned, held) = refs[:-3], refs[-3:]
    k = pl.program_id(0)

    @pl.when(k == 0)
    def _():
        fill_time(d, pad, act[...])
        turned[...] = jnp.transpose(grad_q[...].astype(F32)).astype(BF)

    write_grad(d, w, ids, dot(turned[...], time_window(d, pad, k)), outs, held)


def unit_grad_kernel(d, w, *refs):
    ids, a, grad_s, grad_q, act, *refs = refs
    outs, (pad, time_pad, time_turned, turned, held) = refs[:-5], refs[-5:]
    k = pl.program_id(0)

    @pl.when(k == 0)
    def _():
        fill_space(d, pad, grad_s[...].astype(F32))
        turned[...] = jnp.transpose(a[...].astype(F32)).astype(BF)
        fill_time(d, time_pad, act[...])
        time_turned[...] = jnp.transpose(grad_q[...].astype(F32)).astype(BF)

    @pl.when(k < SPACE)
    def _():
        window = space_window(d, pad, 2 - lax.div(k, 3), 2 - lax.rem(k, 3))
        write_grad(d, w, ids, dot(turned[...], window), outs, held)

    @pl.when(k >= SPACE)
    def _():
        window = time_window(d, time_pad, k - SPACE)
        write_grad(d, w, ids, dot(time_turned[...], window), outs, held)


def last_space_grad_kernel(d, w, *refs):
    ids, *refs = refs
    terms, refs = refs[: d.nz], refs[d.nz :]
    a, grad_pre, s, coef_one, count, mask, tot_out, *refs = refs
    outs, (pad, turned, held) = refs[:-3], refs[-3:]
    k = pl.program_id(0)

    @pl.when(k == 0)
    def _():
        total = total_of(d, ids, terms)
        tot_out[...] = total
        coef = coef_one[...]
        normed = normed_of(s[...], coef)
        grad_s = norm_back(grad_pre[...], normed, coef, total, count[4:5, 0:1], mask[...])
        fill_space(d, pad, grad_s)
        turned[...] = jnp.transpose(a[...].astype(F32)).astype(BF)

    window = space_window(d, pad, 2 - lax.div(k, 3), 2 - lax.rem(k, 3))
    write_grad(d, w, ids, dot(turned[...], window), outs, held)


def squares_kernel(*refs):
    *values, out = refs
    row = lax.broadcasted_iota(jnp.int32, (8, LANES), 0)
    lane = lax.broadcasted_iota(jnp.int32, (8, LANES), 1)
    total = jnp.zeros((8, LANES), F32)
    for i, value in enumerate(values):
        here = (row == i // 5) & (lane == i % 5)
        lanes = jnp.sum(value[...], axis=0, keepdims=True)
        total = jnp.where(here, jnp.sum(lanes, axis=1, keepdims=True), total)
    out[...] = total


def sds(shape, dtype=F32):
    return jax.ShapeDtypeStruct(shape, dtype)


def call(body, name, ins, outs, scratch, flops, megabytes=24):
    return pl.pallas_call(
        body,
        name=name,
        out_shape=outs,
        in_specs=[spec for spec, _ in ins],
        out_specs=[whole()] * len(outs),
        scratch_shapes=scratch,
        compiler_params=pltpu.CompilerParams(vmem_limit_bytes=megabytes * MB),
        cost_estimate=pl.CostEstimate(flops=flops, bytes_accessed=8 * MB, transcendentals=0),
    )(*[value for _, value in ins])


def w_ins(weight):
    return [
        (in_hbm(), pltpu.with_memory_space_constraint(piece, pltpu.HBM))
        for piece in weight.arrays
    ]


def v_ins(*values):
    return [(whole(), value) for value in values]


def grad_call(d, body, name, kind, taps, ids, values, first_outs, scratch):
    if kind == "ring":
        shape, count = (d.nz, 2, taps, d.rows, d.half), 4
        spec = pl.BlockSpec((d.nz, 2, 1, d.rows, d.half), lambda k: (0, 0, k, 0, 0))
    elif kind == "parts":
        shape, count = (2, 2, taps, d.rows, d.half), d.groups // 2
        spec = pl.BlockSpec((2, 2, 1, d.rows, d.half), lambda k: (0, 0, k, 0, 0))
        first_outs = [*first_outs, sds((d.groups, *shape[1:]), BF)]
    else:
        shape, count = (taps, d.channels, d.half), 1
        spec = pl.BlockSpec((1, d.channels, d.half), lambda k: (k, 0, 0))
    fixed = [pl.BlockSpec(out.shape, lambda k: (0, 0)) for out in first_outs]
    if kind == "parts":
        fixed[-1] = pl.BlockSpec((d.groups, 2, 1, d.rows, d.half), lambda k: (0, 0, k, 0, 0))
    outs = pl.pallas_call(
        functools.partial(body, d, Weight(kind, (), 0, 1)),
        name=name,
        grid=(taps,),
        out_shape=list(first_outs) + [sds(shape, BF)] * count,
        in_specs=[smem()] + [whole()] * len(values),
        out_specs=fixed + [spec] * count,
        scratch_shapes=scratch
        + [pltpu.VMEM((d.channels, d.cells), BF), pltpu.VMEM((d.channels, d.half), BF)],
        compiler_params=pltpu.CompilerParams(vmem_limit_bytes=24 * MB),
        cost_estimate=pl.CostEstimate(flops=1, bytes_accessed=1, transcendentals=0),
    )(ids, *values)
    return outs[: len(first_outs)], outs[len(first_outs) :]


def swap(value, axis, distance=1):
    size = lax.axis_size(axis)
    return lax.ppermute(value, axis, [(i, i ^ distance) for i in range(size)])


def across_yy(values, *besides):
    size = lax.axis_size("yy")
    distance = 1
    while distance < size:
        other = swap(values, "yy", distance)
        distance *= 2
        values = values + (after(other, *besides) if distance >= size else other)
    return values


def around_tm(values):
    size = lax.axis_size("tm")
    return [values] + [
        lax.ppermute(values, "tm", [(i, (i + k) % size) for i in range(size)])
        for k in range(1, size)
    ]


def data_sums(values, last=(), first=()):
    terms = around_tm(across_yy(values, *first))
    return [after(term, *last) if k == len(terms) - 1 else term for k, term in enumerate(terms)]


def data_sums_gather(values):
    distance = 1
    while distance < lax.axis_size("yy"):
        other = swap(values, "yy", distance)
        values = jnp.concatenate([values[:8] + other[:8], values[8:], other[8:]], axis=0)
        distance *= 2
    terms = around_tm(values)
    return [term[:8] for term in terms], terms


def pick(index, first, second):
    return jnp.where(index == 0, first, second)


def after(value, *earlier):
    if not earlier:
        return value
    return lax.optimization_barrier((value, *earlier))[0]


def turn(value):
    size = lax.axis_size("tm")
    return lax.ppermute(value, "tm", [(i, (i + 1) % size) for i in range(size)])


def together(*values):
    return lax.optimization_barrier(values)


def gather_ring(both, besides):
    held, across, made = [both], [], []
    for beside in besides:
        moves = [swap(held[-1], "yy")]
        if len(held) < lax.axis_size("tm"):
            moves.append(turn(held[-1]))
        extra = beside(held[-1], made[-1] if made else None)
        results = together(*moves, *extra)
        across.append(results[0])
        held += results[1 : len(moves)]
        made.append(results[len(moves) :])
    own = held + across
    return Weight("blocks", own + [swap(block, "u") for block in own], 0, both.shape[1]), made


def gather_all(d, s, both, *earlier):
    gathered = lax.all_gather(both, ("u",) + DATA, axis=0, tiled=False)
    gathered = after(gathered, *earlier).reshape(2, d.groups, *both.shape)
    taps = both.shape[1]
    if d.pieces:
        return Weight("all", (gathered,), 0, taps)
    parts = gathered.reshape(2, d.ny, d.nz, 2, taps, d.rows, d.half)
    parts = jnp.where(s == 0, parts, parts[:, :, :, ::-1])
    natural = parts.transpose(4, 1, 3, 0, 2, 5, 6).reshape(taps, d.channels, d.half)
    return Weight("natural", (natural,), 0, taps)


def added(*values):
    total = values[0].astype(F32)
    for value in values[1:]:
        total = total + value.astype(F32)
    return total.astype(BF)


def reduce_ring(d, gradients, beside):
    def joined(yrel, k, *others, second=None):
        parts = [outs[yrel][k].astype(F32) + outs[2 + yrel][k].astype(F32) for outs in gradients]
        total = jnp.concatenate(parts, axis=1)
        for other in others:
            total = total + other.astype(F32)
        if second is not None:
            total = jnp.stack([total[0], total[1] + second.astype(F32)])
        return total.astype(BF)

    first = joined(1, 1)
    by_y, by_z = swap(first[0], "yy"), turn(first[1])
    moving = joined(0, 1)
    moving = jnp.stack([added(moving[0], by_y), moving[1]])
    for k in list(range(2, d.nz)) + [0]:
        across = swap(joined(1, k, second=by_z if k == 2 else None), "yy")
        turned = turn(moving)
        if k == 3:
            turned, *made = together(turned, *beside(moving))
        moving = joined(0, k, across, turned)
    return moving, made


def reduce_all(d, s, u, kind, outs, *earlier):
    if kind == "parts":
        keep, *sends = outs
        theirs = [swap(send, "u") for send in sends]
    else:
        (natural,) = outs
        taps = natural.shape[0]
        parts = natural.reshape(taps, d.ny, 2, 2, d.nz, d.rows, d.half)
        parts = parts.transpose(3, 1, 4, 2, 0, 5, 6)
        parts = jnp.where(u == 0, parts, parts[::-1])
        parts = jnp.where(s == 0, parts, parts[:, :, :, ::-1])
        keep, send = parts.reshape(2, d.groups, 2, taps, d.rows, d.half)
        theirs = [swap(send, "u")]
    keep, theirs = after((keep, theirs), *earlier)
    both = added(keep, jnp.concatenate(theirs, axis=0))
    return both, lax.psum_scatter(both, DATA, scatter_dimension=0, tiled=False)


def own_rows(d, s, mine, theirs):
    other = swap(theirs, "s")
    return pick(s, mine, other), pick(s, other, mine)[..., : d.mid - d.half]


def whole_rows(halves_of_rows):
    return jnp.concatenate(halves_of_rows, axis=-1).astype(F32)


def halves(d, values):
    fill = [(0, 0)] * (values.ndim - 1) + [(0, 2 * d.half - d.mid)]
    return values[..., : d.half], jnp.pad(values[..., d.half :], fill)


def rows_of(gain, shift):
    return jnp.concatenate(
        [gain[None], shift[None], jnp.zeros((6, gain.shape[0]), F32)], axis=0
    )


def square_rows(values):
    return jnp.sum(values * values, axis=tuple(range(1, values.ndim - 1)))


def adam_part(weight, gradient, moment_one, moment_two, decay):
    new_one = BETA_ONE * moment_one + (1.0 - BETA_ONE) * gradient
    new_two = BETA_TWO * moment_two + (1.0 - BETA_TWO) * gradient * gradient
    direction = (
        new_one / (1.0 - BETA_ONE**STEP) / (jnp.sqrt(new_two / (1.0 - BETA_TWO**STEP)) + EPS_ADAM)
        + decay * weight
    )
    return (new_one, new_two, direction)


def on_device(
    clips_x,
    frames,
    labels,
    spatial_weight,
    temporal_weight,
    head_weight,
    affine,
    head_bias,
    spatial_first,
    spatial_second,
    temporal_first,
    temporal_second,
    head_first,
    head_second,
    affine_first,
    affine_second,
    bias_first,
    bias_second,
):
    s, u, z, yy = (lax.axis_index(axis) for axis in ("s", "u", "tm", "yy"))
    ny, nz = lax.axis_size("yy"), lax.axis_size("tm")
    micro, clips, _, height, width, channels = clips_x.shape
    mid = spatial_weight.shape[3]
    rows = spatial_weight.shape[0]
    classes = head_weight.shape[1]
    d = Dims(clips, nz, height, width, channels, mid, rows, ny, nz)
    assert nz == 4 and micro == 2
    ids = jnp.stack([s, u, yy, z]).astype(jnp.int32)
    denominator = micro * clips * 4 * ny

    def prepared(weight, l):
        return halves(d, weight[:, l].astype(BF).transpose(1, 0, 2))

    def paired(parts, *earlier):
        first = jnp.concatenate([part[0] for part in parts], axis=0)
        second = jnp.concatenate([part[1] for part in parts], axis=0)
        send = after(pick(s, second, first), *earlier)
        return jnp.stack([pick(s, first, second), swap(send, "s")])

    def by_index(index, mine, other):
        return jnp.stack([pick(index, mine, other), pick(index, other, mine)])

    pairs = []
    for value in (clips_x, jnp.stack([frames, labels]).transpose(1, 0, 2)):
        kept = pick(u, value[0], value[1])
        pairs.append(by_index(u, kept, swap(pick(u, value[1], value[0]), "u")))
    early = paired([prepared(spatial_weight, 0), prepared(temporal_weight, 0)])

    def beside_first(*_):
        four, info = (by_index(s, pair, swap(pair, "s")) for pair in pairs)
        return four.reshape(nz, clips, height * width, channels), info

    def clips_home(four):
        return lax.all_to_all(four, "tm", split_axis=0, concat_axis=0, tiled=True)

    def beside_second(block, first):
        weights = after((spatial_weight, temporal_weight, head_weight), block)
        slot = jnp.pad(weights[2].astype(BF), ((0, 0), (0, d.half - classes)))[None]
        parts = [prepared(weights[0], 1), prepared(weights[1], 1), (slot, slot)]
        return [paired(parts), clips_home(first[0])]

    def beside_third(block, _):
        weights = after((spatial_weight, temporal_weight, head_weight), block)
        gains, bias = after((affine, head_bias), block)
        bias_row = jnp.full((1, channels), -1e30, F32).at[0, :classes].set(bias)
        rows_one, rows_two = [], []
        for l in range(2):
            low, high = halves(d, gains[l, :, :mid])
            mine = pick(s, low, high)
            rows_one.append(rows_of(mine[0], mine[1]))
            rows_two.append(rows_of(gains[l, 0, mid:], gains[l, 1, mid:]))
        squares = [square_rows(weight[:, l]) for weight in weights[:2] for l in range(2)]
        return [bias_row, *rows_one, *rows_two, *squares, square_rows(weights[2])]

    if d.pieces:
        early_w, made = gather_ring(
            early, [beside_first, beside_second, beside_third, lambda *_: []]
        )
        (_, info_four), (late, clip_all), small, _ = made
    else:
        early_w = gather_all(d, s, early)
        first = beside_first()
        info_four = first[1]
        (late, clip_all), small = beside_second(early, first), beside_third(early, None)
    bias_row, *small = small
    gains_one, gains_two, weight_squares = small[:2], small[2:4], small[4:]

    x = clip_all.reshape(nz, clips, height * width, channels)
    x = x.transpose(0, 2, 1, 3).reshape(d.cells, channels)

    mine_info = lax.dynamic_index_in_dim(
        info_four.reshape(nz, 2, clips), z, 0, keepdims=False
    )
    my_frames, my_labels = mine_info[0], mine_info[1]
    valid = (jnp.arange(nz, dtype=jnp.int32)[:, None] * 8 < my_frames[None, :]).astype(F32)
    mask = jnp.broadcast_to(valid[:, None, :], (nz, height * width, clips)).reshape(d.cells, 1)
    divisor = (my_frames // 8).astype(F32) * (height * width)
    clip_info = jnp.broadcast_to(jnp.tile(divisor, 8 // clips)[:, None], (8, LANES))
    label_rows = jnp.broadcast_to(jnp.tile(my_labels, 8 // clips)[:, None], (8, LANES))
    x, mask, clip_info, label_rows = together(x, mask, clip_info, label_rows)

    wide, narrow = (d.cells, d.half), (d.cells, channels)
    space_flops = 2 * d.cells * SPACE * channels * d.half
    time_flops = 2 * d.cells * TIME * channels * d.half

    def first_space(weight):
        parts = [weight.part(0, SPACE), weight.part(SPACE, TIME)]
        return call(
            functools.partial(first_space_kernel, d, parts),
            "space0",
            [(smem(), ids)] + w_ins(weight) + v_ins(x, mask),
            [sds(wide), sds((8, d.half)), parts[1].natural(d)],
            [pltpu.VMEM(parts[0].natural(d).shape, BF)]
            + [part.semaphores(d) for part in parts]
            + [space_scratch(d, channels)],
            space_flops,
        )

    def next_space(weight, q, terms, count):
        sizes = (SPACE, TIME, 1)
        parts = [weight.part(sum(sizes[:i]), size) for i, size in enumerate(sizes)]
        return call(
            functools.partial(second_space_kernel, d, parts),
            "space1",
            [(smem(), ids)] + w_ins(weight) + v_ins(*terms, q, count, gains_two[0], mask),
            [sds(narrow, BF), sds((8, channels)), sds(wide), sds((8, d.half))]
            + [part.natural(d) for part in parts],
            [part.semaphores(d) for part in parts] + [space_scratch(d, channels)],
            space_flops,
        )

    def time_next(l, s_value, terms, *count):
        return call(
            functools.partial(time_kernel, d),
            f"time{l}",
            [(smem(), ids)] + v_ins(time_w[l], *terms, s_value, *count, gains_one[l], mask),
            [sds(wide, BF), sds(narrow, BF), sds((8, d.half))],
            [time_scratch(d, d.half)],
            time_flops,
        )

    def joined(q_part):
        return call(
            join_kernel,
            "join",
            v_ins(q_part, swap(q_part, "s"), mask),
            [sds(narrow, BF), sds((8, channels))],
            [],
            d.cells * channels,
            12,
        )

    s0, sums, time_first = first_space(early_w)
    time_w = [time_first, None]
    terms = data_sums(sums)
    act0, q_part, coef_one0 = time_next(0, s0, terms)
    count = coef_one0
    q0, sums = joined(q_part)
    terms = data_sums(sums)
    late_w = gather_all(d, s, late, terms[0])
    a_mid, coef_two0, s1, sums, space_w, time_w[1], head_w = next_space(late_w, q0, terms, count)
    terms = data_sums(sums)
    act1, q_part, coef_one1 = time_next(1, s1, terms, count)
    q1, sums = joined(q_part)
    terms = data_sums(sums)
    coef_two1, grad_two, sums = call(
        functools.partial(head_kernel, d, float(denominator), classes),
        "head",
        [(smem(), ids)]
        + v_ins(head_w, *terms, q1, count, gains_two[1], mask, x, bias_row, clip_info, label_rows),
        [sds((8, channels)), sds(narrow), sds((16, channels))],
        [],
        4 * d.cells * channels,
    )
    terms, carried = data_sums_gather(sums)

    def time_back(l, grad, q, coef_two, terms, s_value, coef_one):
        return call(
            functools.partial(time_back_kernel, d),
            f"time_back{l}",
            [(smem(), ids)]
            + v_ins(time_w[l], *terms, grad, q, coef_two, count, mask, s_value, coef_one),
            [sds(narrow, BF), sds(wide), sds((8, d.half)), sds((8, channels))],
            [time_scratch(d, channels)],
            time_flops,
        )

    late_kind = "parts" if d.pieces else "natural"
    early_kind = "ring" if d.pieces else "natural"

    grad_q1, grad_one, sums, tot_two1 = time_back(
        1, grad_two, q1, coef_two1, terms, s1, coef_one1
    )
    terms = data_sums(sums)
    grad_s1, ga_part, tot_one1 = call(
        functools.partial(space_back_kernel, d),
        "space_back",
        [(smem(), ids)] + v_ins(space_w, *terms, grad_one, s1, coef_one1, count, mask),
        [sds(wide, BF), sds(narrow, BF), sds((8, d.half))],
        [space_scratch(d, d.half), pltpu.VMEM((d.cells, channels), F32)],
        space_flops,
    )
    ga_other = swap(ga_part, "s")
    late_first, late_outs = grad_call(
        d,
        unit_grad_kernel,
        "unit_grad1",
        late_kind,
        SPACE + TIME,
        ids,
        (a_mid, grad_s1, grad_q1, act1),
        [],
        [
            space_scratch(d, d.half),
            time_scratch(d, d.half),
            pltpu.VMEM((d.channels, d.cells), BF),
        ],
    )
    late_outs = [*late_first, *late_outs]
    grad_two, sums = call(
        join_back_kernel,
        "join_back",
        v_ins(ga_part, after(ga_other, *late_outs), q0, coef_two0, mask),
        [sds(narrow), sds((8, channels))],
        [],
        20 * 10**9,
        12,
    )
    late_both, late_sum = reduce_all(d, s, u, late_kind, late_outs, sums)

    terms = data_sums(sums, (late_both,))
    grad_q0, grad_one, sums, tot_two0 = time_back(
        0, grad_two, q0, coef_two0, terms, s0, coef_one0
    )
    _, time_outs0 = grad_call(
        d,
        time_grad_kernel,
        "time_grad0",
        early_kind,
        TIME,
        ids,
        (grad_q0, act0),
        [],
        [time_scratch(d, d.half)],
    )
    if d.pieces:
        time_outs0 = [*time_outs0[:2], *(swap(send, "u") for send in time_outs0[2:])]
    terms = data_sums(sums, time_outs0[2:], time_outs0[:2])
    (tot_one0,), space_outs0 = grad_call(
        d,
        last_space_grad_kernel,
        "space_grad0",
        early_kind,
        SPACE,
        ids,
        (*terms, x, grad_one, s0, coef_one0, count, mask),
        [sds((8, d.half))],
        [space_scratch(d, d.half)],
    )

    def head_steps(value):
        rows_all = jnp.concatenate([term[8:] for term in after(carried, value)], axis=0)
        rows_all = jnp.concatenate([rows_all, swap(rows_all, "u")], axis=0)
        rows_all = rows_all.reshape(-1, 8, channels)
        pooled_all = rows_all[:, :clips].reshape(-1, channels)
        logit_all = rows_all[:, clips : 2 * clips].reshape(-1, channels)
        loss_sum = jnp.sum(logit_all[:, classes])
        logit_all = logit_all[:, :classes]
        bias_grad = jnp.sum(logit_all, axis=0)
        base = d.row_base(yy, s, u, z)
        pooled_mine = lax.dynamic_slice_in_dim(pooled_all, base, rows, 1)
        head_grad = lax.dot_general(
            pooled_mine.astype(BF),
            logit_all.astype(BF),
            (((0,), (0,)), ((), ())),
            preferred_element_type=F32,
        )
        head_one, head_two, head_dir = adam_part(head_weight, head_grad, head_first, head_second, DECAY)
        bias_one, bias_two, bias_dir = adam_part(head_bias, bias_grad, bias_first, bias_second, 0.0)
        return (
            loss_sum, head_one, head_two, head_dir, square_rows(head_dir), bias_one, bias_two, bias_dir
        )

    late_sum = own_rows(d, s, *after((late_sum[0], late_sum[1]), *space_outs0))
    if d.pieces:
        early_sum, head_made = reduce_ring(
            d,
            [[*space_outs0[:2], *(swap(send, "u") for send in space_outs0[2:])], time_outs0],
            head_steps,
        )
    else:
        early_outs = [jnp.concatenate([space_outs0[0], time_outs0[0]], axis=0)]
        _, early_sum = reduce_all(d, s, u, early_kind, early_outs)
        head_made = head_steps(early_sum)
    loss_sum, head_one, head_two, head_dir, head_squares, bias_one, bias_two, bias_dir = head_made
    early_sum = whole_rows(own_rows(d, s, after(early_sum[0], *late_sum), early_sum[1]))
    late_sum = whole_rows(late_sum)

    ones = jnp.stack([tot_one0[:2], tot_one1[:2]])
    twos = jnp.stack([tot_two0[:2], tot_two1[:2]])
    small = jnp.concatenate([ones, twos], axis=-1)
    small = small + swap(small, "u")
    ones, twos = small[..., : d.half], small[..., d.half :]
    ones_other = swap(ones, "s")
    low, high = pick(s, ones, ones_other), pick(s, ones_other, ones)
    both = jnp.concatenate([low, high[..., : mid - d.half], twos], axis=-1)
    affine_grad = jnp.stack([both[:, 1], both[:, 0]], axis=1)

    def units(first, second):
        return jnp.stack([first, second]).transpose(2, 0, 1, 3)

    spatial_grad = units(early_sum[:SPACE], late_sum[:SPACE])
    temporal_grad = units(early_sum[SPACE:], late_sum[SPACE:])
    space_one, space_two, space_dir = adam_part(
        spatial_weight, spatial_grad, spatial_first, spatial_second, DECAY
    )
    time_one, time_two, time_dir = adam_part(
        temporal_weight, temporal_grad, temporal_first, temporal_second, DECAY
    )
    affine_one, affine_two, affine_dir = adam_part(
        affine, affine_grad, affine_first, affine_second, 0.0
    )
    dir_squares = [square_rows(v[:, l]) for v in (space_dir, time_dir) for l in range(2)]
    dir_squares.append(head_squares)
    padded = pl.pallas_call(
        squares_kernel,
        name="squares",
        out_shape=sds((8, LANES)),
        in_specs=[whole()] * 10,
        out_specs=whole(),
    )(*weight_squares, *dir_squares)
    native, by_tap = (Layout(major_to_minor=order) for order in ((0, 2, 1, 3), (1, 2, 0, 3)))
    moments = together(
        *(with_layout_constraint(v, by_tap) for v in (space_one, space_two, time_one, time_two))
    )
    moments = [with_layout_constraint(value, native) for value in moments]
    space_one, space_two, time_one, time_two = moments
    padded = padded + swap(padded, "u")
    padded = padded + after(swap(padded, "s"), affine_one, affine_two, affine_dir)
    terms = data_sums(padded, moments[1:3], (moments[0], moments[3]))
    terms = jnp.stack(terms)
    padded = sum(terms[lax.rem(z + (nz - place), nz)] for place in range(nz))
    norms = jnp.sqrt(padded[:2, :5])
    trust = norms[0] / norms[1]
    new_space = spatial_weight - RATE * trust[0:2][None, :, None, None] * space_dir
    new_time = temporal_weight - RATE * trust[2:4][None, :, None, None] * time_dir
    new_head = head_weight - RATE * trust[4] * head_dir
    new_affine = affine - RATE_SMALL * affine_dir
    new_bias = head_bias - RATE_SMALL * bias_dir
    return (
        loss_sum,
        space_one,
        space_two,
        new_space,
        time_one,
        time_two,
        new_time,
        head_one,
        head_two,
        new_head,
        affine_one,
        affine_two,
        new_affine,
        bias_one,
        bias_two,
        new_bias,
        norms,
    )


def solution(mesh):
    dp, tm = mesh.shape["dp"], mesh.shape["tm"]
    fine = Mesh(mesh.devices.reshape(dp // 4, 2, 2, tm), ALL)
    dp_axes = ("yy", "s", "u")
    owner = P(ALL)
    return jax.shard_map(
        on_device,
        mesh=fine,
        in_specs=(
            P(None, dp_axes, "tm"),
            P(None, dp_axes),
            P(None, dp_axes),
            owner,
            owner,
            owner,
            P(),
            P(),
            owner,
            owner,
            owner,
            owner,
            owner,
            owner,
            P(),
            P(),
            P(),
            P(),
        ),
        out_specs=(P(),) + (owner,) * 9 + (P(),) * 7,
        check_vma=False,
    )
```

```python
import functools

import jax
import jax.numpy as jnp
from jax import lax
from jax.experimental import pallas as pl
from jax.experimental.layout import Layout, with_layout_constraint
from jax.experimental.pallas import tpu as pltpu
from jax.sharding import Mesh
from jax.sharding import PartitionSpec as P

STEP = 5
EPS_NORM = 1e-05
EPS_ADAM = 1e-06
BETA_ONE = 0.5
BETA_TWO = 0.5
DECAY = 0.01
RATE = 0.3
RATE_SMALL = 0.1

F32 = jnp.float32
BF = jnp.bfloat16
LANES = 128
SPACE, TIME = 9, 3
ALL = ("yy", "s", "u", "tm")
DATA = ("yy", "tm")
MB = 1 << 20


def whole():
    return pl.BlockSpec(memory_space=pltpu.VMEM)


def in_hbm():
    return pl.BlockSpec(memory_space=pltpu.HBM)


def smem():
    return pl.BlockSpec(memory_space=pltpu.SMEM)


def dot(a, b):
    return jnp.dot(a, b, preferred_element_type=F32)


def dot_nt(a, b):
    return lax.dot_general(a, b, (((1,), (1,)), ((), ())), preferred_element_type=F32)


class Dims:
    def __init__(self, clips, frames, height, width, channels, mid, rows, ny, nz):
        self.clips, self.frames, self.height, self.width = clips, frames, height, width
        self.channels, self.mid, self.rows, self.ny, self.nz = channels, mid, rows, ny, nz
        self.line = width * clips
        self.plane = height * self.line
        self.cells = frames * self.plane
        tiles = mid // LANES
        assert tiles % 2 == 1
        self.main = tiles // 2 * LANES
        self.half = self.main + LANES
        self.groups = ny * nz
        self.pieces = rows % 16 == 0 and ny == 2

    def row_base(self, yy, s, u, z):
        return (((yy * 2 + s) * 2 + u) * self.nz + z) * self.rows


class Weight:
    def __init__(self, kind, arrays, first, taps):
        self.kind, self.arrays, self.first, self.taps = kind, arrays, first, taps

    def part(self, first, taps):
        return Weight(self.kind, self.arrays, self.first + first, taps)

    def copies_needed(self, d):
        return 1 if self.kind == "natural" else 4 * d.groups

    def natural(self, d):
        return sds((self.taps, d.channels, self.arrays[0].shape[-1]), BF)

    def semaphores(self, d):
        return pltpu.SemaphoreType.DMA((self.copies_needed(d),))

    def places(self, d, ids):
        s, u, yy, z = (ids[i] for i in range(4))
        for urel in range(2):
            for i in range(d.groups):
                for srel in range(2):
                    if self.kind == "all":
                        row = d.row_base(i // d.nz, srel ^ s, urel, i % d.nz)
                        yield 0, (urel, i, srel), row
                        continue
                    if self.kind in ("blocks", "ring"):
                        yrel, k = i // d.nz, i % d.nz
                        row = d.row_base(
                            yrel ^ yy, srel ^ s, urel ^ u, lax.rem(z + (d.nz - k), d.nz)
                        )
                        if self.kind == "blocks":
                            yield urel * d.groups + i, (srel,), row
                        else:
                            yield urel * 2 + yrel, (k, srel), row
                    else:
                        row = d.row_base(i // d.nz, srel ^ s, urel ^ u, i % d.nz)
                        if urel == 0:
                            yield 0, (i, srel), row
                        else:
                            yield 1 + i // 2, (i % 2, srel), row

    def start(self, d, ids, refs, scratch, sems):
        taps = pl.ds(self.first, self.taps)
        copies = []
        if self.kind == "natural":
            copies.append(pltpu.make_async_copy(refs[0].at[taps], scratch, sems.at[0]))
        else:
            for operand, index, row in self.places(d, ids):
                copies.append(
                    pltpu.make_async_copy(
                        refs[operand].at[(*index, taps)],
                        scratch.at[:, pl.ds(pl.multiple_of(row, 16), d.rows), :],
                        sems.at[len(copies)],
                    )
                )
        for copy in copies:
            copy.start()
        return copies


def space_scratch(d, width):
    return pltpu.VMEM((d.frames, (d.height + 2) * d.line, 3 * width), BF)


def time_scratch(d, width):
    return pltpu.VMEM(((d.frames + 2) * d.plane, width), BF)


def fill_space(d, pad, values):
    cells, width = values.shape
    place = lax.broadcasted_iota(jnp.int32, (cells, width), 0)
    column = lax.rem(lax.div(place, d.clips), d.width)
    edge = jnp.zeros((d.frames, d.line, 3 * width), BF)
    pad[:, 0 : d.line, :] = edge
    pad[:, d.line + d.plane :, :] = edge
    left = jnp.where(column > 0, pltpu.roll(values, d.clips, 0), 0.0)
    right = jnp.where(column < d.width - 1, pltpu.roll(values, cells - d.clips, 0), 0.0)
    for j, moved in enumerate((left, values, right)):
        block = moved.astype(BF).reshape(d.frames, d.plane, width)
        pad[:, d.line : d.line + d.plane, j * width : (j + 1) * width] = block


def space_window(d, pad, i, j=None):
    rows = pl.ds(pl.multiple_of(i * d.line, d.line), d.plane)
    if j is None:
        block = pad[:, rows, :]
    else:
        width = pad.shape[-1] // 3
        block = pad[:, rows, pl.ds(pl.multiple_of(j * width, LANES), width)]
    return block.reshape(d.cells, block.shape[-1])


def fill_time(d, pad, values):
    width = values.shape[1]
    edge = jnp.zeros((d.plane, width), BF)
    pad[0 : d.plane, :] = edge
    pad[d.plane + d.cells :, :] = edge
    pad[d.plane : d.plane + d.cells, :] = values


def time_window(d, pad, k):
    return pad[pl.ds(pl.multiple_of(k * d.plane, d.plane), d.cells), :]


def sums_of(first, second, extra=None):
    width = first.shape[1]
    rows = [jnp.sum(first, axis=0, keepdims=True), jnp.sum(second, axis=0, keepdims=True)]
    if extra is not None:
        rows.append(extra)
    rows.append(jnp.zeros((8 - len(rows), width), F32))
    return jnp.concatenate(rows, axis=0)


def total_of(d, ids, terms):
    z = ids[3]
    values = [term[...] for term in terms]
    total = None
    for place in range(d.nz):
        here = values[0]
        for k in range(1, d.nz):
            here = jnp.where(lax.rem(z + (d.nz - k), d.nz) == place, values[k], here)
        total = here if total is None else total + here
    return total


def coefs_of(total, count, gains):
    average = total[0:1] / count
    scale = lax.rsqrt(total[1:2] / count - average * average + EPS_NORM)
    return jnp.concatenate(
        [
            average,
            scale,
            gains[0:2],
            jnp.broadcast_to(count, average.shape),
            jnp.zeros((3, total.shape[1]), F32),
        ],
        axis=0,
    )


def normed_of(values, coef):
    return (values - coef[0:1]) * coef[1:2]


def act_slope(pre):
    sigma = jax.nn.sigmoid(pre)
    return sigma * (1.0 + pre * (1.0 - sigma))


def norm_back(grad_pre, normed, coef, total, count, mask):
    scale = coef[2:3] * coef[1:2]
    return mask * (scale * (grad_pre - (total[0:1] + normed * total[1:2]) / count))


class Taps:
    def __init__(self, main, middle=None, first=0):
        self.main, self.middle, self.first = main, middle, first

    def get(self, k, count=1):
        def rows(ref, k):
            block = ref[k : k + count]
            return block.reshape(count * block.shape[1], block.shape[2])

        if self.middle is None:
            return rows(self.main, k)
        return jnp.concatenate([rows(self.main, k), rows(self.middle, self.first + k)], axis=1)


def conv_space_into(d, ids, unit, acc, pad, taps):
    for i in range(3):
        part = dot(space_window(d, pad, i), taps.get(3 * i, 3))
        acc[...] = part if i == 0 else acc[...] + part
    acc[:, d.main :] = jnp.where(ids[0] == unit, acc[:, d.main :], 0.0)


def first_space_kernel(d, parts, *refs):
    ids, *refs = refs
    w_refs, refs = refs[: len(parts[0].arrays)], refs[len(parts[0].arrays) :]
    x, mask, s_out, sums_out, rest, middle, weight, *sems, pad = refs
    copies = parts[0].start(d, ids, w_refs, weight, sems[0])
    later = parts[1].start(d, ids, w_refs, rest, sems[1])
    fill_space(d, pad, x[...].astype(F32))
    for copy in copies:
        copy.wait()
    conv_space_into(d, ids, 0, s_out, pad, Taps(weight))
    for copy in later:
        copy.wait()
    middle[0:SPACE] = weight[:, :, d.main :]
    middle[SPACE:] = rest[:, :, d.main :]
    m = mask[...]
    values = s_out[...]
    count = jnp.sum(m, axis=0, keepdims=True) + jnp.zeros((1, d.half), F32)
    sums_out[...] = sums_of(values * m, values * values * m, count)


def second_space_kernel(d, parts, *refs):
    ids, *refs = refs
    w_refs, refs = refs[: len(parts[0].arrays)], refs[len(parts[0].arrays) :]
    terms, refs = refs[: d.nz], refs[d.nz :]
    q, count, gains, mask, middle, a_out, coef_out, s_out, sums_out, weight, *rest, pad = refs
    rest, sems = rest[: len(parts) - 1], rest[len(parts) - 1 :]
    copies = parts[0].start(d, ids, w_refs, weight, sems[0])
    later = []
    for part, ref, sem in zip(parts[1:], rest, sems[1:]):
        later += part.start(d, ids, w_refs, ref, sem)
    m = mask[...]
    coef = coefs_of(total_of(d, ids, terms), count[4:5, 0:1], gains[...])
    coef_out[...] = coef
    pre = coef[2:3] * normed_of(q[...].astype(F32), coef) + coef[3:4]
    act = jax.nn.silu(pre) * m
    a_out[...] = act.astype(BF)
    fill_space(d, pad, act)
    for copy in copies:
        copy.wait()
    conv_space_into(d, ids, 1, s_out, pad, Taps(weight, middle))
    for copy in later:
        copy.wait()
    values = s_out[...]
    sums_out[...] = sums_of(values * m, values * values * m)


def time_kernel(d, count_w, *refs):
    ids, *refs = refs
    taps, refs = Taps(*refs[:count_w], first=SPACE), refs[count_w:]
    terms, refs = refs[: d.nz], refs[d.nz :]
    s, *counts, gains, mask, a_out, q_out, coef_out, pad = refs
    total = total_of(d, ids, terms)
    count = counts[0][4:5, 0:1] if counts else total[2:3, 0:1]
    coef = coefs_of(total, count, gains[...])
    coef_out[...] = coef
    pre = coef[2:3] * normed_of(s[...], coef) + coef[3:4]
    act = (jax.nn.silu(pre) * mask[...]).astype(BF)
    a_out[...] = act
    fill_time(d, pad, act)
    total = dot_nt(time_window(d, pad, 0), taps.get(0))
    for k in range(1, TIME):
        total = total + dot_nt(time_window(d, pad, k), taps.get(k))
    q_out[...] = total.astype(BF)


def join_kernel(qa, qb, mask, q_out, sums_out):
    total = (qa[...].astype(F32) + qb[...].astype(F32)).astype(BF)
    q_out[...] = total
    values = total.astype(F32)
    m = mask[...]
    sums_out[...] = sums_of(values * m, values * values * m)


def head_kernel(d, denominator, classes, *refs):
    ids, head, *refs = refs
    terms, refs = refs[: d.nz], refs[d.nz :]
    q, count, gains, mask, x, bias, clip_info, labels, *refs = refs
    coef_out, grad_out, sums_out = refs
    m = mask[...]
    coef = coefs_of(total_of(d, ids, terms), count[4:5, 0:1], gains[...])
    coef_out[...] = coef
    normed = normed_of(q[...].astype(F32), coef)
    pre = coef[2:3] * normed + coef[3:4] + x[...].astype(F32)
    sigma = jax.nn.sigmoid(pre)
    y = pre * sigma * m
    folded = jnp.sum(y.reshape(d.cells // 8, 8, d.channels), axis=0)
    step = d.clips
    total = folded
    for k in range(1, 8 // step):
        total = total + pltpu.roll(folded, k * step, 0)
    inverse = 1.0 / clip_info[:, 0:1]
    pooled = total * inverse
    pooled_bf = pooled.astype(BF)
    weight = head[0, :, : d.channels]
    logits = dot(pooled_bf, weight) + bias[...]
    largest = jnp.max(logits, axis=1, keepdims=True)
    shifted = jnp.exp(logits - largest)
    log_total = largest + jnp.log(jnp.sum(shifted, axis=1, keepdims=True))
    lane = lax.broadcasted_iota(jnp.int32, logits.shape, 1)
    onehot = jnp.where(lane == labels[:, 0:1], 1.0, 0.0)
    inside = lane < classes
    kept = jnp.where(inside, logits, 0.0)
    loss = log_total - jnp.sum(kept * onehot, axis=1, keepdims=True)
    grad_logits = jnp.where(inside, (jnp.exp(logits - log_total) - onehot) / denominator, 0.0)
    grad_pooled = dot_nt(grad_logits.astype(BF), weight) * inverse
    grad_y = jnp.broadcast_to(grad_pooled[None], (d.cells // 8, 8, d.channels)).reshape(
        d.cells, d.channels
    )
    grad_pre = grad_y * m * (sigma * (1.0 + pre * (1.0 - sigma)))
    grad_out[...] = grad_pre
    sums_out[0:8, :] = sums_of(grad_pre, grad_pre * normed)
    carried = jnp.where(lane == classes, loss, grad_logits)
    sums_out[8:16, :] = jnp.concatenate(
        [
            pooled_bf.astype(F32)[0 : d.clips],
            carried[0 : d.clips],
            jnp.zeros((8 - 2 * d.clips, d.channels), F32),
        ],
        axis=0,
    )


def time_back_kernel(d, count_w, *refs):
    ids, *refs = refs
    taps, refs = Taps(*refs[:count_w], first=SPACE), refs[count_w:]
    terms, refs = refs[: d.nz], refs[d.nz :]
    grad_two, q, coef_two, count, mask, s, coef_one, *refs = refs
    gq_out, grad_out, sums_out, tot_out, pad = refs
    m = mask[...]
    total = total_of(d, ids, terms)
    tot_out[...] = total
    coef = coef_two[...]
    normed = normed_of(q[...].astype(F32), coef)
    grad_q = norm_back(grad_two[...], normed, coef, total, count[4:5, 0:1], m).astype(BF)
    gq_out[...] = grad_q
    fill_time(d, pad, grad_q)
    grad = dot(time_window(d, pad, TIME - 1), taps.get(0))
    for k in range(1, TIME):
        grad = grad + dot(time_window(d, pad, TIME - 1 - k), taps.get(k))
    grad = grad.astype(BF).astype(F32)
    coef = coef_one[...]
    normed = normed_of(s[...], coef)
    pre = coef[2:3] * normed + coef[3:4]
    grad_pre = grad * m * act_slope(pre)
    grad_out[...] = grad_pre
    sums_out[...] = sums_of(grad_pre, grad_pre * normed)


def space_back_kernel(d, count_w, *refs):
    ids, *refs = refs
    taps, refs = Taps(*refs[:count_w], first=0), refs[count_w:]
    terms, refs = refs[: d.nz], refs[d.nz :]
    grad_pre, s, coef_one, count, mask, *refs = refs
    gs_out, ga_out, tot_out, pad, acc = refs
    total = total_of(d, ids, terms)
    tot_out[...] = total
    coef = coef_one[...]
    normed = normed_of(s[...], coef)
    grad_s = norm_back(grad_pre[...], normed, coef, total, count[4:5, 0:1], mask[...])
    gs_out[...] = grad_s.astype(BF)
    fill_space(d, pad, grad_s)
    for i in range(3):
        part = sum(dot_nt(space_window(d, pad, 2 - i, 2 - j), taps.get(3 * i + j)) for j in range(3))
        acc[...] = part if i == 0 else acc[...] + part
    ga_out[...] = acc[...].astype(BF)


def join_back_kernel(ga, gb, q, coef_two, mask, grad_out, sums_out):
    coef = coef_two[...]
    normed = normed_of(q[...].astype(F32), coef)
    pre = coef[2:3] * normed + coef[3:4]
    grad = ga[...].astype(F32) + gb[...].astype(F32)
    grad_pre = grad * mask[...] * act_slope(pre)
    grad_out[...] = grad_pre
    sums_out[...] = sums_of(grad_pre, grad_pre * normed)


def write_grad(d, w, ids, tap, value, outs, held):
    if w.kind == "natural":
        outs[0][tap] = value.astype(BF)
        return
    held[tap] = value.astype(BF)
    for operand, index, row in w.places(d, ids):
        outs[operand][(*index, tap)] = held[tap, pl.ds(pl.multiple_of(row, 16), d.rows), :]


def space_grads(d, turned, pad, i):
    part = dot(turned[...], space_window(d, pad, 2 - i))
    return [part[:, (2 - j) * d.half : (3 - j) * d.half] for j in range(3)]


def time_grads(d, turned, pad):
    return [dot(turned[...], time_window(d, pad, k)) for k in range(TIME)]


def write_late(d, w, ids, values, middle, outs, held):
    for tap, value in enumerate(values):
        middle[tap] = value[:, d.main :].astype(BF)
        write_grad(d, w, ids, tap, value[:, : d.main], outs, held)


def write_early(d, w, ids, values, middle, outs, held):
    for tap, value in enumerate(values):
        tile = jnp.where(ids[0] == 0, value[:, d.main :], middle[tap].astype(F32))
        value = jnp.concatenate([value[:, : d.main], tile], axis=1)
        write_grad(d, w, ids, tap, value, outs, held)


def time_grad_kernel(d, w, *refs):
    ids, middle, grad_q, act, *refs = refs
    outs, (pad, turned, held) = refs[:-3], refs[-3:]
    fill_time(d, pad, act[...])
    turned[...] = jnp.transpose(grad_q[...].astype(F32)).astype(BF)
    write_early(d, w, ids, time_grads(d, turned, pad), middle, outs, held)


def unit_grad_kernel(d, w, *refs):
    ids, a, grad_s, grad_q, act, middle, *refs = refs
    outs, (pad, time_pad, time_turned, turned, held) = refs[:-5], refs[-5:]
    k = pl.program_id(0)

    @pl.when(k == 0)
    def _():
        fill_space(d, pad, grad_s[...].astype(F32))
        turned[...] = jnp.transpose(a[...].astype(F32)).astype(BF)
        fill_time(d, time_pad, act[...])
        time_turned[...] = jnp.transpose(grad_q[...].astype(F32)).astype(BF)

    @pl.when(k < SPACE // 3)
    def _():
        write_late(d, w, ids, space_grads(d, turned, pad, k), middle, outs, held)

    @pl.when(k >= SPACE // 3)
    def _():
        write_late(d, w, ids, time_grads(d, time_turned, time_pad), middle, outs, held)


def last_space_grad_kernel(d, w, *refs):
    ids, middle, *refs = refs
    terms, refs = refs[: d.nz], refs[d.nz :]
    a, grad_pre, s, coef_one, count, mask, tot_out, *refs = refs
    outs, (pad, turned, held) = refs[:-3], refs[-3:]
    k = pl.program_id(0)

    @pl.when(k == 0)
    def _():
        total = total_of(d, ids, terms)
        tot_out[...] = total
        coef = coef_one[...]
        normed = normed_of(s[...], coef)
        grad_s = norm_back(grad_pre[...], normed, coef, total, count[4:5, 0:1], mask[...])
        fill_space(d, pad, grad_s)
        turned[...] = jnp.transpose(a[...].astype(F32)).astype(BF)

    write_early(d, w, ids, space_grads(d, turned, pad, k), middle, outs, held)


def squares_kernel(*refs):
    *values, out = refs
    row = lax.broadcasted_iota(jnp.int32, (8, LANES), 0)
    lane = lax.broadcasted_iota(jnp.int32, (8, LANES), 1)
    total = jnp.zeros((8, LANES), F32)
    for i, value in enumerate(values):
        here = (row == i // 5) & (lane == i % 5)
        lanes = jnp.sum(value[...], axis=0, keepdims=True)
        total = jnp.where(here, jnp.sum(lanes, axis=1, keepdims=True), total)
    out[...] = total


def sds(shape, dtype=F32):
    return jax.ShapeDtypeStruct(shape, dtype)


def call(body, name, ins, outs, scratch, flops, megabytes=14):
    return pl.pallas_call(
        body,
        name=name,
        out_shape=outs,
        in_specs=[spec for spec, _ in ins],
        out_specs=[whole()] * len(outs),
        scratch_shapes=scratch,
        compiler_params=pltpu.CompilerParams(vmem_limit_bytes=megabytes * MB),
        cost_estimate=pl.CostEstimate(flops=flops, bytes_accessed=8 * MB, transcendentals=0),
    )(*[value for _, value in ins])


def w_ins(weight):
    return [
        (in_hbm(), pltpu.with_memory_space_constraint(piece, pltpu.HBM))
        for piece in weight.arrays
    ]


def v_ins(*values):
    return [(whole(), value) for value in values]


def grad_call(d, body, name, kind, taps, width, ids, values, first_outs, scratch, middle=None):
    if kind == "ring":
        shape, count = (d.nz, 2, taps, d.rows, width), 4
        spec = pl.BlockSpec((d.nz, 2, 3, d.rows, width), lambda k: (0, 0, k, 0, 0))
    elif kind == "parts":
        shape, count = (2, 2, taps, d.rows, width), d.groups // 2
        spec = pl.BlockSpec((2, 2, 3, d.rows, width), lambda k: (0, 0, k, 0, 0))
        first_outs = [*first_outs, sds((d.groups, *shape[1:]), BF)]
    else:
        shape, count = (taps, d.channels, width), 1
        spec = pl.BlockSpec((3, d.channels, width), lambda k: (k, 0, 0))
    fixed = [pl.BlockSpec(out.shape, lambda k: (0, 0)) for out in first_outs]
    if kind == "parts":
        fixed[-1] = pl.BlockSpec((d.groups, 2, 3, d.rows, width), lambda k: (0, 0, k, 0, 0))
    first = 0 if middle is None else middle[1] // 3
    tile = pl.BlockSpec((3, d.channels, LANES), lambda k: (k + first, 0, 0))
    if middle is None:
        ins, in_specs = values, []
        first_outs, fixed = [sds((taps, d.channels, LANES), BF), *first_outs], [tile, *fixed]
    else:
        ins, in_specs = (middle[0], *values), [tile]
    outs = pl.pallas_call(
        functools.partial(body, d, Weight(kind, (), 0, 1)),
        name=name,
        grid=(taps // 3,),
        out_shape=list(first_outs) + [sds(shape, BF)] * count,
        in_specs=[smem()] + in_specs + [whole()] * len(values),
        out_specs=fixed + [spec] * count,
        scratch_shapes=scratch
        + [pltpu.VMEM((d.channels, d.cells), BF), pltpu.VMEM((3, d.channels, width), BF)],
        compiler_params=pltpu.CompilerParams(vmem_limit_bytes=30 * MB),
        cost_estimate=pl.CostEstimate(flops=1, bytes_accessed=1, transcendentals=0),
    )(ids, *ins)
    return outs[: len(first_outs)], outs[len(first_outs) :]


def swap(value, axis, distance=1):
    size = lax.axis_size(axis)
    return lax.ppermute(value, axis, [(i, i ^ distance) for i in range(size)])


def across_yy(values, *besides):
    size = lax.axis_size("yy")
    distance = 1
    while distance < size:
        other = swap(values, "yy", distance)
        distance *= 2
        values = values + (after(other, *besides) if distance >= size else other)
    return values


def around_tm(values):
    size = lax.axis_size("tm")
    return [values] + [
        lax.ppermute(values, "tm", [(i, (i + k) % size) for i in range(size)])
        for k in range(1, size)
    ]


def data_sums(values, last=(), first=()):
    terms = around_tm(across_yy(values, *first))
    return [after(term, *last) if k == len(terms) - 1 else term for k, term in enumerate(terms)]


def data_sums_gather(values):
    distance = 1
    while distance < lax.axis_size("yy"):
        other = swap(values, "yy", distance)
        values = jnp.concatenate([values[:8] + other[:8], values[8:], other[8:]], axis=0)
        distance *= 2
    terms = around_tm(values)
    return [term[:8] for term in terms], terms


def pick(index, first, second):
    return jnp.where(index == 0, first, second)


def after(value, *earlier):
    if not earlier:
        return value
    return lax.optimization_barrier((value, *earlier))[0]


def turn(value):
    size = lax.axis_size("tm")
    return lax.ppermute(value, "tm", [(i, (i + 1) % size) for i in range(size)])


def together(*values):
    return lax.optimization_barrier(values)


def gather_ring(both, besides):
    held, across, made = [both], [], []
    for beside in besides:
        moves = [swap(held[-1], "yy")]
        if len(held) < lax.axis_size("tm"):
            moves.append(turn(held[-1]))
        extra = beside(held[-1], made[-1] if made else None)
        results = together(*moves, *extra)
        across.append(results[0])
        held += results[1 : len(moves)]
        made.append(results[len(moves) :])
    own = held + across
    return Weight("blocks", own + [swap(block, "u") for block in own], 0, both.shape[1]), made


def gather_all(d, s, both, *earlier):
    gathered = lax.all_gather(both, ("u",) + DATA, axis=0, tiled=False)
    gathered = after(gathered, *earlier).reshape(2, d.groups, *both.shape)
    taps = both.shape[1]
    if d.pieces:
        return Weight("all", (gathered,), 0, taps)
    parts = gathered.reshape(2, d.ny, d.nz, 2, taps, d.rows, -1)
    parts = jnp.where(s == 0, parts, parts[:, :, :, ::-1])
    natural = parts.transpose(4, 1, 3, 0, 2, 5, 6).reshape(taps, d.channels, -1)
    return Weight("natural", (natural,), 0, taps)


def added(*values):
    total = values[0].astype(F32)
    for value in values[1:]:
        total = total + value.astype(F32)
    return total.astype(BF)


def reduce_ring(d, gradients, besides):
    def joined(yrel, k, *others, second=None):
        parts = [outs[yrel][k].astype(F32) + outs[2 + yrel][k].astype(F32) for outs in gradients]
        total = jnp.concatenate(parts, axis=1)
        for other in others:
            total = total + other.astype(F32)
        if second is not None:
            total = jnp.stack([total[0], total[1] + second.astype(F32)])
        return total.astype(BF)

    first = joined(1, 1)
    by_y, by_z = swap(first[0], "yy"), turn(first[1])
    moving = joined(0, 1)
    moving, made = jnp.stack([added(moving[0], by_y), moving[1]]), []
    for k, beside in zip(list(range(2, d.nz)) + [0], besides, strict=True):
        across = swap(joined(1, k, second=by_z if k == 2 else None), "yy")
        turned = turn(moving)
        extra = beside(moving, made)
        if extra:
            turned, *extra = together(turned, *extra)
        made.append(extra)
        moving = joined(0, k, across, turned)
    return moving, made


def reduce_all(d, s, u, kind, outs, *earlier):
    if kind == "parts":
        keep, *sends = outs
        theirs = [swap(send, "u") for send in sends]
    else:
        (natural,) = outs
        taps = natural.shape[0]
        parts = natural.reshape(taps, d.ny, 2, 2, d.nz, d.rows, -1)
        parts = parts.transpose(3, 1, 4, 2, 0, 5, 6)
        parts = jnp.where(u == 0, parts, parts[::-1])
        parts = jnp.where(s == 0, parts, parts[:, :, :, ::-1])
        keep, send = parts.reshape(2, d.groups, 2, taps, d.rows, -1)
        theirs = [swap(send, "u")]
    keep, theirs = after((keep, theirs), *earlier)
    both = added(keep, jnp.concatenate(theirs, axis=0))
    return both, lax.psum_scatter(both, DATA, scatter_dimension=0, tiled=False)


def own_rows(s, mine, theirs):
    other = swap(theirs, "s")
    return pick(s, mine, other), pick(s, other, mine)


def joined_channels(*parts):
    return jnp.concatenate(parts, axis=-1).astype(F32)


def halves(d, values, unit):
    low, middle, high = (
        values[..., : d.main],
        values[..., d.main : d.half],
        values[..., d.half :],
    )
    empty = jnp.zeros_like(middle)
    first, second = (middle, empty) if unit == 0 else (empty, middle)
    return jnp.concatenate([low, first], axis=-1), jnp.concatenate([high, second], axis=-1)


def rows_of(gain, shift):
    return jnp.concatenate(
        [gain[None], shift[None], jnp.zeros((6, gain.shape[0]), F32)], axis=0
    )


def square_rows(values):
    return jnp.sum(values * values, axis=tuple(range(1, values.ndim - 1)))


def adam_part(weight, gradient, moment_one, moment_two, decay):
    new_one = BETA_ONE * moment_one + (1.0 - BETA_ONE) * gradient
    new_two = BETA_TWO * moment_two + (1.0 - BETA_TWO) * gradient * gradient
    direction = (
        new_one / (1.0 - BETA_ONE**STEP) / (jnp.sqrt(new_two / (1.0 - BETA_TWO**STEP)) + EPS_ADAM)
        + decay * weight
    )
    return (new_one, new_two, direction)


def on_device(
    clips_x,
    frames,
    labels,
    spatial_weight,
    temporal_weight,
    head_weight,
    affine,
    head_bias,
    spatial_first,
    spatial_second,
    temporal_first,
    temporal_second,
    head_first,
    head_second,
    affine_first,
    affine_second,
    bias_first,
    bias_second,
):
    s, u, z, yy = (lax.axis_index(axis) for axis in ("s", "u", "tm", "yy"))
    ny, nz = lax.axis_size("yy"), lax.axis_size("tm")
    micro, clips, _, height, width, channels = clips_x.shape
    mid = spatial_weight.shape[3]
    rows = spatial_weight.shape[0]
    classes = head_weight.shape[1]
    d = Dims(clips, nz, height, width, channels, mid, rows, ny, nz)
    assert nz == 4 and micro == 2
    ids = jnp.stack([s, u, yy, z]).astype(jnp.int32)
    denominator = micro * clips * 4 * ny

    def prepared(weight, l):
        return weight[:, l].astype(BF).transpose(1, 0, 2)

    def paired(first, second):
        return jnp.stack([pick(s, first, second), swap(pick(s, second, first), "s")])

    def by_index(index, mine, other):
        return jnp.stack([pick(index, mine, other), pick(index, other, mine)])

    pairs = []
    for value in (clips_x, jnp.stack([frames, labels]).transpose(1, 0, 2)):
        kept = pick(u, value[0], value[1])
        pairs.append(by_index(u, kept, swap(pick(u, value[1], value[0]), "u")))
    units = [
        jnp.concatenate([prepared(weight, l) for weight in (spatial_weight, temporal_weight)], axis=0)
        for l in range(2)
    ]
    early = paired(
        units[0][..., : d.half],
        jnp.concatenate([units[0][..., d.half :], units[1][..., d.main : d.half]], axis=-1),
    )

    def beside_first(*_):
        four, info = (by_index(s, pair, swap(pair, "s")) for pair in pairs)
        return four.reshape(nz, clips, height * width, channels), info

    def clips_home(four):
        return lax.all_to_all(four, "tm", split_axis=0, concat_axis=0, tiled=True)

    def beside_second(block, first):
        weights = after((spatial_weight, temporal_weight, head_weight), block)
        slot = jnp.pad(weights[2].astype(BF), ((0, 0), (0, d.main - classes)))[None]
        parts = [prepared(weights[0], 1), prepared(weights[1], 1)]
        sides = [
            jnp.concatenate([part[..., start : start + d.main] for part in parts] + [slot], axis=0)
            for start in (0, d.half)
        ]
        return [paired(*sides), clips_home(first[0])]

    def beside_third(block, second):
        x = second[1].reshape(nz, clips, height * width, channels)
        x = x.transpose(0, 2, 1, 3).reshape(d.cells, channels)
        weights = after((spatial_weight, temporal_weight, head_weight), block)
        gains, bias = after((affine, head_bias), block)
        bias_row = jnp.full((1, channels), -1e30, F32).at[0, :classes].set(bias)
        rows_one, rows_two = [], []
        for l in range(2):
            low, high = halves(d, gains[l, :, :mid], l)
            mine = pick(s, low, high)
            rows_one.append(rows_of(mine[0], mine[1]))
            rows_two.append(rows_of(gains[l, 0, mid:], gains[l, 1, mid:]))
        squares = [square_rows(weight[:, l]) for weight in weights[:2] for l in range(2)]
        return [x, bias_row, *rows_one, *rows_two, *squares, square_rows(weights[2])]

    if d.pieces:
        early_w, made = gather_ring(
            early, [beside_first, beside_second, beside_third, lambda *_: []]
        )
        (_, info_four), (late, _), small, _ = made
    else:
        early_w = gather_all(d, s, early)
        first = beside_first()
        info_four = first[1]
        second = beside_second(early, first)
        late, small = second[0], beside_third(early, second)
    x, bias_row, *small = small
    gains_one, gains_two, weight_squares = small[:2], small[2:4], small[4:]

    mine_info = lax.dynamic_index_in_dim(
        info_four.reshape(nz, 2, clips), z, 0, keepdims=False
    )
    my_frames, my_labels = mine_info[0], mine_info[1]
    valid = (jnp.arange(nz, dtype=jnp.int32)[:, None] * 8 < my_frames[None, :]).astype(F32)
    mask = jnp.broadcast_to(valid[:, None, :], (nz, height * width, clips)).reshape(d.cells, 1)
    divisor = (my_frames // 8).astype(F32) * (height * width)
    clip_info = jnp.broadcast_to(jnp.tile(divisor, 8 // clips)[:, None], (8, LANES))
    label_rows = jnp.broadcast_to(jnp.tile(my_labels, 8 // clips)[:, None], (8, LANES))
    mask, clip_info, label_rows = together(mask, clip_info, label_rows)

    wide, narrow = (d.cells, d.half), (d.cells, channels)
    space_flops = 2 * d.cells * SPACE * channels * d.half
    time_flops = 2 * d.cells * TIME * channels * d.half

    def first_space(weight):
        parts = [weight.part(0, SPACE), weight.part(SPACE, TIME)]
        return call(
            functools.partial(first_space_kernel, d, parts),
            "space0",
            [(smem(), ids)] + w_ins(weight) + v_ins(x, mask),
            [
                sds(wide),
                sds((8, d.half)),
                parts[1].natural(d),
                sds((SPACE + TIME, d.channels, LANES), BF),
            ],
            [pltpu.VMEM(parts[0].natural(d).shape, BF)]
            + [part.semaphores(d) for part in parts]
            + [space_scratch(d, channels)],
            space_flops,
            20,
        )

    def next_space(weight, middle, q, terms, count):
        sizes = (SPACE, TIME, 1)
        parts = [weight.part(sum(sizes[:i]), size) for i, size in enumerate(sizes)]
        return call(
            functools.partial(second_space_kernel, d, parts),
            "space1",
            [(smem(), ids)] + w_ins(weight) + v_ins(*terms, q, count, gains_two[0], mask, middle),
            [sds(narrow, BF), sds((8, channels)), sds(wide), sds((8, d.half))]
            + [part.natural(d) for part in parts],
            [part.semaphores(d) for part in parts] + [space_scratch(d, channels)],
            space_flops,
        )

    def time_next(l, s_value, terms, *count):
        return call(
            functools.partial(time_kernel, d, len(time_w[l])),
            f"time{l}",
            [(smem(), ids)] + v_ins(*time_w[l], *terms, s_value, *count, gains_one[l], mask),
            [sds(wide, BF), sds(narrow, BF), sds((8, d.half))],
            [time_scratch(d, d.half)],
            time_flops,
        )

    def joined(q_part):
        return call(
            join_kernel,
            "join",
            v_ins(q_part, swap(q_part, "s"), mask),
            [sds(narrow, BF), sds((8, channels))],
            [],
            d.cells * channels,
            12,
        )

    s0, sums, time_first, middle = first_space(early_w)
    time_w = [(time_first,), None]
    terms = data_sums(sums)
    act0, q_part, coef_one0 = time_next(0, s0, terms)
    count = coef_one0
    q0, sums = joined(q_part)
    terms = data_sums(sums)
    late_w = gather_all(d, s, late, terms[0])
    a_mid, coef_two0, s1, sums, space_late, time_late, head_w = next_space(
        late_w, middle, q0, terms, count
    )
    time_w[1] = (time_late, middle)
    terms = data_sums(sums)
    act1, q_part, coef_one1 = time_next(1, s1, terms, count)
    q1, sums = joined(q_part)
    terms = data_sums(sums)
    coef_two1, grad_two, sums = call(
        functools.partial(head_kernel, d, float(denominator), classes),
        "head",
        [(smem(), ids)]
        + v_ins(head_w, *terms, q1, count, gains_two[1], mask, x, bias_row, clip_info, label_rows),
        [sds((8, channels)), sds(narrow), sds((16, channels))],
        [],
        4 * d.cells * channels,
    )
    terms, carried = data_sums_gather(sums)

    def time_back(l, grad, q, coef_two, terms, s_value, coef_one):
        return call(
            functools.partial(time_back_kernel, d, len(time_w[l])),
            f"time_back{l}",
            [(smem(), ids)]
            + v_ins(*time_w[l], *terms, grad, q, coef_two, count, mask, s_value, coef_one),
            [sds(narrow, BF), sds(wide), sds((8, d.half)), sds((8, channels))],
            [time_scratch(d, channels)],
            1,
        )

    late_kind = "parts" if d.pieces else "natural"
    early_kind = "ring" if d.pieces else "natural"

    grad_q1, grad_one, sums, tot_two1 = time_back(
        1, grad_two, q1, coef_two1, terms, s1, coef_one1
    )
    terms = data_sums(sums)
    grad_s1, ga_part, tot_one1 = call(
        functools.partial(space_back_kernel, d, 2),
        "space_back",
        [(smem(), ids)] + v_ins(space_late, middle, *terms, grad_one, s1, coef_one1, count, mask),
        [sds(wide, BF), sds(narrow, BF), sds((8, d.half))],
        [space_scratch(d, d.half), pltpu.VMEM((d.cells, channels), F32)],
        space_flops,
    )
    ga_other = swap(ga_part, "s")
    late_first, late_outs = grad_call(
        d,
        unit_grad_kernel,
        "unit_grad1",
        late_kind,
        SPACE + TIME,
        d.main,
        ids,
        (a_mid, grad_s1, grad_q1, act1),
        [],
        [
            space_scratch(d, d.half),
            time_scratch(d, d.half),
            pltpu.VMEM((d.channels, d.cells), BF),
        ],
    )
    middle_grad, *late_first = late_first
    late_outs = [*late_first, *late_outs]
    grad_two, sums = call(
        join_back_kernel,
        "join_back",
        v_ins(ga_part, after(ga_other, *late_outs), q0, coef_two0, mask),
        [sds(narrow), sds((8, channels))],
        [],
        20 * 10**9,
        12,
    )
    late_both, late_sum = reduce_all(d, s, u, late_kind, late_outs, sums)

    terms = data_sums(after(sums, late_both))
    grad_q0, grad_one, sums, tot_two0 = time_back(
        0, grad_two, q0, coef_two0, terms, s0, coef_one0
    )
    _, time_outs0 = grad_call(
        d,
        time_grad_kernel,
        "time_grad0",
        early_kind,
        TIME,
        d.half,
        ids,
        (grad_q0, act0),
        [],
        [time_scratch(d, d.half)],
        (middle_grad, SPACE),
    )
    if d.pieces:
        time_outs0 = [*time_outs0[:2], *(swap(send, "u") for send in time_outs0[2:])]
    terms = data_sums(sums, time_outs0[2:], time_outs0[:2])
    (tot_one0,), space_outs0 = grad_call(
        d,
        last_space_grad_kernel,
        "space_grad0",
        early_kind,
        SPACE,
        d.half,
        ids,
        (*terms, x, grad_one, s0, coef_one0, count, mask),
        [sds((8, d.half))],
        [space_scratch(d, d.half)],
        (middle_grad, 0),
    )

    def head_steps(value):
        rows_all = jnp.concatenate([term[8:] for term in after(carried, value)], axis=0)
        rows_all = jnp.concatenate([rows_all, swap(rows_all, "u")], axis=0)
        rows_all = rows_all.reshape(-1, 8, channels)
        pooled_all = rows_all[:, :clips].reshape(-1, channels)
        logit_all = rows_all[:, clips : 2 * clips].reshape(-1, channels)
        loss_sum = jnp.sum(logit_all[:, classes])
        logit_all = logit_all[:, :classes]
        bias_grad = jnp.sum(logit_all, axis=0)
        base = d.row_base(yy, s, u, z)
        pooled_mine = lax.dynamic_slice_in_dim(pooled_all, base, rows, 1)
        head_grad = lax.dot_general(
            pooled_mine.astype(BF),
            logit_all.astype(BF),
            (((0,), (0,)), ((), ())),
            preferred_element_type=F32,
        )
        head_one, head_two, head_dir = adam_part(head_weight, head_grad, head_first, head_second, DECAY)
        bias_one, bias_two, bias_dir = adam_part(head_bias, bias_grad, bias_first, bias_second, 0.0)
        return (
            loss_sum, head_one, head_two, head_dir, square_rows(head_dir), bias_one, bias_two, bias_dir
        )

    def affine_steps(value):
        one0, one1, two0, two1 = after((tot_one0, tot_one1, tot_two0, tot_two1), value)
        ones, twos = jnp.stack([one0[:2], one1[:2]]), jnp.stack([two0[:2], two1[:2]])
        small = jnp.concatenate([ones, twos], axis=-1)
        small = small + swap(small, "u")
        ones, twos = small[..., : d.half], small[..., d.half :]
        ones_other = swap(ones, "s")
        low, high = pick(s, ones, ones_other), pick(s, ones_other, ones)
        ones = [
            jnp.concatenate([low[0], high[0, :, : d.main]], axis=-1),
            jnp.concatenate([low[1, :, : d.main], high[1, :, d.main :], high[1, :, : d.main]], axis=-1),
        ]
        both = jnp.concatenate([jnp.stack(ones), twos], axis=-1)
        affine_grad = jnp.stack([both[:, 1], both[:, 0]], axis=1)
        one, two, direction = adam_part(affine, affine_grad, affine_first, affine_second, 0.0)
        return one, two, affine - RATE_SMALL * direction

    if d.pieces:
        early_sum, made = reduce_ring(
            d,
            [[*space_outs0[:2], *(swap(send, "u") for send in space_outs0[2:])], time_outs0],
            [
                lambda value, _: (),
                lambda value, _: (late_sum[0], late_sum[1], *head_steps(value)),
                lambda value, made: (*own_rows(s, *made[1][:2]), *affine_steps(value)),
            ],
        )
        late_sum, head_made, affine_made = made[2][:2], made[1][2:], made[2][2:]
    else:
        early_outs = [jnp.concatenate([space_outs0[0], time_outs0[0]], axis=0)]
        _, early_sum = reduce_all(d, s, u, early_kind, early_outs)
        late_sum = own_rows(s, late_sum[0], late_sum[1])
        head_made = head_steps(early_sum)
        affine_made = affine_steps(early_sum)
    loss_sum, head_one, head_two, head_dir, head_squares, bias_one, bias_two, bias_dir = head_made
    low, high = own_rows(s, early_sum[0], early_sum[1])
    early_sum = joined_channels(low, high[..., : d.main])
    late_sum = joined_channels(late_sum[0], high[..., d.main :], late_sum[1])

    def both_units(first, second):
        return jnp.stack([first, second]).transpose(2, 0, 1, 3)

    spatial_grad = both_units(early_sum[:SPACE], late_sum[:SPACE])
    temporal_grad = both_units(early_sum[SPACE:], late_sum[SPACE:])
    space_one, space_two, space_dir = adam_part(
        spatial_weight, spatial_grad, spatial_first, spatial_second, DECAY
    )
    time_one, time_two, time_dir = adam_part(
        temporal_weight, temporal_grad, temporal_first, temporal_second, DECAY
    )
    affine_one, affine_two, new_affine = affine_made
    dir_squares = [square_rows(v[:, l]) for v in (space_dir, time_dir) for l in range(2)]
    dir_squares.append(head_squares)
    padded = pl.pallas_call(
        squares_kernel,
        name="squares",
        out_shape=sds((8, LANES)),
        in_specs=[whole()] * 10,
        out_specs=whole(),
    )(*weight_squares, *dir_squares)
    native, by_tap = (Layout(major_to_minor=order) for order in ((0, 2, 1, 3), (1, 2, 0, 3)))
    moments = together(
        *(with_layout_constraint(v, by_tap) for v in (space_one, space_two, time_one, time_two))
    )
    moments = [with_layout_constraint(value, native) for value in moments]
    space_one, space_two, time_one, time_two = moments
    padded = padded + swap(padded, "u")
    padded = padded + swap(padded, "s")
    terms = data_sums(padded, moments[1:3], (moments[0], moments[3]))
    terms = jnp.stack(terms)
    padded = sum(terms[lax.rem(z + (nz - place), nz)] for place in range(nz))
    norms = jnp.sqrt(padded[:2, :5])
    trust = norms[0] / norms[1]
    new_space = spatial_weight - RATE * trust[0:2][None, :, None, None] * space_dir
    new_time = temporal_weight - RATE * trust[2:4][None, :, None, None] * time_dir
    new_head = head_weight - RATE * trust[4] * head_dir
    new_bias = head_bias - RATE_SMALL * bias_dir
    return (
        loss_sum,
        space_one,
        space_two,
        new_space,
        time_one,
        time_two,
        new_time,
        head_one,
        head_two,
        new_head,
        affine_one,
        affine_two,
        new_affine,
        bias_one,
        bias_two,
        new_bias,
        norms,
    )


def solution(mesh):
    dp, tm = mesh.shape["dp"], mesh.shape["tm"]
    fine = Mesh(mesh.devices.reshape(dp // 4, 2, 2, tm), ALL)
    dp_axes = ("yy", "s", "u")
    owner = P(ALL)
    return jax.shard_map(
        on_device,
        mesh=fine,
        in_specs=(
            P(None, dp_axes, "tm"),
            P(None, dp_axes),
            P(None, dp_axes),
            owner,
            owner,
            owner,
            P(),
            P(),
            owner,
            owner,
            owner,
            owner,
            owner,
            owner,
            P(),
            P(),
            P(),
            P(),
        ),
        out_specs=(P(),) + (owner,) * 9 + (P(),) * 7,
        check_vma=False,
    )
```

```python
import functools

import jax
import jax.numpy as jnp
from jax import lax
from jax.experimental import pallas as pl
from jax.experimental.layout import Layout, with_layout_constraint
from jax.experimental.pallas import tpu as pltpu
from jax.sharding import Mesh
from jax.sharding import PartitionSpec as P

STEP = 5
EPS_NORM = 1e-05
EPS_ADAM = 1e-06
BETA_ONE = 0.5
BETA_TWO = 0.5
DECAY = 0.01
RATE = 0.3
RATE_SMALL = 0.1

F32 = jnp.float32
BF = jnp.bfloat16
LANES = 128
SPACE, TIME = 9, 3
ALL = ("yy", "s", "u", "tm")
DATA = ("yy", "tm")
MB = 1 << 20


def whole():
    return pl.BlockSpec(memory_space=pltpu.VMEM)


def in_hbm():
    return pl.BlockSpec(memory_space=pltpu.HBM)


def smem():
    return pl.BlockSpec(memory_space=pltpu.SMEM)


def dot(a, b):
    return jnp.dot(a, b, preferred_element_type=F32)


def dot_nt(a, b):
    return lax.dot_general(a, b, (((1,), (1,)), ((), ())), preferred_element_type=F32)


class Dims:
    def __init__(self, clips, frames, height, width, channels, mid, rows, ny, nz):
        self.clips, self.frames, self.height, self.width = clips, frames, height, width
        self.channels, self.mid, self.rows, self.ny, self.nz = channels, mid, rows, ny, nz
        self.line = width * clips
        self.plane = height * self.line
        self.cells = frames * self.plane
        tiles = mid // LANES
        assert tiles % 2 == 1
        self.main = tiles // 2 * LANES
        self.half = self.main + LANES
        self.groups = ny * nz
        self.pieces = rows % 16 == 0 and ny == 2

    def row_base(self, yy, s, u, z):
        return (((yy * 2 + s) * 2 + u) * self.nz + z) * self.rows


class Weight:
    def __init__(self, kind, arrays, first, taps):
        self.kind, self.arrays, self.first, self.taps = kind, arrays, first, taps

    def part(self, first, taps):
        return Weight(self.kind, self.arrays, self.first + first, taps)

    def copies_needed(self, d):
        return 1 if self.kind == "natural" else 4 * d.groups

    def natural(self, d):
        return sds((self.taps, d.channels, self.arrays[0].shape[-1]), BF)

    def semaphores(self, d):
        return pltpu.SemaphoreType.DMA((self.copies_needed(d),))

    def places(self, d, ids):
        s, u, yy, z = (ids[i] for i in range(4))
        for urel in range(2):
            for i in range(d.groups):
                for srel in range(2):
                    if self.kind == "all":
                        row = d.row_base(i // d.nz, srel ^ s, urel, i % d.nz)
                        yield 0, (urel, i, srel), row
                        continue
                    if self.kind in ("blocks", "ring"):
                        yrel, k = i // d.nz, i % d.nz
                        row = d.row_base(
                            yrel ^ yy, srel ^ s, urel ^ u, lax.rem(z + (d.nz - k), d.nz)
                        )
                        if self.kind == "blocks":
                            yield urel * d.groups + i, (srel,), row
                        else:
                            yield urel * 2 + yrel, (k, srel), row
                    else:
                        row = d.row_base(i // d.nz, srel ^ s, urel ^ u, i % d.nz)
                        if urel == 0:
                            yield 0, (i, srel), row
                        else:
                            yield 1 + i // 2, (i % 2, srel), row

    def start(self, d, ids, refs, scratch, sems):
        taps = pl.ds(self.first, self.taps)
        copies = []
        if self.kind == "natural":
            copies.append(pltpu.make_async_copy(refs[0].at[taps], scratch, sems.at[0]))
        else:
            for operand, index, row in self.places(d, ids):
                copies.append(
                    pltpu.make_async_copy(
                        refs[operand].at[(*index, taps)],
                        scratch.at[:, pl.ds(pl.multiple_of(row, 16), d.rows), :],
                        sems.at[len(copies)],
                    )
                )
        for copy in copies:
            copy.start()
        return copies


def space_scratch(d, width):
    return pltpu.VMEM((d.frames, (d.height + 2) * d.line, 3 * width), BF)


def time_scratch(d, width):
    return pltpu.VMEM(((d.frames + 2) * d.plane, width), BF)


def fill_space(d, pad, values):
    cells, width = values.shape
    place = lax.broadcasted_iota(jnp.int32, (cells, width), 0)
    column = lax.rem(lax.div(place, d.clips), d.width)
    edge = jnp.zeros((d.frames, d.line, 3 * width), BF)
    pad[:, 0 : d.line, :] = edge
    pad[:, d.line + d.plane :, :] = edge
    left = jnp.where(column > 0, pltpu.roll(values, d.clips, 0), 0.0)
    right = jnp.where(column < d.width - 1, pltpu.roll(values, cells - d.clips, 0), 0.0)
    for j, moved in enumerate((left, values, right)):
        block = moved.astype(BF).reshape(d.frames, d.plane, width)
        pad[:, d.line : d.line + d.plane, j * width : (j + 1) * width] = block


def space_window(d, pad, i, j=None):
    rows = pl.ds(pl.multiple_of(i * d.line, d.line), d.plane)
    if j is None:
        block = pad[:, rows, :]
    else:
        width = pad.shape[-1] // 3
        block = pad[:, rows, pl.ds(pl.multiple_of(j * width, LANES), width)]
    return block.reshape(d.cells, block.shape[-1])


def fill_time(d, pad, values):
    width = values.shape[1]
    edge = jnp.zeros((d.plane, width), BF)
    pad[0 : d.plane, :] = edge
    pad[d.plane + d.cells :, :] = edge
    pad[d.plane : d.plane + d.cells, :] = values


def time_window(d, pad, k):
    return pad[pl.ds(pl.multiple_of(k * d.plane, d.plane), d.cells), :]


def sums_of(first, second, extra=None):
    width = first.shape[1]
    rows = [jnp.sum(first, axis=0, keepdims=True), jnp.sum(second, axis=0, keepdims=True)]
    if extra is not None:
        rows.append(extra)
    rows.append(jnp.zeros((8 - len(rows), width), F32))
    return jnp.concatenate(rows, axis=0)


def total_of(d, ids, terms):
    z = ids[3]
    values = [term[...] for term in terms]
    total = None
    for place in range(d.nz):
        here = values[0]
        for k in range(1, d.nz):
            here = jnp.where(lax.rem(z + (d.nz - k), d.nz) == place, values[k], here)
        total = here if total is None else total + here
    return total


def coefs_of(total, count, gains):
    average = total[0:1] / count
    scale = lax.rsqrt(total[1:2] / count - average * average + EPS_NORM)
    return jnp.concatenate(
        [
            average,
            scale,
            gains[0:2],
            jnp.broadcast_to(count, average.shape),
            jnp.zeros((3, total.shape[1]), F32),
        ],
        axis=0,
    )


def normed_of(values, coef):
    return (values - coef[0:1]) * coef[1:2]


def act_slope(pre):
    sigma = jax.nn.sigmoid(pre)
    return sigma * (1.0 + pre * (1.0 - sigma))


def norm_back(grad_pre, normed, coef, total, count, mask):
    scale = coef[2:3] * coef[1:2]
    return mask * (scale * (grad_pre - (total[0:1] + normed * total[1:2]) / count))


class Taps:
    def __init__(self, main, middle=None, first=0):
        self.main, self.middle, self.first = main, middle, first

    def get(self, k, count=1):
        def rows(ref, k):
            block = ref[k : k + count]
            return block.reshape(count * block.shape[1], block.shape[2])

        if self.middle is None:
            return rows(self.main, k)
        return jnp.concatenate([rows(self.main, k), rows(self.middle, self.first + k)], axis=1)


def conv_space_into(d, ids, unit, acc, pad, taps):
    for i in range(3):
        part = dot(space_window(d, pad, i), taps.get(3 * i, 3))
        acc[...] = part if i == 0 else acc[...] + part
    acc[:, d.main :] = jnp.where(ids[0] == unit, acc[:, d.main :], 0.0)


def first_space_kernel(d, parts, *refs):
    ids, *refs = refs
    w_refs, refs = refs[: len(parts[0].arrays)], refs[len(parts[0].arrays) :]
    x, mask, s_out, sums_out, rest, middle, weight, *sems, pad = refs
    copies = parts[0].start(d, ids, w_refs, weight, sems[0])
    later = parts[1].start(d, ids, w_refs, rest, sems[1])
    fill_space(d, pad, x[...].astype(F32))
    for copy in copies:
        copy.wait()
    conv_space_into(d, ids, 0, s_out, pad, Taps(weight))
    for copy in later:
        copy.wait()
    middle[0:SPACE] = weight[:, :, d.main :]
    middle[SPACE:] = rest[:, :, d.main :]
    m = mask[...]
    values = s_out[...]
    count = jnp.sum(m, axis=0, keepdims=True) + jnp.zeros((1, d.half), F32)
    sums_out[...] = sums_of(values * m, values * values * m, count)


def second_space_kernel(d, parts, *refs):
    ids, *refs = refs
    w_refs, refs = refs[: len(parts[0].arrays)], refs[len(parts[0].arrays) :]
    terms, refs = refs[: d.nz], refs[d.nz :]
    q, count, gains, mask, middle, a_out, coef_out, s_out, sums_out, weight, *rest, pad = refs
    rest, sems = rest[: len(parts) - 1], rest[len(parts) - 1 :]
    copies = parts[0].start(d, ids, w_refs, weight, sems[0])
    later = []
    for part, ref, sem in zip(parts[1:], rest, sems[1:]):
        later += part.start(d, ids, w_refs, ref, sem)
    m = mask[...]
    coef = coefs_of(total_of(d, ids, terms), count[4:5, 0:1], gains[...])
    coef_out[...] = coef
    pre = coef[2:3] * normed_of(q[...].astype(F32), coef) + coef[3:4]
    act = jax.nn.silu(pre) * m
    a_out[...] = act.astype(BF)
    fill_space(d, pad, act)
    for copy in copies:
        copy.wait()
    conv_space_into(d, ids, 1, s_out, pad, Taps(weight, middle))
    for copy in later:
        copy.wait()
    values = s_out[...]
    sums_out[...] = sums_of(values * m, values * values * m)


def time_kernel(d, count_w, *refs):
    ids, *refs = refs
    taps, refs = Taps(*refs[:count_w], first=SPACE), refs[count_w:]
    terms, refs = refs[: d.nz], refs[d.nz :]
    s, *counts, gains, mask, a_out, q_out, coef_out, pad = refs
    total = total_of(d, ids, terms)
    count = counts[0][4:5, 0:1] if counts else total[2:3, 0:1]
    coef = coefs_of(total, count, gains[...])
    coef_out[...] = coef
    pre = coef[2:3] * normed_of(s[...], coef) + coef[3:4]
    act = (jax.nn.silu(pre) * mask[...]).astype(BF)
    a_out[...] = act
    fill_time(d, pad, act)
    total = dot_nt(time_window(d, pad, 0), taps.get(0))
    for k in range(1, TIME):
        total = total + dot_nt(time_window(d, pad, k), taps.get(k))
    q_out[...] = total.astype(BF)


def join_kernel(qa, qb, mask, q_out, sums_out):
    total = (qa[...].astype(F32) + qb[...].astype(F32)).astype(BF)
    q_out[...] = total
    values = total.astype(F32)
    m = mask[...]
    sums_out[...] = sums_of(values * m, values * values * m)


def head_kernel(d, denominator, classes, *refs):
    ids, head, *refs = refs
    terms, refs = refs[: d.nz], refs[d.nz :]
    q, count, gains, mask, x, bias, clip_info, labels, *refs = refs
    coef_out, grad_out, sums_out = refs
    m = mask[...]
    coef = coefs_of(total_of(d, ids, terms), count[4:5, 0:1], gains[...])
    coef_out[...] = coef
    normed = normed_of(q[...].astype(F32), coef)
    pre = coef[2:3] * normed + coef[3:4] + x[...].astype(F32)
    sigma = jax.nn.sigmoid(pre)
    y = pre * sigma * m
    folded = jnp.sum(y.reshape(d.cells // 8, 8, d.channels), axis=0)
    step = d.clips
    total = folded
    for k in range(1, 8 // step):
        total = total + pltpu.roll(folded, k * step, 0)
    inverse = 1.0 / clip_info[:, 0:1]
    pooled = total * inverse
    pooled_bf = pooled.astype(BF)
    weight = head[0, :, : d.channels]
    logits = dot(pooled_bf, weight) + bias[...]
    largest = jnp.max(logits, axis=1, keepdims=True)
    shifted = jnp.exp(logits - largest)
    log_total = largest + jnp.log(jnp.sum(shifted, axis=1, keepdims=True))
    lane = lax.broadcasted_iota(jnp.int32, logits.shape, 1)
    onehot = jnp.where(lane == labels[:, 0:1], 1.0, 0.0)
    inside = lane < classes
    kept = jnp.where(inside, logits, 0.0)
    loss = log_total - jnp.sum(kept * onehot, axis=1, keepdims=True)
    grad_logits = jnp.where(inside, (jnp.exp(logits - log_total) - onehot) / denominator, 0.0)
    grad_pooled = dot_nt(grad_logits.astype(BF), weight) * inverse
    grad_y = jnp.broadcast_to(grad_pooled[None], (d.cells // 8, 8, d.channels)).reshape(
        d.cells, d.channels
    )
    grad_pre = grad_y * m * (sigma * (1.0 + pre * (1.0 - sigma)))
    grad_out[...] = grad_pre
    sums_out[0:8, :] = sums_of(grad_pre, grad_pre * normed)
    carried = jnp.where(lane == classes, loss, grad_logits)
    sums_out[8:16, :] = jnp.concatenate(
        [
            pooled_bf.astype(F32)[0 : d.clips],
            carried[0 : d.clips],
            jnp.zeros((8 - 2 * d.clips, d.channels), F32),
        ],
        axis=0,
    )


def time_back_kernel(d, count_w, *refs):
    ids, *refs = refs
    taps, refs = Taps(*refs[:count_w], first=SPACE), refs[count_w:]
    terms, refs = refs[: d.nz], refs[d.nz :]
    grad_two, q, coef_two, count, mask, s, coef_one, *refs = refs
    gq_out, grad_out, sums_out, tot_out, pad = refs
    m = mask[...]
    total = total_of(d, ids, terms)
    tot_out[...] = total
    coef = coef_two[...]
    normed = normed_of(q[...].astype(F32), coef)
    grad_q = norm_back(grad_two[...], normed, coef, total, count[4:5, 0:1], m).astype(BF)
    gq_out[...] = grad_q
    fill_time(d, pad, grad_q)
    grad = dot(time_window(d, pad, TIME - 1), taps.get(0))
    for k in range(1, TIME):
        grad = grad + dot(time_window(d, pad, TIME - 1 - k), taps.get(k))
    grad = grad.astype(BF).astype(F32)
    coef = coef_one[...]
    normed = normed_of(s[...], coef)
    pre = coef[2:3] * normed + coef[3:4]
    grad_pre = grad * m * act_slope(pre)
    grad_out[...] = grad_pre
    sums_out[...] = sums_of(grad_pre, grad_pre * normed)


def space_back_kernel(d, count_w, *refs):
    ids, *refs = refs
    taps, refs = Taps(*refs[:count_w], first=0), refs[count_w:]
    terms, refs = refs[: d.nz], refs[d.nz :]
    grad_pre, s, coef_one, count, mask, *refs = refs
    gs_out, ga_out, tot_out, pad, acc = refs
    total = total_of(d, ids, terms)
    tot_out[...] = total
    coef = coef_one[...]
    normed = normed_of(s[...], coef)
    grad_s = norm_back(grad_pre[...], normed, coef, total, count[4:5, 0:1], mask[...])
    gs_out[...] = grad_s.astype(BF)
    fill_space(d, pad, grad_s)
    for i in range(3):
        part = sum(dot_nt(space_window(d, pad, 2 - i, 2 - j), taps.get(3 * i + j)) for j in range(3))
        acc[...] = part if i == 0 else acc[...] + part
    ga_out[...] = acc[...].astype(BF)


def join_back_kernel(ga, gb, q, coef_two, mask, grad_out, sums_out):
    coef = coef_two[...]
    normed = normed_of(q[...].astype(F32), coef)
    pre = coef[2:3] * normed + coef[3:4]
    grad = ga[...].astype(F32) + gb[...].astype(F32)
    grad_pre = grad * mask[...] * act_slope(pre)
    grad_out[...] = grad_pre
    sums_out[...] = sums_of(grad_pre, grad_pre * normed)


def write_grad(d, w, ids, tap, value, outs, held):
    if w.kind == "natural":
        outs[0][tap] = value.astype(BF)
        return
    held[tap] = value.astype(BF)
    for operand, index, row in w.places(d, ids):
        outs[operand][(*index, tap)] = held[tap, pl.ds(pl.multiple_of(row, 16), d.rows), :]


def space_grads(d, turned, pad, i):
    part = dot(turned[...], space_window(d, pad, 2 - i))
    return [part[:, (2 - j) * d.half : (3 - j) * d.half] for j in range(3)]


def time_grads(d, turned, pad):
    return [dot(turned[...], time_window(d, pad, k)) for k in range(TIME)]


def write_late(d, w, ids, values, middle, outs, held):
    for tap, value in enumerate(values):
        middle[tap] = value[:, d.main :].astype(BF)
        write_grad(d, w, ids, tap, value[:, : d.main], outs, held)


def write_early(d, w, ids, values, middle, outs, held):
    for tap, value in enumerate(values):
        tile = jnp.where(ids[0] == 0, value[:, d.main :], middle[tap].astype(F32))
        value = jnp.concatenate([value[:, : d.main], tile], axis=1)
        write_grad(d, w, ids, tap, value, outs, held)


def time_grad_kernel(d, w, *refs):
    ids, middle, grad_q, act, *refs = refs
    outs, (pad, turned, held) = refs[:-3], refs[-3:]
    fill_time(d, pad, act[...])
    turned[...] = jnp.transpose(grad_q[...].astype(F32)).astype(BF)
    write_early(d, w, ids, time_grads(d, turned, pad), middle, outs, held)


def unit_grad_kernel(d, w, *refs):
    ids, a, grad_s, grad_q, act, middle, *refs = refs
    outs, (pad, time_pad, time_turned, turned, held) = refs[:-5], refs[-5:]
    k = pl.program_id(0)

    @pl.when(k == 0)
    def _():
        fill_space(d, pad, grad_s[...].astype(F32))
        turned[...] = jnp.transpose(a[...].astype(F32)).astype(BF)
        fill_time(d, time_pad, act[...])
        time_turned[...] = jnp.transpose(grad_q[...].astype(F32)).astype(BF)

    @pl.when(k < SPACE // 3)
    def _():
        write_late(d, w, ids, space_grads(d, turned, pad, k), middle, outs, held)

    @pl.when(k >= SPACE // 3)
    def _():
        write_late(d, w, ids, time_grads(d, time_turned, time_pad), middle, outs, held)


def last_space_grad_kernel(d, w, *refs):
    ids, middle, *refs = refs
    terms, refs = refs[: d.nz], refs[d.nz :]
    a, grad_pre, s, coef_one, count, mask, tot_out, *refs = refs
    outs, (pad, turned, held) = refs[:-3], refs[-3:]
    k = pl.program_id(0)

    @pl.when(k == 0)
    def _():
        total = total_of(d, ids, terms)
        tot_out[...] = total
        coef = coef_one[...]
        normed = normed_of(s[...], coef)
        grad_s = norm_back(grad_pre[...], normed, coef, total, count[4:5, 0:1], mask[...])
        fill_space(d, pad, grad_s)
        turned[...] = jnp.transpose(a[...].astype(F32)).astype(BF)

    write_early(d, w, ids, space_grads(d, turned, pad, k), middle, outs, held)


def squares_kernel(at, count, *refs):
    *values, out = refs
    row = lax.broadcasted_iota(jnp.int32, (8, LANES), 0)
    lane = lax.broadcasted_iota(jnp.int32, (8, LANES), 1)
    total = values[count][...] if len(values) > count else jnp.zeros((8, LANES), F32)
    for i, value in enumerate(values[:count]):
        lanes = jnp.sum(value[...], axis=0, keepdims=True)
        here = (row == at) & (lane == i)
        total = jnp.where(here, jnp.sum(lanes, axis=1, keepdims=True), total)
    out[...] = total


def square_sums(at, values, *base):
    return pl.pallas_call(
        functools.partial(squares_kernel, at, len(values)),
        name="squares",
        out_shape=sds((8, LANES)),
        in_specs=[whole()] * (len(values) + len(base)),
        out_specs=whole(),
    )(*values, *base)


def sds(shape, dtype=F32):
    return jax.ShapeDtypeStruct(shape, dtype)


def call(body, name, ins, outs, scratch, flops, megabytes=14):
    return pl.pallas_call(
        body,
        name=name,
        out_shape=outs,
        in_specs=[spec for spec, _ in ins],
        out_specs=[whole()] * len(outs),
        scratch_shapes=scratch,
        compiler_params=pltpu.CompilerParams(vmem_limit_bytes=megabytes * MB),
        cost_estimate=pl.CostEstimate(flops=flops, bytes_accessed=8 * MB, transcendentals=0),
    )(*[value for _, value in ins])


def w_ins(weight):
    return [
        (in_hbm(), pltpu.with_memory_space_constraint(piece, pltpu.HBM))
        for piece in weight.arrays
    ]


def v_ins(*values):
    return [(whole(), value) for value in values]


def grad_call(d, body, name, kind, taps, width, ids, values, first_outs, scratch, middle=None):
    if kind == "ring":
        shape, count = (d.nz, 2, taps, d.rows, width), 4
        spec = pl.BlockSpec((d.nz, 2, 3, d.rows, width), lambda k: (0, 0, k, 0, 0))
    elif kind == "parts":
        shape, count = (2, 2, taps, d.rows, width), d.groups // 2
        spec = pl.BlockSpec((2, 2, 3, d.rows, width), lambda k: (0, 0, k, 0, 0))
        first_outs = [*first_outs, sds((d.groups, *shape[1:]), BF)]
    else:
        shape, count = (taps, d.channels, width), 1
        spec = pl.BlockSpec((3, d.channels, width), lambda k: (k, 0, 0))
    fixed = [pl.BlockSpec(out.shape, lambda k: (0, 0)) for out in first_outs]
    if kind == "parts":
        fixed[-1] = pl.BlockSpec((d.groups, 2, 3, d.rows, width), lambda k: (0, 0, k, 0, 0))
    first = 0 if middle is None else middle[1] // 3
    tile = pl.BlockSpec((3, d.channels, LANES), lambda k: (k + first, 0, 0))
    if middle is None:
        ins, in_specs = values, []
        first_outs, fixed = [sds((taps, d.channels, LANES), BF), *first_outs], [tile, *fixed]
    else:
        ins, in_specs = (middle[0], *values), [tile]
    outs = pl.pallas_call(
        functools.partial(body, d, Weight(kind, (), 0, 1)),
        name=name,
        grid=(taps // 3,),
        out_shape=list(first_outs) + [sds(shape, BF)] * count,
        in_specs=[smem()] + in_specs + [whole()] * len(values),
        out_specs=fixed + [spec] * count,
        scratch_shapes=scratch
        + [pltpu.VMEM((d.channels, d.cells), BF), pltpu.VMEM((3, d.channels, width), BF)],
        compiler_params=pltpu.CompilerParams(vmem_limit_bytes=30 * MB),
        cost_estimate=pl.CostEstimate(flops=1, bytes_accessed=1, transcendentals=0),
    )(ids, *ins)
    return outs[: len(first_outs)], outs[len(first_outs) :]


def swap(value, axis, distance=1):
    size = lax.axis_size(axis)
    return lax.ppermute(value, axis, [(i, i ^ distance) for i in range(size)])


def across_yy(values, *besides):
    size = lax.axis_size("yy")
    distance = 1
    while distance < size:
        other = swap(values, "yy", distance)
        distance *= 2
        values = values + (after(other, *besides) if distance >= size else other)
    return values


def around_tm(values):
    size = lax.axis_size("tm")
    return [values] + [
        lax.ppermute(values, "tm", [(i, (i + k) % size) for i in range(size)])
        for k in range(1, size)
    ]


def data_sums(values, last=(), first=()):
    terms = around_tm(across_yy(values, *first))
    return [after(term, *last) if k == len(terms) - 1 else term for k, term in enumerate(terms)]


def data_sums_gather(values):
    distance = 1
    while distance < lax.axis_size("yy"):
        other = swap(values, "yy", distance)
        values = jnp.concatenate([values[:8] + other[:8], values[8:], other[8:]], axis=0)
        distance *= 2
    terms = around_tm(values)
    return [term[:8] for term in terms], terms


def pick(index, first, second):
    return jnp.where(index == 0, first, second)


def after(value, *earlier):
    if not earlier:
        return value
    return lax.optimization_barrier((value, *earlier))[0]


def turn(value):
    size = lax.axis_size("tm")
    return lax.ppermute(value, "tm", [(i, (i + 1) % size) for i in range(size)])


def together(*values):
    return lax.optimization_barrier(values)


def gather_ring(both, besides):
    held, across, made = [both], [], []
    for beside in besides:
        moves = [swap(held[-1], "yy")]
        if len(held) < lax.axis_size("tm"):
            moves.append(turn(held[-1]))
        extra = beside(held[-1], made[-1] if made else None)
        results = together(*moves, *extra)
        across.append(results[0])
        held += results[1 : len(moves)]
        made.append(results[len(moves) :])
    own = held + across
    return Weight("blocks", own + [swap(block, "u") for block in own], 0, both.shape[1]), made


def gather_all(d, s, both, *earlier):
    gathered = lax.all_gather(both, ("u",) + DATA, axis=0, tiled=False)
    gathered = after(gathered, *earlier).reshape(2, d.groups, *both.shape)
    taps = both.shape[1]
    if d.pieces:
        return Weight("all", (gathered,), 0, taps)
    parts = gathered.reshape(2, d.ny, d.nz, 2, taps, d.rows, -1)
    parts = jnp.where(s == 0, parts, parts[:, :, :, ::-1])
    natural = parts.transpose(4, 1, 3, 0, 2, 5, 6).reshape(taps, d.channels, -1)
    return Weight("natural", (natural,), 0, taps)


def added(*values):
    total = values[0].astype(F32)
    for value in values[1:]:
        total = total + value.astype(F32)
    return total.astype(BF)


def reduce_ring(d, gradients, besides):
    def joined(yrel, k, *others, second=None):
        parts = [outs[yrel][k].astype(F32) + outs[2 + yrel][k].astype(F32) for outs in gradients]
        total = jnp.concatenate(parts, axis=1)
        for other in others:
            total = total + other.astype(F32)
        if second is not None:
            total = jnp.stack([total[0], total[1] + second.astype(F32)])
        return total.astype(BF)

    first = joined(1, 1)
    by_y, by_z = swap(first[0], "yy"), turn(first[1])
    moving = joined(0, 1)
    moving, made = jnp.stack([added(moving[0], by_y), moving[1]]), []
    for k, beside in zip(list(range(2, d.nz)) + [0], besides, strict=True):
        across = swap(joined(1, k, second=by_z if k == 2 else None), "yy")
        turned = turn(moving)
        extra = beside(moving, made)
        if extra:
            turned, *extra = together(turned, *extra)
        made.append(extra)
        moving = joined(0, k, across, turned)
    return moving, made


def reduce_all(d, s, u, kind, outs, *earlier):
    if kind == "parts":
        keep, *sends = outs
        theirs = [swap(send, "u") for send in sends]
    else:
        (natural,) = outs
        taps = natural.shape[0]
        parts = natural.reshape(taps, d.ny, 2, 2, d.nz, d.rows, -1)
        parts = parts.transpose(3, 1, 4, 2, 0, 5, 6)
        parts = jnp.where(u == 0, parts, parts[::-1])
        parts = jnp.where(s == 0, parts, parts[:, :, :, ::-1])
        keep, send = parts.reshape(2, d.groups, 2, taps, d.rows, -1)
        theirs = [swap(send, "u")]
    keep, theirs = after((keep, theirs), *earlier)
    both = added(keep, jnp.concatenate(theirs, axis=0))
    return both, lax.psum_scatter(both, DATA, scatter_dimension=0, tiled=False)


def own_rows(s, mine, theirs):
    other = swap(theirs, "s")
    return pick(s, mine, other), pick(s, other, mine)


def joined_channels(*parts):
    return jnp.concatenate(parts, axis=-1).astype(F32)


def halves(d, values, unit):
    low, middle, high = (
        values[..., : d.main],
        values[..., d.main : d.half],
        values[..., d.half :],
    )
    empty = jnp.zeros_like(middle)
    first, second = (middle, empty) if unit == 0 else (empty, middle)
    return jnp.concatenate([low, first], axis=-1), jnp.concatenate([high, second], axis=-1)


def rows_of(gain, shift):
    return jnp.concatenate(
        [gain[None], shift[None], jnp.zeros((6, gain.shape[0]), F32)], axis=0
    )


def square_rows(values):
    return jnp.sum(values * values, axis=tuple(range(1, values.ndim - 1)))


def adam_part(weight, gradient, moment_one, moment_two, decay):
    new_one = BETA_ONE * moment_one + (1.0 - BETA_ONE) * gradient
    new_two = BETA_TWO * moment_two + (1.0 - BETA_TWO) * gradient * gradient
    direction = (
        new_one / (1.0 - BETA_ONE**STEP) / (jnp.sqrt(new_two / (1.0 - BETA_TWO**STEP)) + EPS_ADAM)
        + decay * weight
    )
    return (new_one, new_two, direction)


def on_device(
    clips_x,
    frames,
    labels,
    spatial_weight,
    temporal_weight,
    head_weight,
    affine,
    head_bias,
    spatial_first,
    spatial_second,
    temporal_first,
    temporal_second,
    head_first,
    head_second,
    affine_first,
    affine_second,
    bias_first,
    bias_second,
):
    s, u, z, yy = (lax.axis_index(axis) for axis in ("s", "u", "tm", "yy"))
    ny, nz = lax.axis_size("yy"), lax.axis_size("tm")
    micro, clips, _, height, width, channels = clips_x.shape
    mid = spatial_weight.shape[3]
    rows = spatial_weight.shape[0]
    classes = head_weight.shape[1]
    d = Dims(clips, nz, height, width, channels, mid, rows, ny, nz)
    assert nz == 4 and micro == 2
    ids = jnp.stack([s, u, yy, z]).astype(jnp.int32)
    denominator = micro * clips * 4 * ny

    def prepared(weight, l):
        return weight[:, l].astype(BF).transpose(1, 0, 2)

    def paired(first, second):
        return jnp.stack([pick(s, first, second), swap(pick(s, second, first), "s")])

    def by_index(index, mine, other):
        return jnp.stack([pick(index, mine, other), pick(index, other, mine)])

    pairs = []
    for value in (clips_x, jnp.stack([frames, labels]).transpose(1, 0, 2)):
        kept = pick(u, value[0], value[1])
        pairs.append(by_index(u, kept, swap(pick(u, value[1], value[0]), "u")))
    units = [
        jnp.concatenate([prepared(weight, l) for weight in (spatial_weight, temporal_weight)], axis=0)
        for l in range(2)
    ]
    early = paired(
        units[0][..., : d.half],
        jnp.concatenate([units[0][..., d.half :], units[1][..., d.main : d.half]], axis=-1),
    )

    def beside_first(*_):
        four, info = (by_index(s, pair, swap(pair, "s")) for pair in pairs)
        return four.reshape(nz, clips, height * width, channels), info

    def clips_home(four):
        return lax.all_to_all(four, "tm", split_axis=0, concat_axis=0, tiled=True)

    def beside_second(block, first):
        weights = after((spatial_weight, temporal_weight, head_weight), block)
        slot = jnp.pad(weights[2].astype(BF), ((0, 0), (0, d.main - classes)))[None]
        parts = [prepared(weights[0], 1), prepared(weights[1], 1)]
        sides = [
            jnp.concatenate([part[..., start : start + d.main] for part in parts] + [slot], axis=0)
            for start in (0, d.half)
        ]
        return [paired(*sides), clips_home(first[0])]

    def beside_third(block, second):
        x = second[1].reshape(nz, clips, height * width, channels)
        x = x.transpose(0, 2, 1, 3).reshape(d.cells, channels)
        weights = after((spatial_weight, temporal_weight, head_weight), block)
        gains, bias = after((affine, head_bias), block)
        bias_row = jnp.full((1, channels), -1e30, F32).at[0, :classes].set(bias)
        rows_one, rows_two = [], []
        for l in range(2):
            low, high = halves(d, gains[l, :, :mid], l)
            mine = pick(s, low, high)
            rows_one.append(rows_of(mine[0], mine[1]))
            rows_two.append(rows_of(gains[l, 0, mid:], gains[l, 1, mid:]))
        squares = [square_rows(weight[:, l]) for weight in weights[:2] for l in range(2)]
        return [x, bias_row, *rows_one, *rows_two, square_sums(0, [*squares, square_rows(weights[2])])]

    if d.pieces:
        early_w, made = gather_ring(
            early, [beside_first, beside_second, beside_third, lambda *_: []]
        )
        (_, info_four), (late, _), small, _ = made
    else:
        early_w = gather_all(d, s, early)
        first = beside_first()
        info_four = first[1]
        second = beside_second(early, first)
        late, small = second[0], beside_third(early, second)
    x, bias_row, *small = small
    gains_one, gains_two, weight_squares = small[:2], small[2:4], small[4]

    mine_info = lax.dynamic_index_in_dim(
        info_four.reshape(nz, 2, clips), z, 0, keepdims=False
    )
    my_frames, my_labels = mine_info[0], mine_info[1]
    valid = (jnp.arange(nz, dtype=jnp.int32)[:, None] * 8 < my_frames[None, :]).astype(F32)
    mask = jnp.broadcast_to(valid[:, None, :], (nz, height * width, clips)).reshape(d.cells, 1)
    divisor = (my_frames // 8).astype(F32) * (height * width)
    clip_info = jnp.broadcast_to(jnp.tile(divisor, 8 // clips)[:, None], (8, LANES))
    label_rows = jnp.broadcast_to(jnp.tile(my_labels, 8 // clips)[:, None], (8, LANES))
    mask, clip_info, label_rows = together(mask, clip_info, label_rows)

    wide, narrow = (d.cells, d.half), (d.cells, channels)
    space_flops = 2 * d.cells * SPACE * channels * d.half
    time_flops = 2 * d.cells * TIME * channels * d.half

    def first_space(weight):
        parts = [weight.part(0, SPACE), weight.part(SPACE, TIME)]
        return call(
            functools.partial(first_space_kernel, d, parts),
            "space0",
            [(smem(), ids)] + w_ins(weight) + v_ins(x, mask),
            [
                sds(wide),
                sds((8, d.half)),
                parts[1].natural(d),
                sds((SPACE + TIME, d.channels, LANES), BF),
            ],
            [pltpu.VMEM(parts[0].natural(d).shape, BF)]
            + [part.semaphores(d) for part in parts]
            + [space_scratch(d, channels)],
            space_flops,
            20,
        )

    def next_space(weight, middle, q, terms, count):
        sizes = (SPACE, TIME, 1)
        parts = [weight.part(sum(sizes[:i]), size) for i, size in enumerate(sizes)]
        return call(
            functools.partial(second_space_kernel, d, parts),
            "space1",
            [(smem(), ids)] + w_ins(weight) + v_ins(*terms, q, count, gains_two[0], mask, middle),
            [sds(narrow, BF), sds((8, channels)), sds(wide), sds((8, d.half))]
            + [part.natural(d) for part in parts],
            [part.semaphores(d) for part in parts] + [space_scratch(d, channels)],
            space_flops,
        )

    def time_next(l, s_value, terms, *count):
        return call(
            functools.partial(time_kernel, d, len(time_w[l])),
            f"time{l}",
            [(smem(), ids)] + v_ins(*time_w[l], *terms, s_value, *count, gains_one[l], mask),
            [sds(wide, BF), sds(narrow, BF), sds((8, d.half))],
            [time_scratch(d, d.half)],
            time_flops,
        )

    def joined(q_part):
        return call(
            join_kernel,
            "join",
            v_ins(q_part, swap(q_part, "s"), mask),
            [sds(narrow, BF), sds((8, channels))],
            [],
            d.cells * channels,
            12,
        )

    s0, sums, time_first, middle = first_space(early_w)
    time_w = [(time_first,), None]
    terms = data_sums(sums)
    act0, q_part, coef_one0 = time_next(0, s0, terms)
    count = coef_one0
    q0, sums = joined(q_part)
    terms = data_sums(sums)
    late_w = gather_all(d, s, late, terms[0])
    a_mid, coef_two0, s1, sums, space_late, time_late, head_w = next_space(
        late_w, middle, q0, terms, count
    )
    time_w[1] = (time_late, middle)
    terms = data_sums(sums)
    act1, q_part, coef_one1 = time_next(1, s1, terms, count)
    q1, sums = joined(q_part)
    terms = data_sums(sums)
    coef_two1, grad_two, sums = call(
        functools.partial(head_kernel, d, float(denominator), classes),
        "head",
        [(smem(), ids)]
        + v_ins(head_w, *terms, q1, count, gains_two[1], mask, x, bias_row, clip_info, label_rows),
        [sds((8, channels)), sds(narrow), sds((16, channels))],
        [],
        4 * d.cells * channels,
    )
    terms, carried = data_sums_gather(sums)

    def time_back(l, grad, q, coef_two, terms, s_value, coef_one):
        return call(
            functools.partial(time_back_kernel, d, len(time_w[l])),
            f"time_back{l}",
            [(smem(), ids)]
            + v_ins(*time_w[l], *terms, grad, q, coef_two, count, mask, s_value, coef_one),
            [sds(narrow, BF), sds(wide), sds((8, d.half)), sds((8, channels))],
            [time_scratch(d, channels)],
            1,
        )

    late_kind = "parts" if d.pieces else "natural"
    early_kind = "ring" if d.pieces else "natural"

    grad_q1, grad_one, sums, tot_two1 = time_back(
        1, grad_two, q1, coef_two1, terms, s1, coef_one1
    )
    terms = data_sums(sums)
    grad_s1, ga_part, tot_one1 = call(
        functools.partial(space_back_kernel, d, 2),
        "space_back",
        [(smem(), ids)] + v_ins(space_late, middle, *terms, grad_one, s1, coef_one1, count, mask),
        [sds(wide, BF), sds(narrow, BF), sds((8, d.half))],
        [space_scratch(d, d.half), pltpu.VMEM((d.cells, channels), F32)],
        space_flops,
    )
    ga_other = swap(ga_part, "s")
    late_first, late_outs = grad_call(
        d,
        unit_grad_kernel,
        "unit_grad1",
        late_kind,
        SPACE + TIME,
        d.main,
        ids,
        (a_mid, grad_s1, grad_q1, act1),
        [],
        [
            space_scratch(d, d.half),
            time_scratch(d, d.half),
            pltpu.VMEM((d.channels, d.cells), BF),
        ],
    )
    middle_grad, *late_first = late_first
    late_outs = [*late_first, *late_outs]
    grad_two, sums = call(
        join_back_kernel,
        "join_back",
        v_ins(ga_part, after(ga_other, *late_outs), q0, coef_two0, mask),
        [sds(narrow), sds((8, channels))],
        [],
        20 * 10**9,
        12,
    )
    late_both, late_sum = reduce_all(d, s, u, late_kind, late_outs, sums)

    terms = data_sums(after(sums, late_both))
    grad_q0, grad_one, sums, tot_two0 = time_back(
        0, grad_two, q0, coef_two0, terms, s0, coef_one0
    )
    _, time_outs0 = grad_call(
        d,
        time_grad_kernel,
        "time_grad0",
        early_kind,
        TIME,
        d.half,
        ids,
        (grad_q0, act0),
        [],
        [time_scratch(d, d.half)],
        (middle_grad, SPACE),
    )
    if d.pieces:
        time_outs0 = [*time_outs0[:2], *(swap(send, "u") for send in time_outs0[2:])]
    terms = data_sums(sums, time_outs0[2:], time_outs0[:2])
    (tot_one0,), space_outs0 = grad_call(
        d,
        last_space_grad_kernel,
        "space_grad0",
        early_kind,
        SPACE,
        d.half,
        ids,
        (*terms, x, grad_one, s0, coef_one0, count, mask),
        [sds((8, d.half))],
        [space_scratch(d, d.half)],
        (middle_grad, 0),
    )

    def head_steps(value):
        rows_all = jnp.concatenate([term[8:] for term in after(carried, value)], axis=0)
        rows_all = jnp.concatenate([rows_all, swap(rows_all, "u")], axis=0)
        rows_all = rows_all.reshape(-1, 8, channels)
        pooled_all = rows_all[:, :clips].reshape(-1, channels)
        logit_all = rows_all[:, clips : 2 * clips].reshape(-1, channels)
        loss_sum = jnp.sum(logit_all[:, classes])
        logit_all = logit_all[:, :classes]
        bias_grad = jnp.sum(logit_all, axis=0)
        base = d.row_base(yy, s, u, z)
        pooled_mine = lax.dynamic_slice_in_dim(pooled_all, base, rows, 1)
        head_grad = lax.dot_general(
            pooled_mine.astype(BF),
            logit_all.astype(BF),
            (((0,), (0,)), ((), ())),
            preferred_element_type=F32,
        )
        head_one, head_two, head_dir = adam_part(head_weight, head_grad, head_first, head_second, DECAY)
        bias_one, bias_two, bias_dir = adam_part(head_bias, bias_grad, bias_first, bias_second, 0.0)
        return (
            loss_sum, head_one, head_two, head_dir, square_rows(head_dir), bias_one, bias_two, bias_dir
        )

    def affine_steps(value):
        one0, one1, two0, two1 = after((tot_one0, tot_one1, tot_two0, tot_two1), value)
        ones, twos = jnp.stack([one0[:2], one1[:2]]), jnp.stack([two0[:2], two1[:2]])
        small = jnp.concatenate([ones, twos], axis=-1)
        small = small + swap(small, "u")
        ones, twos = small[..., : d.half], small[..., d.half :]
        ones_other = swap(ones, "s")
        low, high = pick(s, ones, ones_other), pick(s, ones_other, ones)
        ones = [
            jnp.concatenate([low[0], high[0, :, : d.main]], axis=-1),
            jnp.concatenate([low[1, :, : d.main], high[1, :, d.main :], high[1, :, : d.main]], axis=-1),
        ]
        both = jnp.concatenate([jnp.stack(ones), twos], axis=-1)
        affine_grad = jnp.stack([both[:, 1], both[:, 0]], axis=1)
        one, two, direction = adam_part(affine, affine_grad, affine_first, affine_second, 0.0)
        return one, two, affine - RATE_SMALL * direction

    if d.pieces:
        early_sum, made = reduce_ring(
            d,
            [[*space_outs0[:2], *(swap(send, "u") for send in space_outs0[2:])], time_outs0],
            [
                lambda value, _: (),
                lambda value, _: (late_sum[0], late_sum[1], *head_steps(value)),
                lambda value, made: (*own_rows(s, *made[1][:2]), *affine_steps(value)),
            ],
        )
        late_sum, head_made, affine_made = made[2][:2], made[1][2:], made[2][2:]
    else:
        early_outs = [jnp.concatenate([space_outs0[0], time_outs0[0]], axis=0)]
        _, early_sum = reduce_all(d, s, u, early_kind, early_outs)
        late_sum = own_rows(s, late_sum[0], late_sum[1])
        head_made = head_steps(early_sum)
        affine_made = affine_steps(early_sum)
    loss_sum, head_one, head_two, head_dir, head_squares, bias_one, bias_two, bias_dir = head_made
    low, high = own_rows(s, early_sum[0], early_sum[1])
    early_sum = joined_channels(low, high[..., : d.main])
    late_sum = joined_channels(late_sum[0], high[..., d.main :], late_sum[1])

    def both_units(first, second):
        return jnp.stack([first, second]).transpose(2, 0, 1, 3)

    spatial_grad = both_units(early_sum[:SPACE], late_sum[:SPACE])
    temporal_grad = both_units(early_sum[SPACE:], late_sum[SPACE:])
    space_one, space_two, space_dir = adam_part(
        spatial_weight, spatial_grad, spatial_first, spatial_second, DECAY
    )
    time_one, time_two, time_dir = adam_part(
        temporal_weight, temporal_grad, temporal_first, temporal_second, DECAY
    )
    affine_one, affine_two, new_affine = affine_made
    dir_squares = [square_rows(v[:, l]) for v in (space_dir, time_dir) for l in range(2)]
    dir_squares.append(head_squares)
    padded = square_sums(1, dir_squares, weight_squares)
    native, by_tap = (Layout(major_to_minor=order) for order in ((0, 2, 1, 3), (1, 2, 0, 3)))
    moments = together(
        *(with_layout_constraint(v, by_tap) for v in (space_one, space_two, time_one, time_two))
    )
    moments = [with_layout_constraint(value, native) for value in moments]
    space_one, space_two, time_one, time_two = moments
    padded = padded + swap(padded, "u")
    padded = padded + swap(padded, "s")
    terms = data_sums(padded, moments[1:3], (moments[0], moments[3]))
    terms = jnp.stack(terms)
    padded = sum(terms[lax.rem(z + (nz - place), nz)] for place in range(nz))
    norms = jnp.sqrt(padded[:2, :5])
    trust = norms[0] / norms[1]
    new_space = spatial_weight - RATE * trust[0:2][None, :, None, None] * space_dir
    new_time = temporal_weight - RATE * trust[2:4][None, :, None, None] * time_dir
    new_head = head_weight - RATE * trust[4] * head_dir
    new_bias = head_bias - RATE_SMALL * bias_dir
    return (
        loss_sum,
        space_one,
        space_two,
        new_space,
        time_one,
        time_two,
        new_time,
        head_one,
        head_two,
        new_head,
        affine_one,
        affine_two,
        new_affine,
        bias_one,
        bias_two,
        new_bias,
        norms,
    )


def solution(mesh):
    dp, tm = mesh.shape["dp"], mesh.shape["tm"]
    fine = Mesh(mesh.devices.reshape(dp // 4, 2, 2, tm), ALL)
    dp_axes = ("yy", "s", "u")
    owner = P(ALL)
    return jax.shard_map(
        on_device,
        mesh=fine,
        in_specs=(
            P(None, dp_axes, "tm"),
            P(None, dp_axes),
            P(None, dp_axes),
            owner,
            owner,
            owner,
            P(),
            P(),
            owner,
            owner,
            owner,
            owner,
            owner,
            owner,
            P(),
            P(),
            P(),
            P(),
        ),
        out_specs=(P(),) + (owner,) * 9 + (P(),) * 7,
        check_vma=False,
    )
```
